32 devices in a mesh: pb: 8 (over z, y), col: 4 (over x, core).
Axes of the slice: x: 2, y: 2, z: 4, core: 2. Of those that a mesh axis runs over, the one named last changes fastest.
Arguments:
- hidden: bfloat16 [8, 4, 1024, 768], P('pb', 'col'), may hold values from -6 to 6
- lengths: int32 [8, 4], P('pb', 'col'), may hold values from 256 to 1024, as said below
- counts: int32 [8], P('pb'), may hold values from 2 to 4, as said below
- targets: float32 [8, 4], P('pb', 'col'), may hold values from 0.01 to 100
- out_grad: bfloat16 [8, 4, 1024, 768], P('pb', 'col'), may hold values from -6 to 6
- qkv_weight: bfloat16 [768, 2304], P(('pb', 'col')), may hold values from -0.21875 to 0.21875
- qv_bias: bfloat16 [2, 768], P(None, ('pb', 'col')), may hold values from -3 to 3
- out_weight: bfloat16 [768, 768], P(('pb', 'col')), may hold values from -1.75 to 1.75
- out_bias: bfloat16 [768], P(('pb', 'col')), may hold values from -2 to 2
- norm1_gain: bfloat16 [768], P(('pb', 'col')), may hold values from 0.099609375 to 1.8984375
- norm1_bias: bfloat16 [768], P(('pb', 'col')), may hold values from -2 to 2
- up_weight: bfloat16 [768, 3072], P(('pb', 'col')), may hold values from -0.21875 to 0.21875
- up_bias: bfloat16 [3072], P(('pb', 'col')), may hold values from -3 to 3
- down_weight: bfloat16 [3072, 768], P(('pb', 'col')), may hold values from -0.15625 to 0.15625
- down_bias: bfloat16 [768], P(('pb', 'col')), may hold values from -2 to 2
- norm2_gain: bfloat16 [768], P(('pb', 'col')), may hold values from 0.099609375 to 1.8984375
- norm2_bias: bfloat16 [768], P(('pb', 'col')), may hold values from -2 to 2
- rel_bias: bfloat16 [32, 12], replicated, may hold values from -4 to 4
- score_weight: bfloat16 [768], P(('pb', 'col')), may hold values from -0.625 to 0.625
Outputs:
- layer_out: bfloat16 [8, 4, 1024, 768], P('pb', 'col')
- loss: float32 [], replicated
- hidden_grad: bfloat16 [8, 4, 1024, 768], P('pb', 'col')
- qkv_weight_grad: float32 [768, 2304], P(('pb', 'col'))
- qv_bias_grad: float32 [2, 768], P(None, ('pb', 'col'))
- out_weight_grad: float32 [768, 768], P(('pb', 'col'))
- out_bias_grad: float32 [768], P(('pb', 'col'))
- norm1_gain_grad: float32 [768], P(('pb', 'col'))
- norm1_bias_grad: float32 [768], P(('pb', 'col'))
- up_weight_grad: float32 [768, 3072], P(('pb', 'col'))
- up_bias_grad: float32 [3072], P(('pb', 'col'))
- down_weight_grad: float32 [3072, 768], P(('pb', 'col'))
- down_bias_grad: float32 [768], P(('pb', 'col'))
- norm2_gain_grad: float32 [768], P(('pb', 'col'))
- norm2_bias_grad: float32 [768], P(('pb', 'col'))
- rel_bias_grad: float32 [32, 12], replicated
- score_weight_grad: float32 [768], P(('pb', 'col'))
The draws below stay inside these ranges and needn't reach their ends.
Inputs may be any that keep to these rules, and one draw needn't show every extreme that they name: lengths[q, c] counts the live tokens of a pair, the first ones of its 1024 slots; one pair of every draw has all 1024. counts[q] counts the live candidates of a query, the first ones of its 4 slots; one query of every draw has all 4.
All inputs are finite; a program needn't handle non-finite values.
Results may differ from the reference program's by a relative error of at most 0.015.
Values may be sent and summed in bfloat16 or wider, within the bound.
No kernel may reach another device: no remote copies, remote signals or barrier semaphores. Data moves between devices by JAX's collectives and lax.ppermute only.
A program may use at most 320 MiB of HBM per device.

```python
import math
import jax
import jax.numpy as jnp
from jax import lax

D = 768
HEADS = 12
HEAD_DIM = 64
FF = 3072
BUCKETS = 32
SEQ = 1024
QUERIES = 8
CAND = 4


def draw_lengths(key, part):
    total = QUERIES * CAND
    drawn = jax.random.randint(key, (total,), SEQ // 4, SEQ + 1)
    chosen = jax.random.randint(jax.random.fold_in(key, 7), (), 0, total)
    drawn = jnp.where(jnp.arange(total) == chosen, SEQ, drawn)
    return drawn.reshape(QUERIES, CAND).astype(jnp.int32)


def draw_counts(key, part):
    drawn = jax.random.randint(key, (QUERIES,), 2, CAND + 1)
    chosen = jax.random.randint(jax.random.fold_in(key, 11), (), 0, QUERIES)
    drawn = jnp.where(jnp.arange(QUERIES) == chosen, CAND, drawn)
    return drawn.astype(jnp.int32)


def block_levels(stream_key, extent, pieces, least, high):
    level, own = 1.0, jax.random.fold_in(stream_key, 6)
    for axis_at, blocks in pieces:
        steps = jnp.exp(jax.random.uniform(jax.random.fold_in(own, axis_at), (blocks,), jnp.float32, least / len(pieces), high / len(pieces)))
        level = level * jnp.repeat(steps, extent[axis_at] // blocks).reshape([-1 if axis == axis_at else 1 for axis in range(len(extent))])
    return level


def normal_values(rng, dims, deviation, most, split=(), kind=jnp.bfloat16):
    entries = jax.random.normal(rng, dims, jnp.float32) * deviation
    if len(split) > 0:
        entries = block_levels(rng, dims, split, -0.22, 0.18) * entries
    return jnp.clip(entries, min=-most, max=most).astype(kind)


def setup_inputs(seed: int = 0) -> dict:
    key_list = jax.random.split(jax.random.key(seed), 20)
    hidden = normal_values(key_list[0], (QUERIES, CAND, SEQ, D), 1.0, 6.0, ((0, 8), (1, 4)))
    lengths = draw_lengths(jax.random.fold_in(key_list[19], 71), 0)
    counts = draw_counts(jax.random.fold_in(key_list[19], 71), 0)
    targets = jnp.clip(jnp.exp(math.log(100.0) - 9.2103404 * jax.random.uniform(key_list[3], (QUERIES, CAND), jnp.float32) ** block_levels(key_list[3], (QUERIES, CAND), ((0, 8), (1, 4)), -0.2, 0.2)), 0.01, 100.0)
    out_grad = normal_values(key_list[4], (QUERIES, CAND, SEQ, D), 1.0, 6.0, ((0, 8), (1, 4)))
    qkv_weight = normal_values(key_list[5], (D, 3 * D), D ** -0.5, 0.21875, ((0, 32),))
    qv_bias = normal_values(key_list[6], (2, D), 0.5, 3.0, ((1, 32),))
    out_weight = normal_values(key_list[7], (D, D), (D // 64) ** -0.5, 1.75, ((0, 32),))
    out_bias = normal_values(key_list[8], (D,), 0.3, 2.0, ((0, 32),))
    norm1_gain = jnp.clip(1.0 + 0.18 * jax.random.normal(key_list[9], (D,), jnp.float32), 0.099609375, 1.8984375).astype(jnp.bfloat16)
    norm1_bias = normal_values(key_list[10], (D,), 0.3, 2.0, ((0, 32),))
    up_weight = normal_values(key_list[11], (D, FF), D ** -0.5, 0.21875, ((0, 32),))
    up_bias = normal_values(key_list[12], (FF,), 0.5, 3.0, ((0, 32),))
    down_weight = normal_values(key_list[13], (FF, D), (FF // 2) ** -0.5, 0.15625, ((0, 32),))
    down_bias = normal_values(key_list[14], (D,), 0.3, 2.0, ((0, 32),))
    norm2_gain = jnp.clip(1.0 + 0.18 * jax.random.normal(key_list[15], (D,), jnp.float32), 0.099609375, 1.8984375).astype(jnp.bfloat16)
    norm2_bias = normal_values(key_list[16], (D,), 0.3, 2.0, ((0, 32),))
    rel_bias = normal_values(key_list[17], (BUCKETS, HEADS), 1.0, 4.0)
    score_weight = normal_values(key_list[18], (D,), (D // 9) ** -0.5, 0.625, ((0, 32),))
    return dict(hidden=hidden, lengths=lengths, counts=counts, targets=targets, out_grad=out_grad, qkv_weight=qkv_weight, qv_bias=qv_bias, out_weight=out_weight, out_bias=out_bias, norm1_gain=norm1_gain, norm1_bias=norm1_bias, up_weight=up_weight, up_bias=up_bias, down_weight=down_weight, down_bias=down_bias, norm2_gain=norm2_gain, norm2_bias=norm2_bias, rel_bias=rel_bias, score_weight=score_weight)


EDGES = (1, 2, 3, 4, 5, 6, 7, 8, 12, 16, 23, 32, 45, 64, 91)
HIGHEST = lax.Precision.HIGHEST

@jax.custom_vjp
def low(v):
    return lax.optimization_barrier(v.astype(jnp.bfloat16)).astype(jnp.float32)

@jax.custom_vjp
def low_back(v):
    return v

def low_keep(v):
    return (low(v), None)

def low_pass(kept, grad):
    return (grad,)

def back_keep(v):
    return (v, None)

def back_low(kept, grad):
    return (low(grad),)
low.defvjp(low_keep, low_pass)
low_back.defvjp(back_keep, back_low)

def bucket_ids(length):
    places = jnp.arange(length, dtype=jnp.int32)
    offset = places[None, :] - places[:, None]
    magnitude = jnp.abs(offset)
    ids = jnp.where(offset > 0, 16, 0).astype(jnp.int32)
    for edge in EDGES:
        ids = ids + (magnitude >= edge).astype(jnp.int32)
    return ids

def layer_norm(resid, gain, shift):
    centered = resid - lax.optimization_barrier(jnp.mean(resid, axis=-1, keepdims=True))
    spread = lax.optimization_barrier(jnp.mean(centered * centered, axis=-1, keepdims=True))
    return centered * lax.rsqrt(spread + 1e-05) * gain + shift

def one_pair(weights, table, tokens, length):
    qkv_w, qv_b, out_w, out_b, gain1, shift1, up_w, up_b, down_w, down_b, gain2, shift2 = weights
    zeros = jnp.zeros((D,), jnp.float32)
    qkv = jnp.dot(tokens, qkv_w, precision=HIGHEST) + jnp.concatenate([qv_b[0], zeros, qv_b[1]])
    qkv = low(low_back(qkv))
    queries = qkv[:, :D].reshape(SEQ, HEADS, HEAD_DIM)
    keys = qkv[:, D:2 * D].reshape(SEQ, HEADS, HEAD_DIM)
    values = qkv[:, 2 * D:].reshape(SEQ, HEADS, HEAD_DIM)
    scores = jnp.einsum('ihd,jhd->hij', queries, keys, precision=HIGHEST) * HEAD_DIM ** (-0.5) + table
    scores = low_back(scores)
    live = jnp.arange(SEQ, dtype=jnp.int32) < length
    scores = jnp.where(live[None, None, :], scores, -1e+30)
    top = lax.optimization_barrier(jnp.max(scores, axis=-1, keepdims=True))
    expo = jnp.exp(scores - top)
    probs = low(expo / lax.optimization_barrier(jnp.sum(expo, axis=-1, keepdims=True)))
    mixed = jnp.einsum('hij,jhd->ihd', probs, values, precision=HIGHEST).reshape(SEQ, D)
    mixed = low(low_back(mixed))
    attended = low_back(jnp.dot(mixed, out_w, precision=HIGHEST) + out_b)
    normed = layer_norm(tokens + attended, gain1, shift1)
    inner = low_back(jnp.dot(low(normed), up_w, precision=HIGHEST) + up_b)
    activ = low(jax.nn.gelu(inner, approximate=False))
    branch = low_back(jnp.dot(activ, down_w, precision=HIGHEST) + down_b)
    final = layer_norm(normed + branch, gain2, shift2)
    return final * live[:, None].astype(jnp.float32)

def reference(hidden, lengths, counts, targets, out_grad, qkv_weight, qv_bias, out_weight, out_bias, norm1_gain, norm1_bias, up_weight, up_bias, down_weight, down_bias, norm2_gain, norm2_bias, rel_bias, score_weight):
    weights = tuple((w.astype(jnp.float32) for w in (qkv_weight, qv_bias, out_weight, out_bias, norm1_gain, norm1_bias, up_weight, up_bias, down_weight, down_bias, norm2_gain, norm2_bias)))
    ids = bucket_ids(SEQ)

    def forward(hidden_f, rel_f, weight_set, score_f):
        table = jnp.transpose(rel_f[ids], (2, 0, 1))
        tokens = hidden_f.reshape(QUERIES * CAND, SEQ, D)

        def step(pair):
            return one_pair(weight_set, table, pair[0], pair[1])
        finals = lax.map(jax.checkpoint(step), (tokens, lengths.reshape(QUERIES * CAND)))
        scores = jnp.dot(finals[:, 0, :], score_f, precision=HIGHEST).reshape(QUERIES, CAND)
        live = jnp.arange(CAND, dtype=jnp.int32)[None, :] < counts[:, None]
        share = jnp.where(live, targets, 0.0)
        target = share / lax.optimization_barrier(jnp.sum(share, axis=1, keepdims=True))
        masked = jnp.where(live, scores, -1e+30)
        top = lax.optimization_barrier(jnp.max(masked, axis=1, keepdims=True))
        lognorm = top[:, 0] + jnp.log(lax.optimization_barrier(jnp.sum(jnp.exp(masked - top), axis=1)))
        entropy = lognorm - lax.optimization_barrier(jnp.sum(target * scores, axis=1))
        weight = counts.astype(jnp.float32)
        loss = jnp.sum(weight * entropy) / jnp.sum(weight)
        return (finals.reshape(QUERIES, CAND, SEQ, D), loss)
    (final, loss), pullback = jax.vjp(forward, hidden.astype(jnp.float32), rel_bias.astype(jnp.float32), weights, score_weight.astype(jnp.float32))
    grad_hidden, grad_rel, grad_weights, grad_score = pullback((out_grad.astype(jnp.float32), jnp.ones((), jnp.float32)))
    return (final.astype(jnp.bfloat16), loss, grad_hidden.astype(jnp.bfloat16), grad_weights[0], grad_weights[1], grad_weights[2], grad_weights[3], grad_weights[4], grad_weights[5], grad_weights[6], grad_weights[7], grad_weights[8], grad_weights[9], grad_weights[10], grad_weights[11], grad_rel, grad_score)
```

```python
import functools

import jax
import jax.numpy as jnp
from jax import lax
from jax.experimental import pallas as pl
from jax.experimental.pallas import tpu as pltpu
from jax.sharding import PartitionSpec as P

f32=jnp.float32; bf=jnp.bfloat16
NT=(((1,),(1,)),((),())); NN=(((1,),(0,)),((),())); TN=(((0,),(0,)),((),()))
T=128
EDGES = (1, 2, 3, 4, 5, 6, 7, 8, 12, 16, 23, 32, 45, 64, 91)
def strip_ids():
    r=jnp.arange(3*T,dtype=jnp.int32)[None,:]-T-jnp.arange(T,dtype=jnp.int32)[:,None]
    m=jnp.abs(r); ids=jnp.where(r>0,16,0).astype(jnp.int32)
    for e in EDGES: ids=ids+(m>=e).astype(jnp.int32)
    return ids
def tables(rel_bias, length, S):
    ids=strip_ids()
    nb=rel_bias.shape[0]
    oh=(ids[None]==jnp.arange(nb,dtype=jnp.int32)[:,None,None]).astype(bf)
    strips=jnp.einsum("bac,bh->hac",oh,rel_bias,preferred_element_type=f32)
    j=jnp.arange(S,dtype=jnp.int32)[:,None]; lane=jnp.arange(128,dtype=jnp.int32)[None,:]
    jb=j//T; nblk=S//T
    low=(jb<=lane-2)&(lane<nblk); up=(jb>=lane+2)&(lane<nblk)
    mk=jnp.where((lane==nblk)&(j>=length),-1e30,0.0)
    rb=rel_bias.astype(f32)
    kx=jnp.where(low[None],rb[15][:,None,None],jnp.where(up[None],rb[31][:,None,None],mk[None])).astype(bf)
    return strips,kx
def fwd_kernel(BQ, S, q_ref,k_ref,v_ref,kx_ref,st_ref,mix_ref,linv_ref,mf_ref,p_ref):
    nblk=S//T
    lane=lax.broadcasted_iota(jnp.int32,(1,128),1)
    row=lax.broadcasted_iota(jnp.int32,(BQ,128),0)//T
    lane2=lax.broadcasted_iota(jnp.int32,(BQ,128),1)
    q=q_ref[...];k=k_ref[...];v=v_ref[...]
    masks=[lane<64,lane>=64]
    kaug=[jnp.concatenate([k,kx_ref[h]],axis=1) for h in (0,1)]
    vaug=[jnp.where(masks[h],v,jnp.ones_like(v)) for h in (0,1)]
    for i in range(S//BQ):
        outs=[]
        qi=q[i*BQ:(i+1)*BQ]
        qx=((lane2==nblk)|(lane2==row+i*(BQ//T))).astype(f32).astype(bf)
        for h in (0,1):
            qa=jnp.concatenate([jnp.where(masks[h],qi,jnp.zeros_like(qi)),qx],axis=1)
            s=dg(qa,kaug[h],NT)
            rows=[]
            for b in range(BQ//T):
                I=i*(BQ//T)+b
                lo=max(0,(I-1)*T);hi=min(S,(I+2)*T)
                sb=s[b*T:(b+1)*T]
                parts=[]
                if lo>0: parts.append(sb[:,:lo])
                parts.append(sb[:,lo:hi]+st_ref[h,:,lo-(I-1)*T:hi-(I-1)*T])
                if hi<S: parts.append(sb[:,hi:])
                rows.append(jnp.concatenate(parts,axis=1) if len(parts)>1 else parts[0])
            s=jnp.concatenate(rows,axis=0) if len(rows)>1 else rows[0]
            m=jnp.max(s,axis=1,keepdims=True)
            p=jnp.exp(s-m).astype(bf)
            p_ref[h,i*BQ:(i+1)*BQ,:]=p
            outs.append(dg(p,vaug[h],NN))
        o0,o1=outs
        num=jnp.where(masks[0],o0,o1)
        den=jnp.where(masks[0],o1,o0)
        den=pltpu.roll(den,64,1)
        linv=1.0/den
        mf=num*linv
        mf_ref[i*BQ:(i+1)*BQ,:]=mf
        mix_ref[i*BQ:(i+1)*BQ,:]=mf.astype(bf)
        linv_ref[i*BQ:(i+1)*BQ,:]=linv
def attn_fwd(qkv,kx,strips,BQ=128):
    S,W=qkv.shape; npair=W//3//128
    return pl.pallas_call(functools.partial(fwd_kernel,BQ,S),grid=(npair,),
        in_specs=[pl.BlockSpec((S,128),lambda p:(0,p)),pl.BlockSpec((S,128),lambda p:(0,npair+p)),pl.BlockSpec((S,128),lambda p:(0,2*npair+p)),
                  pl.BlockSpec((2,S,128),lambda p:(p,0,0)),pl.BlockSpec((2,T,3*T),lambda p:(p,0,0))],
        out_specs=[pl.BlockSpec((S,128),lambda p:(0,p))]*3+[pl.BlockSpec((2,S,S),lambda p:(p,0,0))],
        out_shape=[jax.ShapeDtypeStruct((S,W//3),bf),jax.ShapeDtypeStruct((S,W//3),f32),jax.ShapeDtypeStruct((S,W//3),f32),jax.ShapeDtypeStruct((2*npair,S,S),bf)],
        compiler_params=pltpu.CompilerParams(vmem_limit_bytes=56*2**20),
        )(qkv,qkv,qkv,kx,strips)
def bwd_kernel(BQ,S,form,scale,kscale,q_ref,k_ref,v_ref,gm_ref,mf_ref,linv_ref,p_ref,dq_ref,dk_ref,dv_ref,near_ref,far_ref,ds_ref):
    nblk=S//T
    lane=lax.broadcasted_iota(jnp.int32,(1,128),1)
    lanes=lax.broadcasted_iota(jnp.int32,(S,128),1)
    rows=lax.broadcasted_iota(jnp.int32,(S,128),0)
    masks=[lane<64,lane>=64]
    q=q_ref[...];k=k_ref[...];v=v_ref[...]
    gm=gm_ref[...].astype(f32);linv=linv_ref[...]
    do=(gm*linv).astype(bf)
    t=do.astype(f32)*mf_ref[...]
    kind=(lanes==rows//T).astype(f32).astype(bf)
    kaug=jnp.concatenate([k,kind],axis=1)
    vx=jnp.where(lanes<2,1.0,0.0).astype(bf)
    vaug=jnp.concatenate([v,vx],axis=1)
    dqs=[];dks=[];dvs=[]
    if form=="T":
        qT=q.T; doT=do.T
    for h in (0,1):
        delta=jnp.sum(jnp.where(masks[h],t,0.0),axis=1,keepdims=True)
        hi=delta.astype(bf).astype(f32); lo=delta-hi
        ex=jnp.where(lanes==0,-hi,jnp.where(lanes==1,-lo,0.0)).astype(bf)
        da=jnp.concatenate([jnp.where(masks[h],do,jnp.zeros_like(do)),ex],axis=1)
        near=[jnp.zeros((T,T),f32) for _ in range(3)]
        dq=[]
        for i in range(S//BQ):
            x=dg(da[i*BQ:(i+1)*BQ],vaug,NT)
            ds=p_ref[h,i*BQ:(i+1)*BQ,:]*x.astype(bf)
            ds_ref[i*BQ:(i+1)*BQ,:]=ds
            dq.append(dg(ds,kaug,NN))
            for b in range(BQ//T):
                I=i*(BQ//T)+b
                for n in (-1,0,1):
                    if 0<=I+n<nblk:
                        near[n+1]=near[n+1]+ds[b*T:(b+1)*T,(I+n)*T:(I+n+1)*T].astype(f32)
        for n in range(3): near_ref[h,:,n*T:(n+1)*T]=near[n]
        dq=jnp.concatenate(dq,axis=0)
        dqs.append(dq[:,:128])
        far=dq[:,128:]
        ib=rows//T
        far_ref[h,0:1,:]=jnp.sum(jnp.where(lanes<=ib-2,far,0.0),axis=0,keepdims=True)
        far_ref[h,1:2,:]=jnp.sum(jnp.where((lanes>=ib+2)&(lanes<nblk),far,0.0),axis=0,keepdims=True)
        far_ref[h,2:8,:]=jnp.zeros((6,128),f32)
        if form=="T":
            dks.append(dg(qT[h*64:(h+1)*64],ds_ref[...],NN))
            dvs.append(dg(doT[h*64:(h+1)*64],p_ref[h],NN))
        else:
            dks.append(dg(ds_ref[...],q,TN))
            dvs.append(dg(p_ref[h],do,TN))
    dq_ref[...]=(jnp.where(masks[0],dqs[0],dqs[1])*scale).astype(bf)
    if form=="T":
        dk_ref[...]=(jnp.concatenate(dks,axis=0)*kscale).T.astype(bf)
        dv_ref[...]=jnp.concatenate(dvs,axis=0).T.astype(bf)
    else:
        dk_ref[...]=(jnp.where(masks[0],dks[0],dks[1])*kscale).astype(bf)
        dv_ref[...]=jnp.where(masks[0],dvs[0],dvs[1]).astype(bf)
def attn_bwd(qkv,gm,mixed,linv,p,BQ=128,form="T",scale=0.125,kscale=1.0):
    S,W=qkv.shape; npair=W//3//128; D=W//3
    blk=lambda o: pl.BlockSpec((S,128),lambda i:(0,o*npair+i))
    return pl.pallas_call(functools.partial(bwd_kernel,BQ,S,form,scale,kscale),grid=(npair,),
        in_specs=[blk(0),blk(1),blk(2),blk(0),blk(0),blk(0),pl.BlockSpec((2,S,S),lambda i:(i,0,0))],
        out_specs=[blk(0),blk(0),blk(0),pl.BlockSpec((2,T,3*T),lambda i:(i,0,0)),pl.BlockSpec((2,8,128),lambda i:(i,0,0))],
        out_shape=[jax.ShapeDtypeStruct((S,D),bf)]*3+[jax.ShapeDtypeStruct((2*npair,T,3*T),f32),jax.ShapeDtypeStruct((2*npair,8,128),f32)],
        scratch_shapes=[pltpu.VMEM((S,S),bf)],
        compiler_params=pltpu.CompilerParams(vmem_limit_bytes=56*2**20),
        )(qkv,qkv,qkv,gm,mixed,linv,p)
def dg(a,b,d=NN): return lax.dot_general(a,b,d,preferred_element_type=f32)
QB,VB,OB,G1,S1,DB,G2,S2,SW,UB=0,1,2,3,4,5,6,7,8,9
def gelu_both(x,mode="poly"):
    e=jnp.exp(x*x*-0.5)
    if mode=="erf":
        cdf=0.5*(1.0+lax.erf(x*0.7071067811865476))
    else:
        t=1.0/(1.0+(0.3275911*0.7071067811865476)*jnp.abs(x))
        q=t*(0.127414796+t*(-0.142248368+t*(0.7107068705+t*(-0.7265760135+t*0.5307027145))))*e
        cdf=jnp.where(x>=0,1.0-q,q)
    return x*cdf, cdf+x*e*0.3989422804014327
def norm(r):
    c=r-jnp.mean(r,axis=-1,keepdims=True)
    s=lax.rsqrt(jnp.mean(c*c,axis=-1,keepdims=True)+1e-05)
    return c*s,s
def norm_bwd(up,u,s,g):
    p=up*g
    return (p-jnp.mean(p,axis=-1,keepdims=True)-u*jnp.mean(p*u,axis=-1,keepdims=True))*s
def whole(a): return pl.BlockSpec(memory_space=pltpu.VMEM)
def qkv_kernel(TR,hid_ref,w_ref,vec_ref,o_ref):
    D=hid_ref.shape[1]
    x=hid_ref[...]
    o_ref[:,:D]=((dg(x,w_ref[:,:D])+vec_ref[QB:QB+1,:])*0.125).astype(bf)
    o_ref[:,D:2*D]=dg(x,w_ref[:,D:2*D]).astype(bf)
    o_ref[:,2*D:]=(dg(x,w_ref[:,2*D:])+vec_ref[VB:VB+1,:]).astype(bf)
def qkv_fwd(hid,w,vec,TR=256):
    R,D=hid.shape;N=w.shape[1]
    return pl.pallas_call(functools.partial(qkv_kernel,TR),grid=(R//TR,),
        in_specs=[pl.BlockSpec((TR,D),lambda i:(i,0)),pl.BlockSpec((D,N),lambda i:(0,0)),pl.BlockSpec(vec.shape,lambda i:(0,0))],
        out_specs=pl.BlockSpec((TR,N),lambda i:(i,0)),out_shape=jax.ShapeDtypeStruct((R,N),bf),
        compiler_params=pltpu.CompilerParams(vmem_limit_bytes=56*2**20))(hid,w,vec)
def post_kernel(TR,mode,len_ref,mix_ref,hid_ref,ow_ref,uw_ref,dw_ref,vec_ref,lo_ref,u1_ref,u2_ref,sc_ref,nl_ref,act_ref,gp_ref,fr_ref):
    D=hid_ref.shape[1];F=uw_ref.shape[1]
    i=pl.program_id(0)
    vec=lambda n: vec_ref[n:n+1,:]
    r=hid_ref[...].astype(f32)+(dg(mix_ref[...],ow_ref[...])+vec(OB))
    u1,s1=norm(r)
    u1_ref[...]=u1
    n=u1*vec(G1)+vec(S1)
    nl=n.astype(bf)
    nl_ref[...]=nl
    br=None
    for c in range(F//D):
        x=dg(nl,uw_ref[:,c*D:(c+1)*D])+vec(UB+c)
        a,gp=gelu_both(x,mode)
        a=a.astype(bf)
        act_ref[:,c*D:(c+1)*D]=a
        gp_ref[:,c*D:(c+1)*D]=gp.astype(bf)
        b=dg(a,dw_ref[c*D:(c+1)*D,:])
        br=b if br is None else br+b
    u2,s2=norm(n+(br+vec(DB)))
    u2_ref[...]=u2
    fin=u2*vec(G2)+vec(S2)
    row=lax.broadcasted_iota(jnp.int32,(TR,D),0)+i*TR
    lo_ref[...]=jnp.where(row<len_ref[0],fin,0.0).astype(bf)
    lane=lax.broadcasted_iota(jnp.int32,(TR,128),1)
    sc_ref[...]=jnp.where(lane==0,s1,s2)
    @pl.when(i==0)
    def _():
        fr_ref[...]=fin[:8]
def post_fwd(length,mixed,hid,ow,uw,dw,vec,TR=256,mode="poly"):
    R,D=hid.shape;F=uw.shape[1]
    rb=lambda n: pl.BlockSpec((TR,n),lambda i:(i,0))
    cb=lambda a: pl.BlockSpec(a.shape,lambda i:(0,0))
    sd=jax.ShapeDtypeStruct
    return pl.pallas_call(functools.partial(post_kernel,TR,mode),grid=(R//TR,),
        in_specs=[pl.BlockSpec(memory_space=pltpu.SMEM),rb(D),rb(D),cb(ow),cb(uw),cb(dw),cb(vec)],
        out_specs=[rb(D),rb(D),rb(D),rb(128),rb(D),rb(F),rb(F),pl.BlockSpec((8,D),lambda i:(0,0))],
        out_shape=[sd((R,D),bf),sd((R,D),f32),sd((R,D),f32),sd((R,128),f32),sd((R,D),bf),sd((R,F),bf),sd((R,F),bf),sd((8,D),f32)],
        compiler_params=pltpu.CompilerParams(vmem_limit_bytes=60*2**20))(length,mixed,hid,ow,uw,dw,vec)
def pbwd_kernel(TR,len_ref,gs_ref,og_ref,u1_ref,u2_ref,sc_ref,mix_ref,nl_ref,act_ref,gp_ref,ow_ref,uw_ref,dw_ref,vec_ref,
                gr1_ref,gm_ref,vg_ref,ddw_ref,duw_ref,dow_ref, gb_s,gi_s,ga_s,mix_s,nl_s,act_s):
    D=og_ref.shape[1];F=uw_ref.shape[1]
    i=pl.program_id(0);n=pl.num_programs(0)
    vec=lambda k: vec_ref[k:k+1,:]
    row=lax.broadcasted_iota(jnp.int32,(TR,D),0)+i*TR
    gf=og_ref[...].astype(f32)
    gf=gf+jnp.where(row==0,gs_ref[0]*vec(SW),0.0)
    gf=jnp.where(row<len_ref[0],gf,0.0)
    @pl.when(i==0)
    def _(): vg_ref[...]=jnp.zeros_like(vg_ref)
    def add(k,v): vg_ref[k:k+1,:]+=jnp.sum(v,axis=0,keepdims=True)
    u2=u2_ref[...]; s1=sc_ref[:,0:1]; s2=sc_ref[:,1:2]
    add(G2,gf*u2); add(S2,gf)
    gr2=norm_bwd(gf,u2,s2,vec(G2))
    gb=gr2.astype(bf)
    here=pl.ds(pl.multiple_of(i*TR,TR),TR)
    gb_s[here,:]=gb; mix_s[here,:]=mix_ref[...]; nl_s[here,:]=nl_ref[...]; act_s[here,:]=act_ref[...]
    add(DB,gb.astype(f32))
    gn=gr2
    for c in range(F//D):
        ga=dg(gb,dw_ref[c*D:(c+1)*D,:],NT)
        gi=(ga*gp_ref[:,c*D:(c+1)*D].astype(f32)).astype(bf)
        gi_s[here,c*D:(c+1)*D]=gi
        add(UB+c,gi.astype(f32))
        gn=gn+dg(gi,uw_ref[:,c*D:(c+1)*D],NT)
    u1=u1_ref[...]
    add(G1,gn*u1); add(S1,gn)
    gr1=norm_bwd(gn,u1,s1,vec(G1))
    gr1_ref[...]=gr1
    ga=gr1.astype(bf)
    ga_s[here,:]=ga
    add(OB,ga.astype(f32))
    gm_ref[...]=dg(ga,ow_ref[...],NT).astype(bf)
    @pl.when(i==n-1)
    def _():
        gball=gb_s[...]
        for c in range(F//D):
            ddw_ref[c*D:(c+1)*D,:]=dg(act_s[:,c*D:(c+1)*D],gball,TN).astype(ddw_ref.dtype)
        nlall=nl_s[...]
        for c in range(F//D):
            duw_ref[:,c*D:(c+1)*D]=dg(nlall,gi_s[:,c*D:(c+1)*D],TN).astype(duw_ref.dtype)
        dow_ref[...]=dg(mix_s[...],ga_s[...],TN).astype(dow_ref.dtype)
def post_bwd(length,gs,og,u1,u2,sc,mixed,nl,act,gp,ow,uw,dw,vec,TR=256):
    R,D=og.shape;F=uw.shape[1]
    rb=lambda n: pl.BlockSpec((TR,n),lambda i:(i,0))
    cb=lambda a: pl.BlockSpec(a.shape,lambda i:(0,0),pipeline_mode=pl.Buffered(1))
    sd=jax.ShapeDtypeStruct
    sm=pl.BlockSpec(memory_space=pltpu.SMEM)
    return pl.pallas_call(functools.partial(pbwd_kernel,TR),grid=(R//TR,),
        in_specs=[sm,sm,rb(D),rb(D),rb(D),rb(128),rb(D),rb(D),rb(F),rb(F),cb(ow),cb(uw),cb(dw),cb(vec)],
        out_specs=[rb(D),rb(D),cb(sd((16,D),f32)),cb(sd((F,D),f32)),cb(sd((D,F),f32)),cb(sd((D,D),f32))],
        out_shape=[sd((R,D),f32),sd((R,D),bf),sd((16,D),f32),sd((F,D),bf),sd((D,F),bf),sd((D,D),bf)],
        scratch_shapes=[pltpu.VMEM((R,D),bf),pltpu.VMEM((R,F),bf),pltpu.VMEM((R,D),bf),pltpu.VMEM((R,D),bf),pltpu.VMEM((R,D),bf),pltpu.VMEM((R,F),bf)],
        compiler_params=pltpu.CompilerParams(vmem_limit_bytes=62*2**20))(length,gs,og,u1,u2,sc,mixed,nl,act,gp,ow,uw,dw,vec)
def dqkv_kernel(TR,hid_ref,gq_ref,gk_ref,gv_ref,gr1_ref,w_ref,hg_ref,dw_ref,vb_ref,x_s,g_s):
    D=hid_ref.shape[1]
    i=pl.program_id(0);n=pl.num_programs(0)
    here=pl.ds(pl.multiple_of(i*TR,TR),TR)
    x_s[here,:]=hid_ref[...]
    acc=gr1_ref[...]
    @pl.when(i==0)
    def _(): vb_ref[...]=jnp.zeros_like(vb_ref)
    for c,r in enumerate((gq_ref,gk_ref,gv_ref)):
        g=r[...]
        g_s[here,c*D:(c+1)*D]=g
        acc=acc+dg(g,w_ref[:,c*D:(c+1)*D],NT)
        if c!=1: vb_ref[c//2:c//2+1,:]+=jnp.sum(g.astype(f32),axis=0,keepdims=True)
    hg_ref[...]=acc.astype(bf)
    @pl.when(i==n-1)
    def _():
        x=x_s[...]
        for c in range(3):
            dw_ref[:,c*D:(c+1)*D]=dg(x,g_s[:,c*D:(c+1)*D],TN).astype(bf)
def dqkv(hid,gq,gk,gv,gr1,w,TR=256):
    R,D=hid.shape;N=w.shape[1]
    rb=lambda n: pl.BlockSpec((TR,n),lambda i:(i,0))
    sd=jax.ShapeDtypeStruct
    return pl.pallas_call(functools.partial(dqkv_kernel,TR),grid=(R//TR,),
        in_specs=[rb(D)]*5+[pl.BlockSpec((D,N),lambda i:(0,0))],
        out_specs=[rb(D),pl.BlockSpec((D,N),lambda i:(0,0)),pl.BlockSpec((8,D),lambda i:(0,0))],
        out_shape=[sd((R,D),bf),sd((D,N),bf),sd((8,D),f32)],
        scratch_shapes=[pltpu.VMEM((R,D),bf),pltpu.VMEM((R,N),bf)],
        compiler_params=pltpu.CompilerParams(vmem_limit_bytes=60*2**20))(hid,gq,gk,gv,gr1,w)

def listwise(scores, weights, counts):
    slots = scores.shape[1]
    live = jnp.arange(slots, dtype=jnp.float32)[None, :] < counts[:, None]
    share = jnp.where(live, weights, 0.0)
    target = share / jnp.sum(share, axis=1, keepdims=True)
    masked = jnp.where(live, scores, -1e30)
    top = jnp.max(masked, axis=1, keepdims=True)
    lognorm = top + jnp.log(jnp.sum(jnp.exp(masked - top), axis=1, keepdims=True))
    entropy = lognorm[:, 0] - jnp.sum(target * scores, axis=1)
    probs = jnp.where(live, jnp.exp(masked - lognorm), 0.0)
    return (entropy, probs - target)


def shards(hidden, lengths, counts, targets, out_grad, qkv_weight, qv_bias, out_weight, out_bias,
           norm1_gain, norm1_bias, up_weight, up_bias, down_weight, down_bias, norm2_gain,
           norm2_bias, rel_bias, score_weight):
    ALL = ("pb", "col")
    _, _, S, D = hidden.shape
    n_dev = lax.axis_size(ALL)
    dev = lax.axis_index(ALL)
    d1 = D // n_dev
    tokens = hidden.reshape(S, D)
    length = lengths.reshape(1)
    small = jnp.concatenate([qv_bias.reshape(-1), out_bias, norm1_gain, norm1_bias, down_bias, norm2_gain, norm2_bias, score_weight, up_bias])
    small = lax.all_gather(small, ALL, axis=0)
    body = small[:, : 9 * d1].reshape(n_dev, 9, d1).transpose(1, 0, 2).reshape(9, D)
    ups = small[:, 9 * d1 :].reshape(-1, D)
    vec = jnp.concatenate([body, ups, jnp.zeros((16 - 9 - ups.shape[0], D), body.dtype)], axis=0).astype(f32)
    gather = lambda w: lax.all_gather(w, ALL, axis=0, tiled=True)
    qkv_w, out_w, up_w, down_w = map(gather, (qkv_weight, out_weight, up_weight, down_weight))
    strips, kx = tables(rel_bias, length[0], S)
    qkv = qkv_fwd(tokens, qkv_w, vec)
    mixed, linv, mixed_f, probs = attn_fwd(qkv, kx, strips, BQ=512)
    layer_out, u1, u2, sc, nl, act, gp, first = post_fwd(length, mixed, tokens, out_w, up_w, down_w, vec, mode="erf")
    own_score = jnp.sum(first[0] * vec[SW])
    count_f = counts.astype(f32)
    near_scores = lax.all_gather(own_score.reshape(1, 1), "col", axis=1, tiled=True)
    near_targets = lax.all_gather(targets, "col", axis=1, tiled=True)
    entropy, difference = listwise(near_scores, near_targets, count_f)
    weighted, total_count = lax.psum((count_f[0] * entropy[0], count_f[0]), "pb")
    loss = weighted / total_count
    gs = lax.dynamic_slice_in_dim(count_f[0] / total_count * difference[0], lax.axis_index("col"), 1)
    gr1, gm, vg, d_down, d_up, d_out = post_bwd(length, gs, out_grad.reshape(S, D), u1, u2, sc, mixed, nl, act, gp, out_w, up_w, down_w, vec)
    dq, dk, dv, near, far = attn_bwd(qkv, gm, mixed_f, linv, probs, BQ=512)
    hidden_grad, d_qkv, vb = dqkv(tokens, dq, dk, dv, gr1, qkv_w)
    ids = strip_ids()
    onehot = (ids[:, :, None] == jnp.arange(rel_bias.shape[0], dtype=jnp.int32)).astype(f32)
    bucket = jnp.einsum("hac,acb->bh", near, onehot, precision=lax.Precision.HIGHEST)
    far = jnp.sum(far, axis=2)
    bucket = bucket.at[15].add(far[:, 0]).at[31].add(far[:, 1])
    scatter = lambda w: lax.psum_scatter(w, ALL, scatter_dimension=0, tiled=True).astype(f32)
    d_down, d_up, d_out, d_qkv = map(scatter, (d_down, d_up, d_out, d_qkv))
    score_grad = gs[0] * first[:1]
    smalls = lax.psum(jnp.concatenate([vg, vb[:2], score_grad], axis=0), ALL)
    bucket = lax.psum(bucket, ALL)
    part = lax.dynamic_slice_in_dim(smalls, dev * d1, d1, axis=1)
    f1 = up_bias.shape[0]
    up_bias_grad = lax.dynamic_slice_in_dim(smalls[UB : UB + 4].reshape(-1), dev * f1, f1)
    return (layer_out.reshape(hidden.shape), loss, hidden_grad.reshape(hidden.shape), d_qkv, part[16:18],
            d_out, part[OB], part[G1], part[S1], d_up, up_bias_grad, d_down, part[DB], part[G2], part[S2],
            bucket, part[18])


def solution(mesh):
    lead = P(("pb", "col"))
    row = P(("pb", "col"), None)
    act = P("pb", "col", None, None)
    side = P(None, ("pb", "col"))
    return jax.shard_map(
        shards,
        mesh=mesh,
        in_specs=(act, P("pb", "col"), P("pb"), P("pb", "col"), act, row, side, row, lead, lead, lead, row, lead, row, lead, lead, lead, P(), lead),
        out_specs=(act, P(), act, row, side, row, lead, lead, lead, row, lead, row, lead, lead, lead, P(), lead),
        check_vma=False,
    )
```

```python
import functools

import jax
import jax.numpy as jnp
from jax import lax
from jax.experimental import pallas as pl
from jax.experimental.pallas import tpu as pltpu
from jax.sharding import PartitionSpec as P

f32=jnp.float32; bf=jnp.bfloat16
NT=(((1,),(1,)),((),())); NN=(((1,),(0,)),((),())); TN=(((0,),(0,)),((),()))
T=128
EDGES = (1, 2, 3, 4, 5, 6, 7, 8, 12, 16, 23, 32, 45, 64, 91)
def strip_ids():
    r=jnp.arange(3*T,dtype=jnp.int32)[None,:]-T-jnp.arange(T,dtype=jnp.int32)[:,None]
    m=jnp.abs(r); ids=jnp.where(r>0,16,0).astype(jnp.int32)
    for e in EDGES: ids=ids+(m>=e).astype(jnp.int32)
    return ids
def tables(rel_bias, length, S):
    ids=strip_ids()
    nb=rel_bias.shape[0]
    oh=(ids[None]==jnp.arange(nb,dtype=jnp.int32)[:,None,None]).astype(bf)
    strips=jnp.einsum("bac,bh->hac",oh,rel_bias,preferred_element_type=f32)
    j=jnp.arange(S,dtype=jnp.int32)[:,None]; lane=jnp.arange(128,dtype=jnp.int32)[None,:]
    jb=j//T; nblk=S//T
    low=(jb<=lane-2)&(lane<nblk); up=(jb>=lane+2)&(lane<nblk)
    mk=jnp.where((lane==nblk)&(j>=length),-1e30,0.0)
    rb=rel_bias.astype(f32)
    kx=jnp.where(low[None],rb[15][:,None,None],jnp.where(up[None],rb[31][:,None,None],mk[None])).astype(bf)
    return strips,kx
def fwd_kernel(BQ, S, q_ref,k_ref,v_ref,kx_ref,st_ref,mix_ref,linv_ref,mf_ref,p_ref):
    nblk=S//T
    lane=lax.broadcasted_iota(jnp.int32,(1,128),1)
    row=lax.broadcasted_iota(jnp.int32,(BQ,128),0)//T
    lane2=lax.broadcasted_iota(jnp.int32,(BQ,128),1)
    q=q_ref[...];k=k_ref[...];v=v_ref[...]
    masks=[lane<64,lane>=64]
    kaug=[jnp.concatenate([k,kx_ref[h]],axis=1) for h in (0,1)]
    vaug=[jnp.where(masks[h],v,jnp.ones_like(v)) for h in (0,1)]
    for i in range(S//BQ):
        outs=[]
        qi=q[i*BQ:(i+1)*BQ]
        qx=((lane2==nblk)|(lane2==row+i*(BQ//T))).astype(f32).astype(bf)
        for h in (0,1):
            qa=jnp.concatenate([jnp.where(masks[h],qi,jnp.zeros_like(qi)),qx],axis=1)
            s=dg(qa,kaug[h],NT)
            rows=[]
            for b in range(BQ//T):
                I=i*(BQ//T)+b
                lo=max(0,(I-1)*T);hi=min(S,(I+2)*T)
                sb=s[b*T:(b+1)*T]
                parts=[]
                if lo>0: parts.append(sb[:,:lo])
                parts.append(sb[:,lo:hi]+st_ref[h,:,lo-(I-1)*T:hi-(I-1)*T])
                if hi<S: parts.append(sb[:,hi:])
                rows.append(jnp.concatenate(parts,axis=1) if len(parts)>1 else parts[0])
            s=jnp.concatenate(rows,axis=0) if len(rows)>1 else rows[0]
            m=jnp.max(s,axis=1,keepdims=True)
            p=jnp.exp(s-m).astype(bf)
            p_ref[h,i*BQ:(i+1)*BQ,:]=p
            outs.append(dg(p,vaug[h],NN))
        o0,o1=outs
        num=jnp.where(masks[0],o0,o1)
        den=jnp.where(masks[0],o1,o0)
        den=pltpu.roll(den,64,1)
        linv=1.0/den
        mf=num*linv
        mf_ref[i*BQ:(i+1)*BQ,:]=mf
        mix_ref[i*BQ:(i+1)*BQ,:]=mf.astype(bf)
        linv_ref[i*BQ:(i+1)*BQ,:]=linv
def attn_fwd(qkv,kx,strips,p0,n,BQ=512):
    S,W=qkv.shape; npair=W//3//128
    blk=lambda o: pl.BlockSpec((S,128),lambda p:(0,o*npair+p0+p))
    out=pl.BlockSpec((S,128),lambda p:(0,p))
    return pl.pallas_call(functools.partial(fwd_kernel,BQ,S),cost_estimate=takes(n*FAST),grid=(n,),
        in_specs=[blk(0),blk(1),blk(2),pl.BlockSpec((2,S,128),lambda p:(p0+p,0,0)),pl.BlockSpec((2,T,3*T),lambda p:(p0+p,0,0))],
        out_specs=[out]*3+[pl.BlockSpec((2,S,S),lambda p:(p,0,0))],
        out_shape=[sd((S,n*128),bf),sd((S,n*128),f32),sd((S,n*128),f32),sd((2*n,S,S),bf)],
        compiler_params=pltpu.CompilerParams(vmem_limit_bytes=56*2**20),
        )(qkv,qkv,qkv,kx,strips)
def bwd_kernel(BQ,S,form,scale,kscale,q_ref,k_ref,v_ref,gm_ref,mf_ref,linv_ref,p_ref,dq_ref,dk_ref,dv_ref,near_ref,far_ref,ds_ref):
    nblk=S//T
    lane=lax.broadcasted_iota(jnp.int32,(1,128),1)
    lanes=lax.broadcasted_iota(jnp.int32,(S,128),1)
    rows=lax.broadcasted_iota(jnp.int32,(S,128),0)
    masks=[lane<64,lane>=64]
    q=q_ref[...];k=k_ref[...];v=v_ref[...]
    gm=gm_ref[...].astype(f32);linv=linv_ref[...]
    do=(gm*linv).astype(bf)
    t=do.astype(f32)*mf_ref[...]
    kind=(lanes==rows//T).astype(f32).astype(bf)
    kaug=jnp.concatenate([k,kind],axis=1)
    vx=jnp.where(lanes<2,1.0,0.0).astype(bf)
    vaug=jnp.concatenate([v,vx],axis=1)
    dqs=[];dks=[];dvs=[]
    if form=="T":
        qT=q.T; doT=do.T
    for h in (0,1):
        delta=jnp.sum(jnp.where(masks[h],t,0.0),axis=1,keepdims=True)
        hi=delta.astype(bf).astype(f32); lo=delta-hi
        ex=jnp.where(lanes==0,-hi,jnp.where(lanes==1,-lo,0.0)).astype(bf)
        da=jnp.concatenate([jnp.where(masks[h],do,jnp.zeros_like(do)),ex],axis=1)
        near=[jnp.zeros((T,T),f32) for _ in range(3)]
        dq=[]
        for i in range(S//BQ):
            x=dg(da[i*BQ:(i+1)*BQ],vaug,NT)
            ds=p_ref[h,i*BQ:(i+1)*BQ,:]*x.astype(bf)
            ds_ref[i*BQ:(i+1)*BQ,:]=ds
            dq.append(dg(ds,kaug,NN))
            for b in range(BQ//T):
                I=i*(BQ//T)+b
                for n in (-1,0,1):
                    if 0<=I+n<nblk:
                        near[n+1]=near[n+1]+ds[b*T:(b+1)*T,(I+n)*T:(I+n+1)*T].astype(f32)
        for n in range(3): near_ref[h,:,n*T:(n+1)*T]=near[n]
        dq=jnp.concatenate(dq,axis=0)
        dqs.append(dq[:,:128])
        far=dq[:,128:]
        ib=rows//T
        far_ref[h,0:1,:]=jnp.sum(jnp.where(lanes<=ib-2,far,0.0),axis=0,keepdims=True)
        far_ref[h,1:2,:]=jnp.sum(jnp.where((lanes>=ib+2)&(lanes<nblk),far,0.0),axis=0,keepdims=True)
        far_ref[h,2:8,:]=jnp.zeros((6,128),f32)
        if form=="T":
            dks.append(dg(qT[h*64:(h+1)*64],ds_ref[...],NN))
            dvs.append(dg(doT[h*64:(h+1)*64],p_ref[h],NN))
        else:
            dks.append(dg(ds_ref[...],q,TN))
            dvs.append(dg(p_ref[h],do,TN))
    dq_ref[...]=(jnp.where(masks[0],dqs[0],dqs[1])*scale).astype(bf)
    if form=="T":
        dk_ref[...]=(jnp.concatenate(dks,axis=0)*kscale).T.astype(bf)
        dv_ref[...]=jnp.concatenate(dvs,axis=0).T.astype(bf)
    else:
        dk_ref[...]=(jnp.where(masks[0],dks[0],dks[1])*kscale).astype(bf)
        dv_ref[...]=jnp.where(masks[0],dvs[0],dvs[1]).astype(bf)
def attn_bwd(qkv,gm,mixed,linv,p,p0,n,BQ=512,form="T",scale=0.125,kscale=1.0):
    S,W=qkv.shape; npair=W//3//128
    blk=lambda o: pl.BlockSpec((S,128),lambda i:(0,o*npair+p0+i))
    own=pl.BlockSpec((S,128),lambda i:(0,i))
    return pl.pallas_call(functools.partial(bwd_kernel,BQ,S,form,scale,kscale),cost_estimate=takes(n*FAST),grid=(n,),
        in_specs=[blk(0),blk(1),blk(2),blk(0),own,own,pl.BlockSpec((2,S,S),lambda i:(i,0,0))],
        out_specs=[own]*3+[pl.BlockSpec((2,T,3*T),lambda i:(i,0,0)),pl.BlockSpec((2,8,128),lambda i:(i,0,0))],
        out_shape=[sd((S,n*128),bf)]*3+[sd((2*n,T,3*T),f32),sd((2*n,8,128),f32)],
        scratch_shapes=[pltpu.VMEM((S,S),bf)],
        compiler_params=pltpu.CompilerParams(vmem_limit_bytes=56*2**20),
        )(qkv,qkv,qkv,gm,mixed,linv,p)
sd=jax.ShapeDtypeStruct
FAST=1.0
def takes(us): return pl.CostEstimate(flops=int(us*1.15e9),bytes_accessed=int(us*1e6),transcendentals=0)
def dg(a,b,d=NN): return lax.dot_general(a,b,d,preferred_element_type=f32)
QB,VB,OB,G1,S1,DB,G2,S2,SW,UB,CT,TG,NV=0,1,2,3,4,5,6,7,8,9,13,14,24
def gelu_both(x,mode="poly"):
    e=jnp.exp(x*x*-0.5)
    if mode=="erf":
        cdf=0.5*(1.0+lax.erf(x*0.7071067811865476))
    else:
        t=1.0/(1.0+(0.3275911*0.7071067811865476)*jnp.abs(x))
        q=t*(0.127414796+t*(-0.142248368+t*(0.7107068705+t*(-0.7265760135+t*0.5307027145))))*e
        cdf=jnp.where(x>=0,1.0-q,q)
    return x*cdf, cdf+x*e*0.3989422804014327
def norm(r):
    c=r-jnp.mean(r,axis=-1,keepdims=True)
    s=lax.rsqrt(jnp.mean(c*c,axis=-1,keepdims=True)+1e-05)
    return c*s,s
def norm_bwd(up,u,s,g):
    p=up*g
    return (p-jnp.mean(p,axis=-1,keepdims=True)-u*jnp.mean(p*u,axis=-1,keepdims=True))*s
def whole(a): return pl.BlockSpec(memory_space=pltpu.VMEM)

BLK=16
RELA=((0,0,0),(0,0,1),(0,1,0),(0,1,1))
RELB=((0,0,2),(0,0,3),(1,0,2),(1,0,3))
RELXA=((1,0,0),(1,0,1),(1,1,0),(1,1,1))
RELYB=((0,1,2),(0,1,3),(1,1,2),(1,1,3))
RELS=(RELA,RELB,RELXA,RELYB)
X_,Y_,Z_,C_=0,1,2,3
def place(pos,rel):
    xr,yr,zr=rel
    return (((pos[Z_]-zr)&3)*2+(pos[Y_]^yr))*2+(pos[X_]^xr)
def slot(pos,k):
    x,y,z=k&1,(k>>1)&1,k>>2
    xr,yr,zr=pos[X_]^x,pos[Y_]^y,(pos[Z_]-z)&3
    return jnp.where(zr<2,(1-xr)*8+yr*2+zr,2+(1-yr)*8+xr*2+zr)
def load(pos,pieces,parts,sem):
    for s in range(8):
        half=pos[C_] if s<4 else 1-pos[C_]
        for b,rel in enumerate(RELS[s%4]):
            k=place(pos,rel)
            R=pieces[s].shape[1]
            rows=pl.ds(pl.multiple_of(k*R,R),R)
            for off,w,dst in parts:
                cols=pl.ds(pl.multiple_of(half*w,w),w)
                pltpu.make_async_copy(pieces[s].at[b,:,pl.ds(off,w)],dst.at[rows,cols],sem).start()
def arrived(dst,sem):
    pltpu.make_async_copy(dst,dst,sem).wait()
ANYS=pl.BlockSpec(memory_space=pltpu.HBM)
SMEM=pl.BlockSpec(memory_space=pltpu.SMEM)
def qkv_kernel(pos,*refs):
    pieces=refs[:8]; hid_ref,o_ref,vec_ref,w_s,sm_s,sems=refs[8:]
    D=hid_ref.shape[1]; N=3*D
    @pl.when(pl.program_id(0)==0)
    def _():
        for s in range(4):
            for b,rel in enumerate(RELS[s]):
                R=pieces[s].shape[1]
                rows=pl.ds(pl.multiple_of(place(pos,rel)*R,R),R)
                pltpu.make_async_copy(pieces[s].at[b,:,pl.ds(N//2,128)],sm_s.at[rows,:],sems.at[1]).start()
        load(pos,pieces,[(0,N//2,w_s)],sems.at[0])
        arrived(sm_s,sems.at[1])
        vec_ref[...]=sm_s[...].astype(f32).T[:NV]
        arrived(w_s,sems.at[0])
    x=hid_ref[...]
    o_ref[:,:D]=((dg(x,w_s[:,:D])+vec_ref[QB:QB+1,:])*0.125).astype(bf)
    o_ref[:,D:2*D]=dg(x,w_s[:,D:2*D]).astype(bf)
    o_ref[:,2*D:]=(dg(x,w_s[:,2*D:])+vec_ref[VB:VB+1,:]).astype(bf)
def qkv_fwd(pos,pieces,hid,TR=256):
    R,D=hid.shape;N=3*D
    return pl.pallas_call(qkv_kernel,cost_estimate=takes(FAST),grid=(R//TR,),
        in_specs=[SMEM]+[ANYS]*8+[pl.BlockSpec((TR,D),lambda i:(i,0))],
        out_specs=[pl.BlockSpec((TR,N),lambda i:(i,0)),pl.BlockSpec((NV,D),lambda i:(0,0))],
        out_shape=[sd((R,N),bf),sd((NV,D),f32)],
        scratch_shapes=[pltpu.VMEM((D,N),bf),pltpu.VMEM((D,128),bf),pltpu.SemaphoreType.DMA((2,))],
        compiler_params=pltpu.CompilerParams(vmem_limit_bytes=56*2**20))(pos,*pieces,hid)
def fetch(w,off,dst,sem):
    pltpu.make_async_copy(w.at[:,pl.ds(off,dst.shape[1])],dst,sem).start()
def fetch_down(w,off,dst,sems):
    D=dst.shape[1]
    for j in range(dst.shape[0]//D):
        pltpu.make_async_copy(w.at[:,pl.ds(off+j*D,D)],dst.at[pl.ds(j*D,D),:],sems.at[j]).start()
def arrived_down(dst,sems):
    D=dst.shape[1]
    for j in range(dst.shape[0]//D):
        arrived(dst.at[pl.ds(j*D,D),:],sems.at[j])
def post_kernel(TR,mode,len_ref,*refs):
    w,m0,m1,m2,hid_ref,vec_ref,lo_ref,u1_ref,u2_ref,sc_ref,nl_ref,act_ref,gp_ref,fr_ref,os_ref,ow_ref,uw_ref,dw_ref,sems=refs
    D=hid_ref.shape[1];F=uw_ref.shape[1]
    i=pl.program_id(0)
    @pl.when(i==0)
    def _():
        fetch(w,0,ow_ref,sems.at[4])
        fetch(w,D,uw_ref,sems.at[5])
        fetch_down(w,D+F,dw_ref,sems)
        arrived(ow_ref,sems.at[4])
        arrived(uw_ref,sems.at[5])
        arrived_down(dw_ref,sems)
    vec=lambda n: vec_ref[n:n+1,:]
    r=hid_ref[...].astype(f32)+(dg(jnp.concatenate([m0[...],m1[...],m2[...]],axis=1),ow_ref[...])+vec(OB))
    u1,s1=norm(r)
    u1_ref[...]=u1
    n=u1*vec(G1)+vec(S1)
    nl=n.astype(bf)
    nl_ref[...]=nl
    br=None
    for c in range(F//D):
        x=dg(nl,uw_ref[:,c*D:(c+1)*D])+vec(UB+c)
        a,gp=gelu_both(x,mode)
        a=a.astype(bf)
        act_ref[:,c*D:(c+1)*D]=a
        gp_ref[:,c*D:(c+1)*D]=gp.astype(bf)
        b=dg(a,dw_ref[c*D:(c+1)*D,:])
        br=b if br is None else br+b
    u2,s2=norm(n+(br+vec(DB)))
    u2_ref[...]=u2
    fin=u2*vec(G2)+vec(S2)
    row=lax.broadcasted_iota(jnp.int32,(TR,D),0)+i*TR
    lo_ref[...]=jnp.where(row<len_ref[0],fin,0.0).astype(bf)
    lane=lax.broadcasted_iota(jnp.int32,(TR,128),1)
    sc_ref[...]=jnp.where(lane==0,s1,s2)
    @pl.when(i==0)
    def _():
        fr_ref[...]=fin[:8]
        own=jnp.sum(fin[:1]*vec(SW),axis=1,keepdims=True)
        os_ref[...]=jnp.broadcast_to(own,(8,128))
def post_fwd(length,w,mixed,hid,vec,TR=256,mode="erf"):
    R,D=hid.shape;F=4*D
    rb=lambda n: pl.BlockSpec((TR,n),lambda i:(i,0))
    cb=lambda a: pl.BlockSpec(a.shape,lambda i:(0,0))
    return pl.pallas_call(functools.partial(post_kernel,TR,mode),cost_estimate=takes(FAST),grid=(R//TR,),
        in_specs=[SMEM,ANYS]+[rb(m.shape[1]) for m in mixed]+[rb(D),cb(vec)],
        out_specs=[rb(D),rb(D),rb(D),rb(128),rb(D),rb(F),rb(F),pl.BlockSpec((8,D),lambda i:(0,0)),pl.BlockSpec((8,128),lambda i:(0,0))],
        out_shape=[sd((R,D),bf),sd((R,D),f32),sd((R,D),f32),sd((R,128),f32),sd((R,D),bf),sd((R,F),bf),sd((R,F),bf),sd((8,D),f32),sd((8,128),f32)],
        scratch_shapes=[pltpu.VMEM((D,D),bf),pltpu.VMEM((D,F),bf),pltpu.VMEM((F,D),bf),pltpu.SemaphoreType.DMA((6,))],
        compiler_params=pltpu.CompilerParams(vmem_limit_bytes=60*2**20))(length,w,*mixed,hid,vec)
def listwise(pos,ncol,d1,scores,vec_ref,info_ref):
    lane=lax.broadcasted_iota(jnp.int32,(1,vec_ref.shape[1]),1)
    pb,col=pos[4],pos[5]
    counts=vec_ref[CT:CT+1,:]
    targets=vec_ref[TG:TG+1,:]+vec_ref[TG+1:TG+2,:]+vec_ref[TG+2:TG+3,:]
    pick=lambda row,dev: jnp.sum(jnp.where(lane==dev*d1,row,0.0),axis=1,keepdims=True)
    total=jnp.sum(counts,axis=1,keepdims=True)*(1.0/ncol)
    mine=pick(counts,pb*ncol)
    n=len(scores)
    live=[(col^r).astype(f32)<mine for r in range(n)]
    share=[jnp.where(live[r],pick(targets,pb*ncol+(col^r)),0.0) for r in range(n)]
    def pairs(f,v):
        while len(v)>1: v=[f(v[i],v[i+1]) for i in range(0,len(v),2)]
        return v[0]
    add=lambda a,b: a+b
    whole=pairs(add,share)
    masked=[jnp.where(live[r],scores[r],-1e30) for r in range(n)]
    top=pairs(jnp.maximum,masked)
    log=top+jnp.log(pairs(add,[jnp.exp(m-top) for m in masked]))
    entropy=log-pairs(add,[share[r]/whole*scores[r] for r in range(n)])
    prob=jnp.where(live[0],jnp.exp(masked[0]-log),0.0)
    gs=mine/total*(prob-share[0]/whole)
    weighted=jnp.where(col==0,mine*entropy,0.0)
    row=lax.broadcasted_iota(jnp.int32,(8,128),0)
    info_ref[...]=jnp.where(row==0,gs,jnp.where(row==1,weighted,total))
def back1_kernel(TR,ncol,d1,pos,len_ref,*refs):
    s_refs=refs[:ncol]
    (w,og_ref,u2_ref,sc_ref,act_ref,gp_ref,vec_ref,gr2_ref,gi_ref,vg_ref,kb_ref,sb_ref,info_ref,
     dw_ref,gb_s,act_s,sems)=refs[ncol:]
    D=og_ref.shape[1];F=act_ref.shape[1];H=D//2
    i=pl.program_id(0);n=pl.num_programs(0)
    @pl.when(i==0)
    def _():
        fetch_down(w,D+F,dw_ref,sems)
        listwise(pos,ncol,d1,[r[0:1,0:1] for r in s_refs],vec_ref,info_ref)
        vg_ref[...]=jnp.zeros_like(vg_ref)
        arrived_down(dw_ref,sems)
    vec=lambda k: vec_ref[k:k+1,:]
    row=lax.broadcasted_iota(jnp.int32,(TR,D),0)+i*TR
    gf=og_ref[...].astype(f32)
    gf=gf+jnp.where(row==0,info_ref[0:1,0:1]*vec(SW),0.0)
    gf=jnp.where(row<len_ref[0],gf,0.0)
    def add(k,v): vg_ref[k:k+1,:]+=jnp.sum(v,axis=0,keepdims=True)
    u2=u2_ref[...]; s2=sc_ref[:,1:2]
    add(G2,gf*u2); add(S2,gf)
    gr2=norm_bwd(gf,u2,s2,vec(G2))
    gr2_ref[...]=gr2
    gb=gr2.astype(bf)
    here=pl.ds(pl.multiple_of(i*TR,TR),TR)
    gb_s[here,:]=gb; act_s[here,:]=act_ref[...]
    add(DB,gb.astype(f32))
    for c in range(F//D):
        ga=dg(gb,dw_ref[c*D:(c+1)*D,:],NT)
        gi=(ga*gp_ref[:,c*D:(c+1)*D].astype(f32)).astype(bf)
        gi_ref[:,c*D:(c+1)*D]=gi
        add(UB+c,gi.astype(f32))
    @pl.when(i==n-1)
    def _():
        gball=gb_s[...]
        core=pos[C_]
        slots=[slot(pos,k) for k in range(BLK)]
        for ref,h in ((sb_ref,1-core),(kb_ref,core)):
            for c in range(F//D//2):
                cols=pl.ds(pl.multiple_of(h*(F//2)+c*D,D),D)
                t=dg(act_s[:,cols],gball,TN).astype(bf)
                for k in range(BLK):
                    ref[slots[k],:,c*D:(c+1)*D]=t[k*(D//BLK):(k+1)*(D//BLK)]
def whole1(a): return pl.BlockSpec(a.shape,lambda i:(0,)*len(a.shape),pipeline_mode=pl.Buffered(1))
def back1(pos,length,scores,d1,w,og,u2,sc,act,gp,vec,TR=256):
    R,D=og.shape;F=act.shape[1]
    rb=lambda n: pl.BlockSpec((TR,n),lambda i:(i,0))
    gb=sd((BLK,D//BLK,F//2),bf)
    return pl.pallas_call(functools.partial(back1_kernel,TR,len(scores),d1),cost_estimate=takes(FAST),grid=(R//TR,),
        in_specs=[SMEM]*2+[whole1(v) for v in scores]+[ANYS]+[rb(D),rb(D),rb(128),rb(F),rb(F),whole1(vec)],
        out_specs=[rb(D),rb(F),whole1(vec),whole1(gb),whole1(gb),whole1(scores[0])],
        out_shape=[sd((R,D),f32),sd((R,F),bf),vec,gb,gb,sd((8,128),f32)],
        scratch_shapes=[pltpu.VMEM((F,D),bf),pltpu.VMEM((R,D),bf),pltpu.VMEM((R,F),bf),pltpu.SemaphoreType.DMA((4,))],
        compiler_params=pltpu.CompilerParams(vmem_limit_bytes=62*2**20))(pos,length,*scores,w,og,u2,sc,act,gp,vec)
def back2_kernel(TR,*refs):
    (w,gr2_ref,u1_ref,sc_ref,gi_ref,vec_ref,gr1_ref,ga_ref,gm_ref,vg_ref,ow_ref,uw_ref,sems)=refs
    D=gr2_ref.shape[1]
    i=pl.program_id(0)
    @pl.when(i==0)
    def _():
        fetch(w,D,uw_ref,sems.at[0])
        fetch(w,0,ow_ref,sems.at[1])
        vg_ref[...]=jnp.zeros_like(vg_ref)
        arrived(uw_ref,sems.at[0])
        arrived(ow_ref,sems.at[1])
    vec=lambda k: vec_ref[k:k+1,:]
    def add(k,v): vg_ref[k:k+1,:]+=jnp.sum(v,axis=0,keepdims=True)
    gn=gr2_ref[...]+dg(gi_ref[...],uw_ref[...],NT)
    u1=u1_ref[...]
    add(G1,gn*u1); add(S1,gn)
    gr1=norm_bwd(gn,u1,sc_ref[:,0:1],vec(G1))
    gr1_ref[...]=gr1
    ga=gr1.astype(bf)
    ga_ref[...]=ga
    add(OB,ga.astype(f32))
    gm_ref[...]=dg(ga,ow_ref[...],NT).astype(bf)
def back2(w,gr2,u1,sc,gi,vec,TR=256):
    R,D=gr2.shape;F=gi.shape[1]
    rb=lambda n: pl.BlockSpec((TR,n),lambda i:(i,0))
    return pl.pallas_call(functools.partial(back2_kernel,TR),cost_estimate=takes(FAST),grid=(R//TR,),
        in_specs=[ANYS,rb(D),rb(D),rb(128),rb(F),whole1(vec)],
        out_specs=[rb(D),rb(D),rb(D),whole1(vec)],
        out_shape=[sd((R,D),f32),sd((R,D),bf),sd((R,D),bf),vec],
        scratch_shapes=[pltpu.VMEM((D,D),bf),pltpu.VMEM((D,F),bf),pltpu.SemaphoreType.DMA((2,))],
        compiler_params=pltpu.CompilerParams(vmem_limit_bytes=56*2**20))(w,gr2,u1,sc,gi,vec)
def wup_kernel(pos,m0,m1,m2,ga_ref,nl_ref,gi_ref,ka_ref,sa_ref,tmp_s):
    D=ga_ref.shape[1];F=gi_ref.shape[1];H=D//2
    core=pos[C_]
    slots=[slot(pos,k) for k in range(BLK)]
    mine,other=[pl.ds(pl.multiple_of(h*H,H),H) for h in (core,1-core)]
    nlall=nl_ref[...]
    for ref,h in ((sa_ref,1-core),(ka_ref,core)):
        for c in range(F//D//2):
            cols=pl.ds(pl.multiple_of(h*(F//2)+c*D,D),D)
            t=dg(nlall,gi_ref[:,cols],TN).astype(bf)
            for k in range(BLK):
                ref[slots[k],:,H+c*D:H+(c+1)*D]=t[k*(D//BLK):(k+1)*(D//BLK)]
    tmp_s[...]=dg(jnp.concatenate([m0[...],m1[...],m2[...]],axis=1),ga_ref[...],TN).astype(bf)
    for k in range(BLK):
        rows=slice(k*(D//BLK),(k+1)*(D//BLK))
        ka_ref[slots[k],:,:H]=tmp_s[rows,mine]
        sa_ref[slots[k],:,:H]=tmp_s[rows,other]
VM=pl.BlockSpec(memory_space=pltpu.VMEM)
def wup(pos,mixed,ga,nl,gi):
    R,D=ga.shape;F=gi.shape[1]
    o=sd((BLK,D//BLK,(D+F)//2),bf)
    return pl.pallas_call(wup_kernel,cost_estimate=takes(FAST),in_specs=[SMEM]+[VM]*6,out_specs=[VM]*2,out_shape=[o,o],
        scratch_shapes=[pltpu.VMEM((D,D),bf)],
        compiler_params=pltpu.CompilerParams(vmem_limit_bytes=56*2**20))(pos,*mixed,ga,nl,gi)
def wqkv_kernel(pos,hid_ref,*refs):
    parts=refs[:9]; k_ref,s_ref,vb_ref,g_s=refs[9:]
    D=hid_ref.shape[1];N=3*D
    vb_ref[...]=jnp.zeros_like(vb_ref)
    w=parts[0].shape[1]
    for j,r in enumerate(parts):
        g=r[...]
        g_s[:,j*w:(j+1)*w]=g
        row,lane=j//3,(j%3)*w
        if row!=1: vb_ref[row//2:row//2+1,lane:lane+w]=jnp.sum(g.astype(f32),axis=0,keepdims=True)
    x=hid_ref[...]
    core=pos[C_]
    slots=[slot(pos,k) for k in range(BLK)]
    for ref,h in ((s_ref,1-core),(k_ref,core)):
        t=dg(x,g_s[:,pl.ds(pl.multiple_of(h*(N//2),N//2),N//2)],TN).astype(bf)
        for k in range(BLK):
            ref[slots[k]]=t[k*(D//BLK):(k+1)*(D//BLK)]
def wqkv(pos,hid,parts):
    R,D=hid.shape;N=3*D
    g=sd((BLK,D//BLK,N//2),bf)
    return pl.pallas_call(wqkv_kernel,cost_estimate=takes(FAST),
        in_specs=[SMEM]+[VM]*10,out_specs=[VM]*3,out_shape=[g,g,sd((8,D),f32)],
        scratch_shapes=[pltpu.VMEM((R,N),bf)],
        compiler_params=pltpu.CompilerParams(vmem_limit_bytes=60*2**20))(pos,hid,*parts)
def hgrad_kernel(pos,*refs):
    pieces=refs[:8]
    parts=refs[8:17]; gr1_ref,hg_ref,w_s,sems=refs[17:]
    D=gr1_ref.shape[1];N=3*D
    @pl.when(pl.program_id(0)==0)
    def _():
        load(pos,pieces,[(0,N//2,w_s)],sems.at[0])
        arrived(w_s,sems.at[0])
    g=jnp.concatenate([r[...] for r in parts],axis=1)
    hg_ref[...]=(gr1_ref[...]+dg(g,w_s[...],NT)).astype(bf)
def hgrad(pos,pieces,parts,gr1,TR=256):
    R,D=gr1.shape;N=3*D
    rb=lambda n: pl.BlockSpec((TR,n),lambda i:(i,0))
    return pl.pallas_call(hgrad_kernel,cost_estimate=takes(FAST),grid=(R//TR,),
        in_specs=[SMEM]+[ANYS]*8+[rb(p.shape[1]) for p in parts]+[rb(D)],
        out_specs=rb(D),out_shape=sd((R,D),bf),
        scratch_shapes=[pltpu.VMEM((D,N),bf),pltpu.SemaphoreType.DMA((1,))],
        compiler_params=pltpu.CompilerParams(vmem_limit_bytes=60*2**20))(pos,*pieces,*parts,gr1)

ALL=("pb","col")
def staged():
    return lax.axis_size("pb")==8 and lax.axis_size("col")==4
def swap_core(v): return lax.ppermute(v,"col",[(i,i^1) for i in range(4)])
def swap_col(v,k): return lax.ppermute(v,"col",[(i,i^k) for i in range(lax.axis_size("col"))])
def swap_x(v): return lax.ppermute(v,"col",[(i,i^2) for i in range(4)])
def swap_y(v): return lax.ppermute(v,"pb",[(i,i^1) for i in range(8)])
def flip_z(v,m): return lax.ppermute(v,"pb",[(i,i^(2*m)) for i in range(8)])
def shift_z(v,k): return lax.ppermute(v,"pb",[(i,(i+2*k)%8) for i in range(8)])
def cat(a): return jnp.concatenate(a,axis=0)
def after(v,*first):
    return lax.optimization_barrier((v,)+first)[0]
def spread1(block):
    o=block[None]
    return [o,shift_z(o,1),shift_z(o,2),shift_z(o,3)]
def spread2(v):
    a=cat(v[:2]);b=cat(v[2:])
    return [cat([a,swap_y(a)]),cat([b,swap_x(b)])]
def spread3(v):
    a,b=v
    return [a,b,swap_x(a),swap_y(b)]
def spread4(own):
    return own+[swap_core(v) for v in own]
def own_order():
    zero=(0,0,0,0)
    return [[place(zero,rel) for rel in rels] for rels in RELS]
def spread_plain(full):
    out=[]
    for half in (0,1):
        cols=jnp.concatenate([w.reshape(BLK,w.shape[0]//BLK,2,w.shape[1]//2)[:,:,half] for w in full],axis=2)
        for order in own_order():
            out.append(jnp.stack([cols[k] for k in order]))
    return out
def add2(a,b): return (a.astype(f32)+b.astype(f32)).astype(bf)
def collect1(keep,r):
    sa,sb,ka,kb=[add2(keep[4*s:4*s+4],r[4*s:4*s+4]) for s in range(4)]
    return ka,kb,swap_x(sa),swap_y(sb)
def collect2(ka,kb,ra,rb):
    ka2,sa2=add2(ka[:2],ra[:2]),add2(ka[2:],ra[2:])
    kb2,sb2=add2(kb[:2],rb[:2]),add2(kb[2:],rb[2:])
    return ka2,kb2,swap_y(sa2),swap_x(sb2)
def collect3(ka2,kb2,ra,rb):
    t0=ka2[0].astype(f32)+ra[0].astype(f32)
    t1=add2(ka2[1],ra[1])
    t2=add2(kb2[0],rb[0]);t3=add2(kb2[1],rb[1])
    return t0,shift_z(t1,3),shift_z(t2,2),shift_z(t3,1)
def collect4(t0,t1,t2,t3):
    t=t0+t1.astype(f32)+t2.astype(f32)+t3.astype(f32)
    c=lax.axis_index("col")&1
    h=t.shape[0]//2
    mine=lax.dynamic_slice_in_dim(t,c*h,h,0)
    other=swap_core(lax.dynamic_slice_in_dim(t,(1-c)*h,h,0).astype(bf)).astype(f32)
    return mine,other,c
def afters(vs,*first):
    return list(lax.optimization_barrier(tuple(vs)+tuple(first))[:len(vs)])
def sides(mine,other,c):
    return jnp.where(c==0,jnp.concatenate([mine,other],axis=1),jnp.concatenate([other,mine],axis=1))
def natural(keep,send):
    order=[int(v) for v in NATURAL]
    keep,send=[jnp.concatenate([v[k] for k in order],axis=0) for v in (keep,send)]
    return jnp.concatenate([keep,send],axis=1)
def slot0(k):
    xr,yr,zr=k&1,(k>>1)&1,(-(k>>2))&3
    return (1-xr)*8+yr*2+zr if zr<2 else 2+(1-yr)*8+xr*2+zr
NATURAL=[slot0(k) for k in range(BLK)]

def shards(hidden, lengths, counts, targets, out_grad, qkv_weight, qv_bias, out_weight, out_bias,
           norm1_gain, norm1_bias, up_weight, up_bias, down_weight, down_bias, norm2_gain,
           norm2_bias, rel_bias, score_weight):
    _, _, S, D = hidden.shape
    F = down_weight.shape[0] * lax.axis_size(ALL)
    n_dev = lax.axis_size(ALL)
    dev = lax.axis_index(ALL)
    d1, f1 = D // n_dev, F // n_dev
    tokens = hidden.reshape(S, D)
    length = lengths.reshape(1)
    fast = staged()
    count_f = counts.astype(f32)
    npb, ncol = lax.axis_size("pb"), lax.axis_size("col")
    pb, col = lax.axis_index("pb"), lax.axis_index("col")
    t1 = targets.astype(bf)
    t2 = (targets - t1.astype(f32)).astype(bf)
    t3 = (targets - t1.astype(f32) - t2.astype(f32)).astype(bf)
    columns = [qv_bias[0], qv_bias[1], out_bias, norm1_gain, norm1_bias, down_bias, norm2_gain, norm2_bias, score_weight]
    columns += [up_bias[j * d1 : (j + 1) * d1] for j in range(4)]
    lane = lax.broadcasted_iota(jnp.int32, (d1, 128), 1)
    panel = jnp.zeros((d1, 128), bf)
    for j, v in enumerate(columns):
        panel = jnp.where(lane == j, v[:, None], panel)
    place0 = lax.broadcasted_iota(jnp.int32, (d1, 128), 0) == 0
    for j, v in enumerate((count_f.reshape(1, 1).astype(bf), t1, t2, t3)):
        panel = jnp.where((lane == CT + j) & place0, v, panel)
    ups = up_weight.reshape(d1, n_dev, 4, d1).transpose(0, 2, 1, 3).reshape(d1, F)
    rest = jnp.concatenate([out_weight, ups] + [down_weight[j * d1 : (j + 1) * d1] for j in range(4)], axis=1)
    w_rest = lax.all_gather(rest, ALL, axis=0, tiled=True)
    if fast:
        c = col & 1
        pos = jnp.stack([col >> 1, pb & 1, pb >> 1, c, pb, col]).astype(jnp.int32)
        half = lambda h: jnp.concatenate([lax.dynamic_slice_in_dim(qkv_weight, h * (3 * D // 2), 3 * D // 2, 1), panel], axis=1)
        got, mine = swap_core(half(1 - c)), half(c)
        q1 = spread1(jnp.where(c == 0, cat([mine, got]), cat([got, mine])))
        p_qkv = spread4(spread3(spread2(q1)))
    else:
        pos = jnp.stack([0 * pb, 0 * pb, 0 * pb, 0 * pb, pb, col]).astype(jnp.int32)
        both = lax.all_gather(jnp.concatenate([qkv_weight, panel], axis=1), ALL, axis=0, tiled=True)
        panel = both[:, 3 * D :]
        p_qkv = spread_plain([both[:, : 3 * D], jnp.concatenate([panel, panel], axis=1)])
    strips, kx = tables(rel_bias, length[0], S)
    qkv, vec = qkv_fwd(pos, p_qkv, tokens)
    attn = [attn_fwd(qkv, kx, strips, 2 * i, 2) for i in range(3)]
    mixed = [v[0] for v in attn]
    layer_out, u1, u2, sc, nl, act, gp, first, own_score = post_fwd(length, w_rest, mixed, tokens, vec)
    scores = [own_score] + [swap_col(own_score, r) for r in range(1, ncol)]
    gr2, gi, vg1, kb, sb, info = back1(pos, length, scores, d1, w_rest, out_grad.reshape(S, D), u2, sc, act, gp, vec)
    if fast:
        rb0 = swap_core(sb)
    gr1, ga, gm, vg2 = back2(w_rest, gr2, u1, sc, gi, vec)
    if fast:
        cb1 = collect1(*afters([kb, rb0], gm))
        nl = afters([nl], cb1[0])[0]
    ka, sa = wup(pos, mixed, ga, nl, gi)
    gm_1 = afters([gm], ka)[0]
    if fast:
        ra0 = swap_core(sa)
    back = lambda i, g: attn_bwd(qkv, g, attn[i][2], attn[i][1], attn[i][3], 2 * i, 2)
    grads = [back(0, gm_1)]
    gm_2 = afters([gm], grads[0][0])[0]
    if fast:
        ca1 = collect1(*afters([ka, ra0], grads[0][0]))
        cb2 = collect2(*afters(cb1, ca1[0], ca1[1]))
        gm_2 = afters([gm], cb2[0], cb2[1])[0]
    grads.append(back(1, gm_2))
    gm_3 = afters([gm], grads[1][0])[0]
    if fast:
        ca2 = collect2(*afters(ca1, grads[1][0]))
        cb3 = collect3(*afters(cb2, ca2[0], ca2[1]))
        gm_3 = afters([gm], ca2[0], ca2[1], cb3[0])[0]
    grads.append(back(2, gm_3))
    parts = [g[j] for j in range(3) for g in grads]
    if fast:
        ca3 = collect3(*afters(ca2, grads[2][0]))
        parts = afters(parts, ca3[0])
    kq, sq, vb = wqkv(pos, tokens, parts)
    if fast:
        rq0 = swap_core(sq)
        mb, ob, _ = collect4(*afters(cb3, kq))
        cq1 = collect1(kq, rq0)
        parts = afters(parts, cq1[0], cq1[1])
    hidden_grad = hgrad(pos, p_qkv, parts, gr1)
    near = cat([g[3] for g in grads])
    far = cat([g[4] for g in grads])
    ids = strip_ids()
    onehot = (ids[:, :, None] == jnp.arange(rel_bias.shape[0], dtype=jnp.int32)).astype(f32)
    bucket = jnp.einsum("hac,acb->bh", near, onehot, precision=lax.Precision.HIGHEST)
    far = jnp.sum(far, axis=2)
    bucket = bucket.at[15].add(far[:, 0]).at[31].add(far[:, 1])
    weighted = info[1, :1]
    last = jnp.concatenate([bucket.reshape(-1), weighted, jnp.zeros((D - bucket.size - 1,), f32)])
    smalls = jnp.concatenate([(vg1 + vg2)[:CT], vb[:2], info[0, 0] * first[:1], last[None]], axis=0)
    h = D // 2
    if fast:
        smalls = smalls + swap_core(smalls)
        smalls = smalls + swap_x(smalls)
        cq2 = collect2(*afters(cq1, hidden_grad))
        smalls = smalls + swap_y(afters([smalls], hidden_grad)[0])
        ma, oa, _ = collect4(*afters(ca3, cq2[0], cq2[1]))
        d_down = sides(mb, ob, c)
        cq3 = collect3(*cq2)
        smalls = smalls + flip_z(afters([smalls], cq3[0])[0], 1)
        d_qkv = sides(*collect4(*cq3))
        smalls = smalls + flip_z(smalls, 2)
        d_out = sides(ma[:, :h], oa[:, :h], c)
        d_up = sides(ma[:, h:], oa[:, h:], c)
    else:
        scatter = lambda w: lax.psum_scatter(w, ALL, scatter_dimension=0, tiled=True).astype(f32)
        d_down, d_qkv = scatter(natural(kb, sb)), scatter(natural(kq, sq))
        d_out = scatter(natural(ka[:, :, :h], sa[:, :, :h]))
        d_up = scatter(natural(ka[:, :, h:], sa[:, :, h:]))
        smalls = lax.psum(smalls, ALL)
    d_down = cat([d_down[:, j * D : (j + 1) * D] for j in range(4)])
    d_up = d_up.reshape(d1, 4, n_dev, d1).transpose(0, 2, 1, 3).reshape(d1, F)
    part = lax.dynamic_slice_in_dim(smalls, dev * d1, d1, axis=1)
    loss = smalls[CT + 3, bucket.size] / info[2, 0]
    bucket = smalls[CT + 3, : bucket.size].reshape(bucket.shape)
    return (layer_out.reshape(hidden.shape), loss, hidden_grad.reshape(hidden.shape), d_qkv, part[CT : CT + 2],
            d_out, part[OB], part[G1], part[S1], d_up, part[UB : UB + 4].reshape(-1), d_down, part[DB], part[G2], part[S2],
            bucket, part[CT + 2])


def solution(mesh):
    lead = P(("pb", "col"))
    row = P(("pb", "col"), None)
    act = P("pb", "col", None, None)
    side = P(None, ("pb", "col"))
    return jax.shard_map(
        shards,
        mesh=mesh,
        in_specs=(act, P("pb", "col"), P("pb"), P("pb", "col"), act, row, side, row, lead, lead, lead, row, lead, row, lead, lead, lead, P(), lead),
        out_specs=(act, P(), act, row, side, row, lead, lead, lead, row, lead, row, lead, lead, lead, P(), lead),
        check_vma=False,
    )
```

```python
import functools

import jax
import jax.numpy as jnp
from jax import lax
from jax.experimental import pallas as pl
from jax.experimental.pallas import tpu as pltpu
from jax.sharding import PartitionSpec as P

f32=jnp.float32; bf=jnp.bfloat16
NT=(((1,),(1,)),((),())); NN=(((1,),(0,)),((),())); TN=(((0,),(0,)),((),()))
T=128
EDGES = (1, 2, 3, 4, 5, 6, 7, 8, 12, 16, 23, 32, 45, 64, 91)
def strip_ids():
    r=jnp.arange(3*T,dtype=jnp.int32)[None,:]-T-jnp.arange(T,dtype=jnp.int32)[:,None]
    m=jnp.abs(r); ids=jnp.where(r>0,16,0).astype(jnp.int32)
    for e in EDGES: ids=ids+(m>=e).astype(jnp.int32)
    return ids
def tables(rel_bias, length, S):
    ids=strip_ids()
    nb=rel_bias.shape[0]
    oh=(ids[None]==jnp.arange(nb,dtype=jnp.int32)[:,None,None]).astype(bf)
    strips=jnp.einsum("bac,bh->hac",oh,rel_bias,preferred_element_type=f32)
    j=jnp.arange(S,dtype=jnp.int32)[:,None]; lane=jnp.arange(128,dtype=jnp.int32)[None,:]
    jb=j//T; nblk=S//T
    low=(jb<=lane-2)&(lane<nblk); up=(jb>=lane+2)&(lane<nblk)
    mk=jnp.where((lane==nblk)&(j>=length),-1e30,0.0)
    rb=rel_bias.astype(f32)
    kx=jnp.where(low[None],rb[15][:,None,None],jnp.where(up[None],rb[31][:,None,None],mk[None])).astype(bf)
    return strips,kx
def fwd_kernel(BQ, S, q_ref,k_ref,v_ref,kx_ref,st_ref,mix_ref,linv_ref,mf_ref,p_ref):
    nblk=S//T
    lane=lax.broadcasted_iota(jnp.int32,(1,128),1)
    row=lax.broadcasted_iota(jnp.int32,(BQ,128),0)//T
    lane2=lax.broadcasted_iota(jnp.int32,(BQ,128),1)
    q=q_ref[...];k=k_ref[...];v=v_ref[...]
    masks=[lane<64,lane>=64]
    kaug=[jnp.concatenate([k,kx_ref[h]],axis=1) for h in (0,1)]
    vaug=[jnp.where(masks[h],v,jnp.ones_like(v)) for h in (0,1)]
    for i in range(S//BQ):
        outs=[]
        qi=q[i*BQ:(i+1)*BQ]
        qx=((lane2==nblk)|(lane2==row+i*(BQ//T))).astype(f32).astype(bf)
        for h in (0,1):
            qa=jnp.concatenate([jnp.where(masks[h],qi,jnp.zeros_like(qi)),qx],axis=1)
            s=dg(qa,kaug[h],NT)
            rows=[]
            for b in range(BQ//T):
                I=i*(BQ//T)+b
                lo=max(0,(I-1)*T);hi=min(S,(I+2)*T)
                sb=s[b*T:(b+1)*T]
                parts=[]
                if lo>0: parts.append(sb[:,:lo])
                parts.append(sb[:,lo:hi]+st_ref[h,:,lo-(I-1)*T:hi-(I-1)*T])
                if hi<S: parts.append(sb[:,hi:])
                rows.append(jnp.concatenate(parts,axis=1) if len(parts)>1 else parts[0])
            s=jnp.concatenate(rows,axis=0) if len(rows)>1 else rows[0]
            m=jnp.max(s,axis=1,keepdims=True)
            p=jnp.exp(s-m).astype(bf)
            p_ref[h,i*BQ:(i+1)*BQ,:]=p
            outs.append(dg(p,vaug[h],NN))
        o0,o1=outs
        num=jnp.where(masks[0],o0,o1)
        den=jnp.where(masks[0],o1,o0)
        den=pltpu.roll(den,64,1)
        linv=1.0/den
        mf=num*linv
        mf_ref[i*BQ:(i+1)*BQ,:]=mf
        mix_ref[i*BQ:(i+1)*BQ,:]=mf.astype(bf)
        linv_ref[i*BQ:(i+1)*BQ,:]=linv
def attn_fwd(qkv,kx,strips,p0,n,BQ=512):
    S,W=qkv.shape; npair=W//3//128
    blk=lambda o: pl.BlockSpec((S,128),lambda p:(0,o*npair+p0+p))
    out=pl.BlockSpec((S,128),lambda p:(0,p))
    return pl.pallas_call(functools.partial(fwd_kernel,BQ,S),cost_estimate=takes(n*5),grid=(n,),
        in_specs=[blk(0),blk(1),blk(2),pl.BlockSpec((2,S,128),lambda p:(p0+p,0,0)),pl.BlockSpec((2,T,3*T),lambda p:(p0+p,0,0))],
        out_specs=[out]*3+[pl.BlockSpec((2,S,S),lambda p:(p,0,0))],
        out_shape=[sd((S,n*128),bf),sd((S,n*128),f32),sd((S,n*128),f32),sd((2*n,S,S),bf)],
        compiler_params=pltpu.CompilerParams(vmem_limit_bytes=56*2**20),
        )(qkv,qkv,qkv,kx,strips)
def bwd_kernel(BQ,S,form,scale,kscale,q_ref,k_ref,v_ref,gm_ref,mf_ref,linv_ref,p_ref,dq_ref,dk_ref,dv_ref,diag_ref,cs_ref,ds_ref):
    nblk=S//T
    lane=lax.broadcasted_iota(jnp.int32,(1,128),1)
    lanes=lax.broadcasted_iota(jnp.int32,(S,128),1)
    rows=lax.broadcasted_iota(jnp.int32,(S,128),0)
    masks=[lane<64,lane>=64]
    q=q_ref[...];k=k_ref[...];v=v_ref[...]
    gm=gm_ref[...].astype(f32);linv=linv_ref[...]
    do=(gm*linv).astype(bf)
    t=do.astype(f32)*mf_ref[...]
    kind=(lanes==rows//T).astype(f32).astype(bf)
    kaug=jnp.concatenate([k,kind],axis=1)
    vx=jnp.where(lanes<2,1.0,0.0).astype(bf)
    vaug=jnp.concatenate([v,vx],axis=1)
    dqs=[];dks=[];dvs=[]
    if form=="T":
        qT=q.T; doT=do.T
    for h in (0,1):
        delta=jnp.sum(jnp.where(masks[h],t,0.0),axis=1,keepdims=True)
        hi=delta.astype(bf).astype(f32); lo=delta-hi
        ex=jnp.where(lanes==0,-hi,jnp.where(lanes==1,-lo,0.0)).astype(bf)
        da=jnp.concatenate([jnp.where(masks[h],do,jnp.zeros_like(do)),ex],axis=1)
        near=[jnp.zeros((T,T),f32) for _ in range(3)]
        dq=[]
        for i in range(S//BQ):
            x=dg(da[i*BQ:(i+1)*BQ],vaug,NT)
            ds=p_ref[h,i*BQ:(i+1)*BQ,:]*x.astype(bf)
            ds_ref[i*BQ:(i+1)*BQ,:]=ds
            dq.append(dg(ds,kaug,NN))
            for b in range(BQ//T):
                I=i*(BQ//T)+b
                for n in (-1,0,1):
                    if 0<=I+n<nblk:
                        near[n+1]=near[n+1]+ds[b*T:(b+1)*T,(I+n)*T:(I+n+1)*T].astype(f32)
        dq=jnp.concatenate(dq,axis=0)
        dqs.append(dq[:,:128])
        far=dq[:,128:]
        ib=rows//T
        total=lambda m: jnp.sum(jnp.sum(jnp.where(m,far,0.0),axis=0,keepdims=True),axis=1,keepdims=True)
        low=total(lanes<=ib-2);up=total((lanes>=ib+2)&(lanes<nblk))
        W=4*T
        y=jnp.concatenate(near+[jnp.zeros((T,T),f32)],axis=1)
        n=T
        while n>8:
            n//=2
            y=y[:n]+pltpu.roll(y[n:],W-n,1)
        sub=lax.broadcasted_iota(jnp.int32,(8,W),0)
        for b in range(3): y=jnp.where(((sub>>b)&1)==1,pltpu.roll(y,W-(1<<b),1),y)
        place=lax.broadcasted_iota(jnp.int32,(1,W),1)
        y=jnp.sum(y,axis=0,keepdims=True)+jnp.where(place==W-1,low,0.0)+jnp.where(place==2*T+1,up,0.0)
        diag_ref[h]=jnp.broadcast_to(y,(8,W))
        if form=="T":
            dks.append(dg(qT[h*64:(h+1)*64],ds_ref[...],NN))
            dvs.append(dg(doT[h*64:(h+1)*64],p_ref[h],NN))
        else:
            dks.append(dg(ds_ref[...],q,TN))
            dvs.append(dg(p_ref[h],do,TN))
    dq=(jnp.where(masks[0],dqs[0],dqs[1])*scale).astype(bf)
    dq_ref[...]=dq
    if form=="T":
        dk_ref[...]=(jnp.concatenate(dks,axis=0)*kscale).T.astype(bf)
        dv=jnp.concatenate(dvs,axis=0).T.astype(bf)
    else:
        dk_ref[...]=(jnp.where(masks[0],dks[0],dks[1])*kscale).astype(bf)
        dv=jnp.where(masks[0],dvs[0],dvs[1]).astype(bf)
    dv_ref[...]=dv
    part=lax.broadcasted_iota(jnp.int32,(8,128),0)
    cs_ref[...]=jnp.where(part==0,jnp.sum(dq.astype(f32),axis=0,keepdims=True),jnp.sum(dv.astype(f32),axis=0,keepdims=True))
def attn_bwd(qkv,gm,mixed,linv,p,p0,n,BQ=512,form="T",scale=0.125,kscale=1.0):
    S,W=qkv.shape; npair=W//3//128
    blk=lambda o: pl.BlockSpec((S,128),lambda i:(0,o*npair+p0+i))
    own=pl.BlockSpec((S,128),lambda i:(0,i))
    return pl.pallas_call(functools.partial(bwd_kernel,BQ,S,form,scale,kscale),cost_estimate=takes(n*6),grid=(n,),
        in_specs=[blk(0),blk(1),blk(2),blk(0),own,own,pl.BlockSpec((2,S,S),lambda i:(i,0,0))],
        out_specs=[own]*3+[pl.BlockSpec((2,8,4*T),lambda i:(i,0,0)),pl.BlockSpec((8,128),lambda i:(0,i))],
        out_shape=[sd((S,n*128),bf)]*3+[sd((2*n,8,4*T),f32),sd((8,n*128),f32)],
        scratch_shapes=[pltpu.VMEM((S,S),bf)],
        compiler_params=pltpu.CompilerParams(vmem_limit_bytes=56*2**20),
        )(qkv,qkv,qkv,gm,mixed,linv,p)
sd=jax.ShapeDtypeStruct
def takes(us): return pl.CostEstimate(flops=int(us*1.15e9),bytes_accessed=int(us*1e6),transcendentals=0)
def dg(a,b,d=NN): return lax.dot_general(a,b,d,preferred_element_type=f32)
QB,VB,OB,G1,S1,DB,G2,S2,SW,UB,CT,TG,NV=0,1,2,3,4,5,6,7,8,9,13,14,24
def gelu_both(x,mode="poly"):
    e=jnp.exp(x*x*-0.5)
    if mode=="erf":
        cdf=0.5*(1.0+lax.erf(x*0.7071067811865476))
    else:
        t=1.0/(1.0+(0.3275911*0.7071067811865476)*jnp.abs(x))
        q=t*(0.127414796+t*(-0.142248368+t*(0.7107068705+t*(-0.7265760135+t*0.5307027145))))*e
        cdf=jnp.where(x>=0,1.0-q,q)
    return x*cdf, cdf+x*e*0.3989422804014327
def norm(r):
    c=r-jnp.mean(r,axis=-1,keepdims=True)
    s=lax.rsqrt(jnp.mean(c*c,axis=-1,keepdims=True)+1e-05)
    return c*s,s
def norm_bwd(up,u,s,g):
    p=up*g
    return (p-jnp.mean(p,axis=-1,keepdims=True)-u*jnp.mean(p*u,axis=-1,keepdims=True))*s
def whole(a): return pl.BlockSpec(memory_space=pltpu.VMEM)

BLK=16
RELA=((0,0,0),(0,0,1),(0,1,0),(0,1,1))
RELB=((0,0,2),(0,0,3),(1,0,2),(1,0,3))
RELXA=((1,0,0),(1,0,1),(1,1,0),(1,1,1))
RELYB=((0,1,2),(0,1,3),(1,1,2),(1,1,3))
RELS=(RELA,RELB,RELXA,RELYB)
X_,Y_,Z_,C_=0,1,2,3
def place(pos,rel):
    xr,yr,zr=rel
    return (((pos[Z_]-zr)&3)*2+(pos[Y_]^yr))*2+(pos[X_]^xr)
def slot(pos,k):
    x,y,z=k&1,(k>>1)&1,k>>2
    xr,yr,zr=pos[X_]^x,pos[Y_]^y,(pos[Z_]-z)&3
    return jnp.where(zr<2,(1-xr)*8+yr*2+zr,2+(1-yr)*8+xr*2+zr)
def load(pos,pieces,parts,sem):
    for s in range(8):
        half=pos[C_] if s<4 else 1-pos[C_]
        for b,rel in enumerate(RELS[s%4]):
            k=place(pos,rel)
            R=pieces[s].shape[1]
            rows=pl.ds(pl.multiple_of(k*R,R),R)
            for off,w,dst in parts:
                cols=pl.ds(pl.multiple_of(half*w,w),w)
                pltpu.make_async_copy(pieces[s].at[b,:,pl.ds(off,w)],dst.at[rows,cols],sem).start()
def arrived(dst,sem):
    pltpu.make_async_copy(dst,dst,sem).wait()
ANYS=pl.BlockSpec(memory_space=pltpu.HBM)
SMEM=pl.BlockSpec(memory_space=pltpu.SMEM)
def qkv_kernel(pos,*refs):
    pieces=refs[:8]; hid_ref,o_ref,vec_ref,w_s,sm_s,sems=refs[8:]
    D=hid_ref.shape[1]; N=3*D
    @pl.when(pl.program_id(0)==0)
    def _():
        for s in range(4):
            for b,rel in enumerate(RELS[s]):
                R=pieces[s].shape[1]
                rows=pl.ds(pl.multiple_of(place(pos,rel)*R,R),R)
                pltpu.make_async_copy(pieces[s].at[b,:,pl.ds(N//2,128)],sm_s.at[rows,:],sems.at[1]).start()
        load(pos,pieces,[(0,N//2,w_s)],sems.at[0])
        arrived(sm_s,sems.at[1])
        vec_ref[...]=sm_s[...].astype(f32).T[:NV]
        arrived(w_s,sems.at[0])
    x=hid_ref[...]
    o_ref[:,:D]=((dg(x,w_s[:,:D])+vec_ref[QB:QB+1,:])*0.125).astype(bf)
    o_ref[:,D:2*D]=dg(x,w_s[:,D:2*D]).astype(bf)
    o_ref[:,2*D:]=(dg(x,w_s[:,2*D:])+vec_ref[VB:VB+1,:]).astype(bf)
def qkv_fwd(pos,pieces,hid,TR=256):
    R,D=hid.shape;N=3*D
    return pl.pallas_call(qkv_kernel,cost_estimate=takes(9),grid=(R//TR,),
        in_specs=[SMEM]+[ANYS]*8+[pl.BlockSpec((TR,D),lambda i:(i,0))],
        out_specs=[pl.BlockSpec((TR,N),lambda i:(i,0)),pl.BlockSpec((NV,D),lambda i:(0,0))],
        out_shape=[sd((R,N),bf),sd((NV,D),f32)],
        scratch_shapes=[pltpu.VMEM((D,N),bf),pltpu.VMEM((D,128),bf),pltpu.SemaphoreType.DMA((2,))],
        compiler_params=pltpu.CompilerParams(vmem_limit_bytes=56*2**20))(pos,*pieces,hid)
def fetch(w,off,dst,sem):
    pltpu.make_async_copy(w.at[:,pl.ds(off,dst.shape[1])],dst,sem).start()
def fetch_down(w,off,dst,sems):
    D=dst.shape[1]
    for j in range(dst.shape[0]//D):
        pltpu.make_async_copy(w.at[:,pl.ds(off+j*D,D)],dst.at[pl.ds(j*D,D),:],sems.at[j]).start()
def arrived_down(dst,sems):
    D=dst.shape[1]
    for j in range(dst.shape[0]//D):
        arrived(dst.at[pl.ds(j*D,D),:],sems.at[j])
def post_kernel(TR,mode,len_ref,*refs):
    w,*parts,hid_ref,vec_ref,lo_ref,u1_ref,u2_ref,sc_ref,nl_ref,act_ref,gp_ref,fr_ref,os_ref,ow_ref,uw_ref,dw_ref,sems=refs
    D=hid_ref.shape[1];F=uw_ref.shape[1]
    i=pl.program_id(0)
    @pl.when(i==0)
    def _():
        fetch(w,0,ow_ref,sems.at[4])
        fetch(w,D,uw_ref,sems.at[5])
        fetch_down(w,D+F,dw_ref,sems)
        arrived(ow_ref,sems.at[4])
    vec=lambda n: vec_ref[n:n+1,:]
    r=hid_ref[...].astype(f32)+(dg(jnp.concatenate([m[...] for m in parts],axis=1),ow_ref[...])+vec(OB))
    u1,s1=norm(r)
    u1_ref[...]=u1.astype(bf)
    n=u1*vec(G1)+vec(S1)
    nl=n.astype(bf)
    nl_ref[...]=nl
    @pl.when(i==0)
    def _():
        arrived(uw_ref,sems.at[5])
        arrived_down(dw_ref,sems)
    br=None
    for c in range(F//D):
        x=dg(nl,uw_ref[:,c*D:(c+1)*D])+vec(UB+c)
        a,gp=gelu_both(x,mode)
        a=a.astype(bf)
        act_ref[:,c*D:(c+1)*D]=a
        gp_ref[:,c*D:(c+1)*D]=gp.astype(bf)
        b=dg(a,dw_ref[c*D:(c+1)*D,:])
        br=b if br is None else br+b
    u2,s2=norm(n+(br+vec(DB)))
    u2_ref[...]=u2.astype(bf)
    fin=u2*vec(G2)+vec(S2)
    row=lax.broadcasted_iota(jnp.int32,(TR,D),0)+i*TR
    lo_ref[...]=jnp.where(row<len_ref[0],fin,0.0).astype(bf)
    lane=lax.broadcasted_iota(jnp.int32,(TR,128),1)
    sc_ref[...]=jnp.where(lane==0,s1,s2)
    @pl.when(i==0)
    def _():
        fr_ref[...]=fin[:8]
        own=jnp.sum(fin[:1]*vec(SW),axis=1,keepdims=True)
        os_ref[...]=jnp.broadcast_to(own,(8,128))
def post_fwd(length,w,mixed,hid,vec,TR=256,mode="erf"):
    R,D=hid.shape;F=4*D
    rb=lambda n: pl.BlockSpec((TR,n),lambda i:(i,0))
    cb=lambda a: pl.BlockSpec(a.shape,lambda i:(0,0))
    return pl.pallas_call(functools.partial(post_kernel,TR,mode),cost_estimate=takes(25),grid=(R//TR,),
        in_specs=[SMEM,ANYS]+[rb(m.shape[1]) for m in mixed]+[rb(D),cb(vec)],
        out_specs=[rb(D),rb(D),rb(D),rb(128),rb(D),rb(F),rb(F),pl.BlockSpec((8,D),lambda i:(0,0)),pl.BlockSpec((8,128),lambda i:(0,0))],
        out_shape=[sd((R,D),bf),sd((R,D),bf),sd((R,D),bf),sd((R,128),f32),sd((R,D),bf),sd((R,F),bf),sd((R,F),bf),sd((8,D),f32),sd((8,128),f32)],
        scratch_shapes=[pltpu.VMEM((D,D),bf),pltpu.VMEM((D,F),bf),pltpu.VMEM((F,D),bf),pltpu.SemaphoreType.DMA((6,))],
        compiler_params=pltpu.CompilerParams(vmem_limit_bytes=60*2**20))(length,w,*mixed,hid,vec)
def listwise(pos,ncol,d1,scores,vec_ref,info_ref):
    lane=lax.broadcasted_iota(jnp.int32,(1,vec_ref.shape[1]),1)
    pb,col=pos[4],pos[5]
    counts=vec_ref[CT:CT+1,:]
    targets=vec_ref[TG:TG+1,:]+vec_ref[TG+1:TG+2,:]+vec_ref[TG+2:TG+3,:]
    pick=lambda row,dev: jnp.sum(jnp.where(lane==dev*d1,row,0.0),axis=1,keepdims=True)
    total=jnp.sum(counts,axis=1,keepdims=True)*(1.0/ncol)
    mine=pick(counts,pb*ncol)
    n=len(scores)
    live=[(col^r).astype(f32)<mine for r in range(n)]
    share=[jnp.where(live[r],pick(targets,pb*ncol+(col^r)),0.0) for r in range(n)]
    def pairs(f,v):
        while len(v)>1: v=[f(v[i],v[i+1]) for i in range(0,len(v),2)]
        return v[0]
    add=lambda a,b: a+b
    whole=pairs(add,share)
    masked=[jnp.where(live[r],scores[r],-1e30) for r in range(n)]
    top=pairs(jnp.maximum,masked)
    log=top+jnp.log(pairs(add,[jnp.exp(m-top) for m in masked]))
    entropy=log-pairs(add,[share[r]/whole*scores[r] for r in range(n)])
    prob=jnp.where(live[0],jnp.exp(masked[0]-log),0.0)
    gs=mine/total*(prob-share[0]/whole)
    weighted=jnp.where(col==0,mine*entropy,0.0)
    row=lax.broadcasted_iota(jnp.int32,(8,128),0)
    info_ref[...]=jnp.where(row==0,gs,jnp.where(row==1,weighted,total))
def whole1(a): return pl.BlockSpec(a.shape,lambda i:(0,)*len(a.shape),pipeline_mode=pl.Buffered(1))
def mid_kernel(TR,ncol,d1,nm,pos,len_ref,*refs):
    s_refs=refs[:ncol]
    w,act,nl=refs[ncol:ncol+3]
    mixed=refs[ncol+3:ncol+3+nm]
    (og_ref,u2_ref,u1_ref,sc_ref,gp_ref,vec_ref,ga_ref,gm_ref,vg_ref,info_ref,keep,send,
     ow_s,uw_s,dw_s,act_s,nl_s,mix_s,gb_s,gi_s,ga_s,stage,sems,outs)=refs[ncol+3+nm:]
    D=og_ref.shape[1];F=gp_ref.shape[1];H=D//2
    i=pl.program_id(0);n=pl.num_programs(0)
    def whole_copies():
        at=0
        todo=[(act,act_s,6),(nl,nl_s,7)]
        for j,m in enumerate(mixed):
            todo.append((m,mix_s.at[:,at:at+m.shape[1]],8+j)); at+=m.shape[1]
        return [pltpu.make_async_copy(a,b,sems.at[k]) for a,b,k in todo]
    @pl.when(i==0)
    def _():
        fetch_down(w,D+F,dw_s,sems)
        fetch(w,D,uw_s,sems.at[4])
        fetch(w,0,ow_s,sems.at[5])
        for c in whole_copies(): c.start()
        listwise(pos,ncol,d1,[r[0:1,0:1] for r in s_refs],vec_ref,info_ref)
        vg_ref[...]=jnp.zeros_like(vg_ref)
        arrived_down(dw_s,sems)
    vec=lambda k: vec_ref[k:k+1,:]
    row=lax.broadcasted_iota(jnp.int32,(TR,D),0)+i*TR
    gf=og_ref[...].astype(f32)
    gf=gf+jnp.where(row==0,info_ref[0:1,0:1]*vec(SW),0.0)
    gf=jnp.where(row<len_ref[0],gf,0.0)
    def add(k,v): vg_ref[k:k+1,:]+=jnp.sum(v,axis=0,keepdims=True)
    u2=u2_ref[...].astype(f32); s1=sc_ref[:,0:1]; s2=sc_ref[:,1:2]
    add(G2,gf*u2); add(S2,gf)
    gr2=norm_bwd(gf,u2,s2,vec(G2))
    gb=gr2.astype(bf)
    here=pl.ds(pl.multiple_of(i*TR,TR),TR)
    gb_s[here,:]=gb
    add(DB,gb.astype(f32))
    @pl.when(i==0)
    def _():
        arrived(uw_s,sems.at[4])
        arrived(ow_s,sems.at[5])
    gn=gr2
    for c in range(F//D):
        g=dg(gb,dw_s[c*D:(c+1)*D,:],NT)
        gi=(g*gp_ref[:,c*D:(c+1)*D].astype(f32)).astype(bf)
        gi_s[here,c*D:(c+1)*D]=gi
        add(UB+c,gi.astype(f32))
        gn=gn+dg(gi,uw_s[:,c*D:(c+1)*D],NT)
    u1=u1_ref[...].astype(f32)
    add(G1,gn*u1); add(S1,gn)
    ga=norm_bwd(gn,u1,s1,vec(G1)).astype(bf)
    ga_ref[...]=ga
    ga_s[here,:]=ga
    add(OB,ga.astype(f32))
    gm_ref[...]=dg(ga,ow_s[...],NT).astype(bf)
    @pl.when(i==n-1)
    def _():
        for c in whole_copies(): c.wait()
        core=pos[C_]
        slots=[slot(pos,k) for k in range(BLK)]
        U=H+F//2
        jobs=[]
        for ref,h in ((send,1-core),(keep,core)):
            for c in range(F//D//2):
                jobs.append((ref,h,c,"down"))
            for c in range(F//D//2):
                jobs.append((ref,h,c,"up"))
        jobs.append((None,None,0,"out"))
        copies=[]
        for j,(ref,h,c,kind) in enumerate(jobs):
            b=j&1
            if j>=2:
                for v in copies[j-2]: v.wait()
            if kind!="out":
                cols=pl.ds(pl.multiple_of(h*(F//2)+c*D,D),D)
            if kind=="down":
                t=dg(act_s[:,cols],gb_s[...],TN)
            elif kind=="up":
                t=dg(nl_s[...],gi_s[:,cols],TN)
            else:
                t=dg(mix_s[...],ga_s[...],TN)
            t=t.astype(bf)
            for k in range(BLK):
                stage[b,slots[k]]=t[k*(D//BLK):(k+1)*(D//BLK)]
            if kind=="out":
                halves=[pl.ds(pl.multiple_of(v*H,H),H) for v in (core,1-core)]
                made=[pltpu.make_async_copy(stage.at[b,:,:,halves[m]],r.at[:,:,pl.ds(0,H)],outs.at[j+m]) for m,r in enumerate((keep,send))]
            else:
                off=(U if kind=="down" else H)+c*D
                made=[pltpu.make_async_copy(stage.at[b],ref.at[:,:,pl.ds(off,D)],outs.at[j])]
            for v in made: v.start()
            copies.append(made)
        for made in copies[-2:]:
            for v in made: v.wait()
def mid(pos,length,scores,d1,w,og,u2,u1,sc,act,gp,nl,mixed,vec,TR=256):
    R,D=og.shape;F=act.shape[1]
    rb=lambda n: pl.BlockSpec((TR,n),lambda i:(i,0))
    o=sd((BLK,D//BLK,(D+2*F)//2),bf)
    return pl.pallas_call(functools.partial(mid_kernel,TR,len(scores),d1,len(mixed)),cost_estimate=takes(32),grid=(R//TR,),
        in_specs=[SMEM]*2+[whole1(v) for v in scores]+[ANYS]*(3+len(mixed))+[rb(D),rb(D),rb(D),rb(128),rb(F),whole1(vec)],
        out_specs=[rb(D),rb(D),whole1(vec),whole1(scores[0]),ANYS,ANYS],
        out_shape=[sd((R,D),bf),sd((R,D),bf),vec,sd((8,128),f32),o,o],
        scratch_shapes=[pltpu.VMEM((D,D),bf),pltpu.VMEM((D,F),bf),pltpu.VMEM((F,D),bf),pltpu.VMEM((R,F),bf),pltpu.VMEM((R,D),bf),pltpu.VMEM((R,D),bf),
                        pltpu.VMEM((R,D),bf),pltpu.VMEM((R,F),bf),pltpu.VMEM((R,D),bf),pltpu.VMEM((2,BLK,D//BLK,D),bf),
                        pltpu.SemaphoreType.DMA((8+len(mixed),)),pltpu.SemaphoreType.DMA((10,))],
        compiler_params=pltpu.CompilerParams(vmem_limit_bytes=60*2**20))(pos,length,*scores,w,act,nl,*mixed,og,u2,u1,sc,gp,vec)
VM=pl.BlockSpec(memory_space=pltpu.VMEM)
def small_kernel(buckets,n,vg,info,first,*refs):
    diags,sums,sm_ref=refs[:n],refs[n:2*n],refs[2*n]
    D=first.shape[1]
    sm_ref[...]=jnp.zeros_like(sm_ref)
    sm_ref[:CT]=vg[:CT]
    at=0
    for r in sums:
        sm_ref[CT:CT+2,at:at+r.shape[1]]=r[0:2]
        at+=r.shape[1]
    sm_ref[CT+2:CT+3]=info[0:1,0:1]*first[0:1]
    place=lax.broadcasted_iota(jnp.int32,(4*T,128),0)
    off=jnp.where(place<3*T,place-T,place-5*T)
    which=jnp.where(off>0,buckets//2,0)
    for e in EDGES: which=which+(jnp.abs(off)>=e).astype(jnp.int32)
    onehot=(which==lax.broadcasted_iota(jnp.int32,(4*T,128),1)).astype(f32)
    diag=jnp.concatenate([d[h,0:1] for d in diags for h in range(d.shape[0])],axis=0)
    sums=lax.dot_general(diag,onehot,NN,precision=lax.Precision.HIGHEST,preferred_element_type=f32)
    sm_ref[CT+3:CT+3+diag.shape[0],:128]=sums
    sm_ref[31:32]=jnp.broadcast_to(info[1:2,0:1],(1,D))
def small_sums(buckets,vg,info,first,diags,sums):
    return pl.pallas_call(functools.partial(small_kernel,buckets,len(diags)),cost_estimate=takes(2),in_specs=[VM]*(3+2*len(diags)),out_specs=VM,
        out_shape=sd((32,first.shape[1]),f32))(vg,info,first,*diags,*sums)
def wqkv_kernel(pos,hid_ref,*refs):
    *parts,k_ref,s_ref,g_s=refs
    D=hid_ref.shape[1];N=3*D
    at=0
    for r in parts:
        g_s[:,at:at+r.shape[1]]=r[...]
        at+=r.shape[1]
    x=hid_ref[...]
    core=pos[C_]
    slots=[slot(pos,k) for k in range(BLK)]
    for ref,h in ((s_ref,1-core),(k_ref,core)):
        t=dg(x,g_s[:,pl.ds(pl.multiple_of(h*(N//2),N//2),N//2)],TN).astype(bf)
        for k in range(BLK):
            ref[slots[k]]=t[k*(D//BLK):(k+1)*(D//BLK)]
def wqkv(pos,hid,parts):
    R,D=hid.shape;N=3*D
    g=sd((BLK,D//BLK,N//2),bf)
    return pl.pallas_call(wqkv_kernel,cost_estimate=takes(9),
        in_specs=[SMEM,VM]+[VM]*len(parts),out_specs=[VM]*2,out_shape=[g,g],
        scratch_shapes=[pltpu.VMEM((R,N),bf)],
        compiler_params=pltpu.CompilerParams(vmem_limit_bytes=60*2**20))(pos,hid,*parts)
def hgrad_kernel(pos,*refs):
    pieces=refs[:8]
    *parts,gr1_ref,hg_ref,w_s,sems=refs[8:]
    D=gr1_ref.shape[1];N=3*D
    @pl.when(pl.program_id(0)==0)
    def _():
        load(pos,pieces,[(0,N//2,w_s)],sems.at[0])
        arrived(w_s,sems.at[0])
    g=jnp.concatenate([r[...] for r in parts],axis=1)
    hg_ref[...]=(gr1_ref[...].astype(f32)+dg(g,w_s[...],NT)).astype(bf)
def hgrad(pos,pieces,parts,gr1,TR=256):
    R,D=gr1.shape;N=3*D
    rb=lambda n: pl.BlockSpec((TR,n),lambda i:(i,0))
    return pl.pallas_call(hgrad_kernel,cost_estimate=takes(10),grid=(R//TR,),
        in_specs=[SMEM]+[ANYS]*8+[rb(p.shape[1]) for p in parts]+[rb(D)],
        out_specs=rb(D),out_shape=sd((R,D),bf),
        scratch_shapes=[pltpu.VMEM((D,N),bf),pltpu.SemaphoreType.DMA((1,))],
        compiler_params=pltpu.CompilerParams(vmem_limit_bytes=60*2**20))(pos,*pieces,*parts,gr1)

ALL=("pb","col")
def staged():
    return lax.axis_size("pb")==8 and lax.axis_size("col")==4
def swap_core(v): return lax.ppermute(v,"col",[(i,i^1) for i in range(4)])
def swap_col(v,k): return lax.ppermute(v,"col",[(i,i^k) for i in range(lax.axis_size("col"))])
def swap_x(v): return lax.ppermute(v,"col",[(i,i^2) for i in range(4)])
def swap_y(v): return lax.ppermute(v,"pb",[(i,i^1) for i in range(8)])
def flip_z(v,m): return lax.ppermute(v,"pb",[(i,i^(2*m)) for i in range(8)])
def shift_z(v,k): return lax.ppermute(v,"pb",[(i,(i+2*k)%8) for i in range(8)])
def cat(a): return jnp.concatenate(a,axis=0)
def after(v,*first):
    return lax.optimization_barrier((v,)+first)[0]
def spread1(block):
    o=block[None]
    return [o,shift_z(o,1),shift_z(o,2),shift_z(o,3)]
def spread2(v):
    a=cat(v[:2]);b=cat(v[2:])
    return [cat([a,swap_y(a)]),cat([b,swap_x(b)])]
def spread3(v):
    a,b=v
    return [a,b,swap_x(a),swap_y(b)]
def spread4(own):
    return own+[swap_core(v) for v in own]
def own_order():
    zero=(0,0,0,0)
    return [[place(zero,rel) for rel in rels] for rels in RELS]
def spread_plain(full):
    out=[]
    for half in (0,1):
        cols=jnp.concatenate([w.reshape(BLK,w.shape[0]//BLK,2,w.shape[1]//2)[:,:,half] for w in full],axis=2)
        for order in own_order():
            out.append(jnp.stack([cols[k] for k in order]))
    return out
def add2(a,b): return (a.astype(f32)+b.astype(f32)).astype(bf)
def collect1(keep,r):
    sa,sb,ka,kb=[add2(keep[4*s:4*s+4],r[4*s:4*s+4]) for s in range(4)]
    return ka,kb,swap_x(sa),swap_y(sb)
def collect2(ka,kb,ra,rb):
    ka2,sa2=add2(ka[:2],ra[:2]),add2(ka[2:],ra[2:])
    kb2,sb2=add2(kb[:2],rb[:2]),add2(kb[2:],rb[2:])
    return ka2,kb2,swap_y(sa2),swap_x(sb2)
def collect3(*panels):
    t=[[ka2[0].astype(f32)+ra[0].astype(f32),add2(ka2[1],ra[1]),add2(kb2[0],rb[0]),add2(kb2[1],rb[1])] for ka2,kb2,ra,rb in panels]
    return [jnp.concatenate(v,axis=1) if len(v)>1 else v[0] for v in zip(*t)]
def send3(t0,t1,t2,t3): return t0,shift_z(t1,3),shift_z(t2,2),shift_z(t3,1)
def collect4(t0,t1,t2,t3):
    t=t0+t1.astype(f32)+t2.astype(f32)+t3.astype(f32)
    c=lax.axis_index("col")&1
    h=t.shape[0]//2
    mine=lax.dynamic_slice_in_dim(t,c*h,h,0)
    other=swap_core(lax.dynamic_slice_in_dim(t,(1-c)*h,h,0).astype(bf)).astype(f32)
    return mine,other
def afters(vs,*first):
    return list(lax.optimization_barrier(tuple(vs)+tuple(first))[:len(vs)])
def sides(mine,other,c):
    return jnp.where(c==0,jnp.concatenate([mine,other],axis=1),jnp.concatenate([other,mine],axis=1))
def natural(keep,send):
    order=[int(v) for v in NATURAL]
    keep,send=[jnp.concatenate([v[k] for k in order],axis=0) for v in (keep,send)]
    return jnp.concatenate([keep,send],axis=1)
def slot0(k):
    xr,yr,zr=k&1,(k>>1)&1,(-(k>>2))&3
    return (1-xr)*8+yr*2+zr if zr<2 else 2+(1-yr)*8+xr*2+zr
NATURAL=[slot0(k) for k in range(BLK)]

def shards(hidden, lengths, counts, targets, out_grad, qkv_weight, qv_bias, out_weight, out_bias,
           norm1_gain, norm1_bias, up_weight, up_bias, down_weight, down_bias, norm2_gain,
           norm2_bias, rel_bias, score_weight):
    _, _, S, D = hidden.shape
    F = down_weight.shape[0] * lax.axis_size(ALL)
    n_dev = lax.axis_size(ALL)
    dev = lax.axis_index(ALL)
    d1, f1 = D // n_dev, F // n_dev
    tokens = hidden.reshape(S, D)
    length = lengths.reshape(1)
    fast = staged()
    count_f = counts.astype(f32)
    npb, ncol = lax.axis_size("pb"), lax.axis_size("col")
    pb, col = lax.axis_index("pb"), lax.axis_index("col")
    t1 = targets.astype(bf)
    t2 = (targets - t1.astype(f32)).astype(bf)
    t3 = (targets - t1.astype(f32) - t2.astype(f32)).astype(bf)
    columns = [qv_bias[0], qv_bias[1], out_bias, norm1_gain, norm1_bias, down_bias, norm2_gain, norm2_bias, score_weight]
    columns += [up_bias[j * d1 : (j + 1) * d1] for j in range(4)]
    lane = lax.broadcasted_iota(jnp.int32, (d1, 128), 1)
    panel = jnp.zeros((d1, 128), bf)
    for j, v in enumerate(columns):
        panel = jnp.where(lane == j, v[:, None], panel)
    place0 = lax.broadcasted_iota(jnp.int32, (d1, 128), 0) == 0
    for j, v in enumerate((count_f.reshape(1, 1).astype(bf), t1, t2, t3)):
        panel = jnp.where((lane == CT + j) & place0, v, panel)
    ups = up_weight.reshape(d1, n_dev, 4, d1).transpose(0, 2, 1, 3).reshape(d1, F)
    rest = jnp.concatenate([out_weight, ups] + [down_weight[j * d1 : (j + 1) * d1] for j in range(4)], axis=1)
    w_rest = lax.all_gather(rest, ALL, axis=0, tiled=True)
    if fast:
        c = col & 1
        pos = jnp.stack([col >> 1, pb & 1, pb >> 1, c, pb, col]).astype(jnp.int32)
        half = lambda h: jnp.concatenate([lax.dynamic_slice_in_dim(qkv_weight, h * (3 * D // 2), 3 * D // 2, 1), panel], axis=1)
        got, mine = swap_core(half(1 - c)), half(c)
        q1 = spread1(jnp.where(c == 0, cat([mine, got]), cat([got, mine])))
        p_qkv = spread4(spread3(spread2(q1)))
    else:
        pos = jnp.stack([0 * pb, 0 * pb, 0 * pb, 0 * pb, pb, col]).astype(jnp.int32)
        both = lax.all_gather(jnp.concatenate([qkv_weight, panel], axis=1), ALL, axis=0, tiled=True)
        panel = both[:, 3 * D :]
        p_qkv = spread_plain([both[:, : 3 * D], jnp.concatenate([panel, panel], axis=1)])
    strips, kx = tables(rel_bias, length[0], S)
    qkv, vec = qkv_fwd(pos, p_qkv, tokens)
    calls = ((0, 2), (2, rel_bias.shape[1] // 2 - 2))
    attn = [attn_fwd(qkv, kx, strips, *call) for call in calls]
    mixed = [v[0] for v in attn]
    layer_out, u1, u2, sc, nl, act, gp, first, own_score = post_fwd(length, w_rest, mixed, tokens, vec)
    scores = [own_score] + [swap_col(own_score, r) for r in range(1, ncol)]
    ga, gm, vg, info, keep, send = mid(pos, length, scores, d1, w_rest, out_grad.reshape(S, D), u2, u1, sc, act, gp, nl, mixed, vec)
    if fast:
        r0 = swap_core(send)
    back = lambda i, g: attn_bwd(qkv, g, attn[i][2], attn[i][1], attn[i][3], *calls[i])
    grads = [back(0, gm)]
    if fast:
        c1 = collect1(*afters([keep, r0], grads[0][0]))
        gm_2 = afters([gm], c1[0], c1[1])[0]
    else:
        gm_2 = gm
    grads.append(back(1, gm_2))
    parts = [g[j] for j in range(3) for g in grads]
    smalls = small_sums(rel_bias.shape[0], vg, info, first, [g[3] for g in grads], [g[4] for g in grads])
    h = D // 2
    if fast:
        smalls = smalls + swap_core(smalls)
        travel = swap_x(smalls)
        c2 = collect2(*afters(c1, smalls))
        smalls = smalls + afters([travel], c2[0], c2[1])[0]
        travel = swap_y(smalls)
        parts = afters(parts, smalls, c2[0], c2[1])
    kq, sq = wqkv(pos, tokens, parts)
    if fast:
        smalls = smalls + afters([travel], kq)[0]
        rq0 = swap_core(afters([sq], smalls)[0])
        c3 = collect3(afters(c2, kq, smalls))
        cq1 = collect1(kq, afters([rq0], *c3)[0])
        c3 = send3(*c3)
        parts = afters(parts, cq1[0], cq1[1])
        hidden_grad = hgrad(pos, p_qkv, parts, ga)
        cq2 = collect2(*afters(cq1, hidden_grad))
        m, o = collect4(*afters(c3, cq2[0], cq2[1]))
        travel = flip_z(afters([smalls], m)[0], 1)
        cq3 = collect3(afters(cq2, m))
        n = (D + F) // 2
        d_out = sides(m[:, :h], o[:, :h], c)
        d_up = sides(m[:, h:n], o[:, h:n], c)
        d_down = sides(m[:, n:], o[:, n:], c)
        smalls = smalls + afters([travel], *cq3)[0]
        travel = flip_z(smalls, 2)
        m, o = collect4(*send3(*cq3))
        smalls = smalls + afters([travel], m)[0]
        d_qkv = sides(m, o, c)
    else:
        hidden_grad = hgrad(pos, p_qkv, parts, ga)
        scatter = lambda w: lax.psum_scatter(w, ALL, scatter_dimension=0, tiled=True).astype(f32)
        n = (D + F) // 2
        d_qkv = scatter(natural(kq, sq))
        d_out = scatter(natural(keep[:, :, :h], send[:, :, :h]))
        d_up = scatter(natural(keep[:, :, h:n], send[:, :, h:n]))
        d_down = scatter(natural(keep[:, :, n:], send[:, :, n:]))
        smalls = lax.psum(smalls, ALL)
    d_down = cat([d_down[:, j * D : (j + 1) * D] for j in range(4)])
    d_up = d_up.reshape(d1, 4, n_dev, d1).transpose(0, 2, 1, 3).reshape(d1, F)
    part = lax.dynamic_slice_in_dim(smalls, dev * d1, d1, axis=1)
    loss = smalls[31, 0] / info[2, 0]
    bucket = smalls[CT + 3 : CT + 3 + rel_bias.shape[1], : rel_bias.shape[0]].T
    return (layer_out.reshape(hidden.shape), loss, hidden_grad.reshape(hidden.shape), d_qkv, part[CT : CT + 2],
            d_out, part[OB], part[G1], part[S1], d_up, part[UB : UB + 4].reshape(-1), d_down, part[DB], part[G2], part[S2],
            bucket, part[CT + 2])


def solution(mesh):
    lead = P(("pb", "col"))
    row = P(("pb", "col"), None)
    act = P("pb", "col", None, None)
    side = P(None, ("pb", "col"))
    return jax.shard_map(
        shards,
        mesh=mesh,
        in_specs=(act, P("pb", "col"), P("pb"), P("pb", "col"), act, row, side, row, lead, lead, lead, row, lead, row, lead, lead, lead, P(), lead),
        out_specs=(act, P(), act, row, side, row, lead, lead, lead, row, lead, row, lead, lead, lead, P(), lead),
        check_vma=False,
    )
```

```python
import functools

import jax
import jax.numpy as jnp
from jax import lax
from jax.experimental import pallas as pl
from jax.experimental.pallas import tpu as pltpu
from jax.sharding import PartitionSpec as P

f32=jnp.float32; bf=jnp.bfloat16
NT=(((1,),(1,)),((),())); NN=(((1,),(0,)),((),())); TN=(((0,),(0,)),((),()))
T=128
EDGES = (1, 2, 3, 4, 5, 6, 7, 8, 12, 16, 23, 32, 45, 64, 91)
def strip_ids():
    r=jnp.arange(3*T,dtype=jnp.int32)[None,:]-T-jnp.arange(T,dtype=jnp.int32)[:,None]
    m=jnp.abs(r); ids=jnp.where(r>0,16,0).astype(jnp.int32)
    for e in EDGES: ids=ids+(m>=e).astype(jnp.int32)
    return ids
def tables(rel_bias, length, S):
    ids=strip_ids()
    nb=rel_bias.shape[0]
    oh=(ids[None]==jnp.arange(nb,dtype=jnp.int32)[:,None,None]).astype(bf)
    strips=jnp.einsum("bac,bh->hac",oh,rel_bias,preferred_element_type=f32)
    j=jnp.arange(S,dtype=jnp.int32)[:,None]; lane=jnp.arange(128,dtype=jnp.int32)[None,:]
    jb=j//T; nblk=S//T
    low=(jb<=lane-2)&(lane<nblk); up=(jb>=lane+2)&(lane<nblk)
    mk=jnp.where((lane==nblk)&(j>=length),-1e30,0.0)
    rb=rel_bias.astype(f32)
    kx=jnp.where(low[None],rb[15][:,None,None],jnp.where(up[None],rb[31][:,None,None],mk[None])).astype(bf)
    return strips,kx
def fwd_kernel(BQ, S, q_ref,k_ref,v_ref,kx_ref,st_ref,mix_ref,linv_ref,mf_ref,p_ref):
    nblk=S//T
    lane=lax.broadcasted_iota(jnp.int32,(1,128),1)
    row=lax.broadcasted_iota(jnp.int32,(BQ,128),0)//T
    lane2=lax.broadcasted_iota(jnp.int32,(BQ,128),1)
    q=q_ref[...];k=k_ref[...];v=v_ref[...]
    masks=[lane<64,lane>=64]
    kaug=[jnp.concatenate([k,kx_ref[h]],axis=1) for h in (0,1)]
    vaug=[jnp.where(masks[h],v,jnp.ones_like(v)) for h in (0,1)]
    for i in range(S//BQ):
        outs=[]
        qi=q[i*BQ:(i+1)*BQ]
        qx=((lane2==nblk)|(lane2==row+i*(BQ//T))).astype(f32).astype(bf)
        for h in (0,1):
            qa=jnp.concatenate([jnp.where(masks[h],qi,jnp.zeros_like(qi)),qx],axis=1)
            s=dg(qa,kaug[h],NT)
            rows=[]
            for b in range(BQ//T):
                I=i*(BQ//T)+b
                lo=max(0,(I-1)*T);hi=min(S,(I+2)*T)
                sb=s[b*T:(b+1)*T]
                parts=[]
                if lo>0: parts.append(sb[:,:lo])
                parts.append(sb[:,lo:hi]+st_ref[h,:,lo-(I-1)*T:hi-(I-1)*T])
                if hi<S: parts.append(sb[:,hi:])
                rows.append(jnp.concatenate(parts,axis=1) if len(parts)>1 else parts[0])
            s=jnp.concatenate(rows,axis=0) if len(rows)>1 else rows[0]
            m=jnp.max(s,axis=1,keepdims=True)
            p=jnp.exp(s-m).astype(bf)
            p_ref[h,i*BQ:(i+1)*BQ,:]=p
            outs.append(dg(p,vaug[h],NN))
        o0,o1=outs
        num=jnp.where(masks[0],o0,o1)
        den=jnp.where(masks[0],o1,o0)
        den=pltpu.roll(den,64,1)
        linv=1.0/den
        mf=num*linv
        mf_ref[i*BQ:(i+1)*BQ,:]=mf
        mix_ref[i*BQ:(i+1)*BQ,:]=mf.astype(bf)
        linv_ref[i*BQ:(i+1)*BQ,:]=linv
def attn_fwd(qkv,kx,strips,p0,n,BQ=512):
    S,W=qkv.shape; npair=W//3//128
    blk=lambda o: pl.BlockSpec((S,128),lambda p:(0,o*npair+p0+p))
    out=pl.BlockSpec((S,128),lambda p:(0,p))
    return pl.pallas_call(functools.partial(fwd_kernel,BQ,S),cost_estimate=takes(n*5),grid=(n,),
        in_specs=[blk(0),blk(1),blk(2),pl.BlockSpec((2,S,128),lambda p:(p0+p,0,0)),pl.BlockSpec((2,T,3*T),lambda p:(p0+p,0,0))],
        out_specs=[out]*3+[pl.BlockSpec((2,S,S),lambda p:(p,0,0))],
        out_shape=[sd((S,n*128),bf),sd((S,n*128),f32),sd((S,n*128),f32),sd((2*n,S,S),bf)],
        compiler_params=pltpu.CompilerParams(vmem_limit_bytes=56*2**20),
        )(qkv,qkv,qkv,kx,strips)
def bwd_kernel(BQ,S,form,scale,kscale,q_ref,k_ref,v_ref,gm_ref,mf_ref,linv_ref,p_ref,dq_ref,dk_ref,dv_ref,diag_ref,cs_ref,ds_ref):
    nblk=S//T
    lane=lax.broadcasted_iota(jnp.int32,(1,128),1)
    lanes=lax.broadcasted_iota(jnp.int32,(S,128),1)
    rows=lax.broadcasted_iota(jnp.int32,(S,128),0)
    masks=[lane<64,lane>=64]
    q=q_ref[...];k=k_ref[...];v=v_ref[...]
    gm=gm_ref[...].astype(f32);linv=linv_ref[...]
    do=(gm*linv).astype(bf)
    t=do.astype(f32)*mf_ref[...]
    kind=(lanes==rows//T).astype(f32).astype(bf)
    kaug=jnp.concatenate([k,kind],axis=1)
    vx=jnp.where(lanes<2,1.0,0.0).astype(bf)
    vaug=jnp.concatenate([v,vx],axis=1)
    dqs=[];dks=[];dvs=[]
    if form=="T":
        qT=q.T; doT=do.T
    for h in (0,1):
        delta=jnp.sum(jnp.where(masks[h],t,0.0),axis=1,keepdims=True)
        hi=delta.astype(bf).astype(f32); lo=delta-hi
        ex=jnp.where(lanes==0,-hi,jnp.where(lanes==1,-lo,0.0)).astype(bf)
        da=jnp.concatenate([jnp.where(masks[h],do,jnp.zeros_like(do)),ex],axis=1)
        near=[jnp.zeros((T,T),f32) for _ in range(3)]
        dq=[]
        for i in range(S//BQ):
            x=dg(da[i*BQ:(i+1)*BQ],vaug,NT)
            ds=p_ref[h,i*BQ:(i+1)*BQ,:]*x.astype(bf)
            ds_ref[i*BQ:(i+1)*BQ,:]=ds
            dq.append(dg(ds,kaug,NN))
            for b in range(BQ//T):
                I=i*(BQ//T)+b
                for n in (-1,0,1):
                    if 0<=I+n<nblk:
                        near[n+1]=near[n+1]+ds[b*T:(b+1)*T,(I+n)*T:(I+n+1)*T].astype(f32)
        dq=jnp.concatenate(dq,axis=0)
        dqs.append(dq[:,:128])
        far=dq[:,128:]
        ib=rows//T
        total=lambda m: jnp.sum(jnp.sum(jnp.where(m,far,0.0),axis=0,keepdims=True),axis=1,keepdims=True)
        low=total(lanes<=ib-2);up=total((lanes>=ib+2)&(lanes<nblk))
        W=4*T
        y=jnp.concatenate(near+[jnp.zeros((T,T),f32)],axis=1)
        n=T
        while n>8:
            n//=2
            y=y[:n]+pltpu.roll(y[n:],W-n,1)
        sub=lax.broadcasted_iota(jnp.int32,(8,W),0)
        for b in range(3): y=jnp.where(((sub>>b)&1)==1,pltpu.roll(y,W-(1<<b),1),y)
        place=lax.broadcasted_iota(jnp.int32,(1,W),1)
        y=jnp.sum(y,axis=0,keepdims=True)+jnp.where(place==W-1,low,0.0)+jnp.where(place==2*T+1,up,0.0)
        diag_ref[h]=jnp.broadcast_to(y,(8,W))
        if form=="T":
            dks.append(dg(qT[h*64:(h+1)*64],ds_ref[...],NN))
            dvs.append(dg(doT[h*64:(h+1)*64],p_ref[h],NN))
        else:
            dks.append(dg(ds_ref[...],q,TN))
            dvs.append(dg(p_ref[h],do,TN))
    dq=(jnp.where(masks[0],dqs[0],dqs[1])*scale).astype(bf)
    dq_ref[...]=dq
    if form=="T":
        dk_ref[...]=(jnp.concatenate(dks,axis=0)*kscale).T.astype(bf)
        dv=jnp.concatenate(dvs,axis=0).T.astype(bf)
    else:
        dk_ref[...]=(jnp.where(masks[0],dks[0],dks[1])*kscale).astype(bf)
        dv=jnp.where(masks[0],dvs[0],dvs[1]).astype(bf)
    dv_ref[...]=dv
    part=lax.broadcasted_iota(jnp.int32,(8,128),0)
    cs_ref[...]=jnp.where(part==0,jnp.sum(dq.astype(f32),axis=0,keepdims=True),jnp.sum(dv.astype(f32),axis=0,keepdims=True))
def attn_bwd(qkv,gm,mixed,linv,p,p0,n,BQ=512,form="T",scale=0.125,kscale=1.0):
    S,W=qkv.shape; npair=W//3//128
    blk=lambda o: pl.BlockSpec((S,128),lambda i:(0,o*npair+p0+i))
    own=pl.BlockSpec((S,128),lambda i:(0,i))
    return pl.pallas_call(functools.partial(bwd_kernel,BQ,S,form,scale,kscale),cost_estimate=takes(n*6),grid=(n,),
        in_specs=[blk(0),blk(1),blk(2),blk(0),own,own,pl.BlockSpec((2,S,S),lambda i:(i,0,0))],
        out_specs=[own]*3+[pl.BlockSpec((2,8,4*T),lambda i:(i,0,0)),pl.BlockSpec((8,128),lambda i:(0,i))],
        out_shape=[sd((S,n*128),bf)]*3+[sd((2*n,8,4*T),f32),sd((8,n*128),f32)],
        scratch_shapes=[pltpu.VMEM((S,S),bf)],
        compiler_params=pltpu.CompilerParams(vmem_limit_bytes=56*2**20),
        )(qkv,qkv,qkv,gm,mixed,linv,p)
sd=jax.ShapeDtypeStruct
def takes(us): return pl.CostEstimate(flops=int(us*1.15e9),bytes_accessed=int(us*1e6),transcendentals=0)
def dg(a,b,d=NN): return lax.dot_general(a,b,d,preferred_element_type=f32)
QB,VB,OB,G1,S1,DB,G2,S2,SW,UB,CT,TG,NV=0,1,2,3,4,5,6,7,8,9,13,14,24
def gelu_both(x,mode="poly"):
    e=jnp.exp(x*x*-0.5)
    if mode=="erf":
        cdf=0.5*(1.0+lax.erf(x*0.7071067811865476))
    else:
        t=1.0/(1.0+(0.3275911*0.7071067811865476)*jnp.abs(x))
        q=t*(0.127414796+t*(-0.142248368+t*(0.7107068705+t*(-0.7265760135+t*0.5307027145))))*e
        cdf=jnp.where(x>=0,1.0-q,q)
    return x*cdf, cdf+x*e*0.3989422804014327
def norm(r):
    c=r-jnp.mean(r,axis=-1,keepdims=True)
    s=lax.rsqrt(jnp.mean(c*c,axis=-1,keepdims=True)+1e-05)
    return c*s,s
def norm_bwd(up,u,s,g):
    p=up*g
    return (p-jnp.mean(p,axis=-1,keepdims=True)-u*jnp.mean(p*u,axis=-1,keepdims=True))*s
def whole(a): return pl.BlockSpec(memory_space=pltpu.VMEM)

BLK=16
SUB=2
RELA=((0,0,0),(0,0,1),(0,1,0),(0,1,1))
RELB=((0,0,2),(0,0,3),(1,0,2),(1,0,3))
RELXA=((1,0,0),(1,0,1),(1,1,0),(1,1,1))
RELYB=((0,1,2),(0,1,3),(1,1,2),(1,1,3))
RELS=(RELA,RELB,RELXA,RELYB)
X_,Y_,Z_,C_=0,1,2,3
def place(pos,rel):
    xr,yr,zr=rel
    return (((pos[Z_]-zr)&3)*2+(pos[Y_]^yr))*2+(pos[X_]^xr)
def slot(pos,k):
    x,y,z=k&1,(k>>1)&1,k>>2
    xr,yr,zr=pos[X_]^x,pos[Y_]^y,(pos[Z_]-z)&3
    return jnp.where(zr<2,(1-xr)*8+yr*2+zr,2+(1-yr)*8+xr*2+zr)
def load(pos,pieces,parts,sem):
    for s in range(8):
        half=pos[C_] if s<4 else 1-pos[C_]
        for b,rel in enumerate(RELS[s%4]):
            k=place(pos,rel)
            R=pieces[s].shape[1]
            rows=pl.ds(pl.multiple_of(k*R,R),R)
            for off,w,dst in parts:
                cols=pl.ds(pl.multiple_of(half*w,w),w)
                pltpu.make_async_copy(pieces[s].at[b,:,pl.ds(off,w)],dst.at[rows,cols],sem).start()
def arrived(dst,sem):
    pltpu.make_async_copy(dst,dst,sem).wait()
ANYS=pl.BlockSpec(memory_space=pltpu.HBM)
SMEM=pl.BlockSpec(memory_space=pltpu.SMEM)
def qkv_kernel(pos,*refs):
    pieces=refs[:8]; hid_ref,o_ref,vec_ref,w_s,sm_s,sems=refs[8:]
    D=hid_ref.shape[1]; N=3*D
    @pl.when(pl.program_id(0)==0)
    def _():
        for s in range(4):
            for b,rel in enumerate(RELS[s]):
                R=pieces[s].shape[1]
                rows=pl.ds(pl.multiple_of(place(pos,rel)*R,R),R)
                pltpu.make_async_copy(pieces[s].at[b,:,pl.ds(N//2,128)],sm_s.at[rows,:],sems.at[1]).start()
        load(pos,pieces,[(0,N//2,w_s)],sems.at[0])
        arrived(sm_s,sems.at[1])
        vec_ref[...]=sm_s[...].astype(f32).T[:NV]
        arrived(w_s,sems.at[0])
    x=hid_ref[...]
    o_ref[:,:D]=((dg(x,w_s[:,:D])+vec_ref[QB:QB+1,:])*0.125).astype(bf)
    o_ref[:,D:2*D]=dg(x,w_s[:,D:2*D]).astype(bf)
    o_ref[:,2*D:]=(dg(x,w_s[:,2*D:])+vec_ref[VB:VB+1,:]).astype(bf)
def qkv_fwd(pos,pieces,hid,TR=256):
    R,D=hid.shape;N=3*D
    return pl.pallas_call(qkv_kernel,cost_estimate=takes(9),grid=(R//TR,),
        in_specs=[SMEM]+[ANYS]*8+[pl.BlockSpec((TR,D),lambda i:(i,0))],
        out_specs=[pl.BlockSpec((TR,N),lambda i:(i,0)),pl.BlockSpec((NV,D),lambda i:(0,0))],
        out_shape=[sd((R,N),bf),sd((NV,D),f32)],
        scratch_shapes=[pltpu.VMEM((D,N),bf),pltpu.VMEM((D,128),bf),pltpu.SemaphoreType.DMA((2,))],
        compiler_params=pltpu.CompilerParams(vmem_limit_bytes=56*2**20))(pos,*pieces,hid)
def fetch(w,off,dst,sem):
    pltpu.make_async_copy(w.at[:,pl.ds(off,dst.shape[1])],dst,sem).start()
def fetch_down(w,off,dst,sems):
    D=dst.shape[1]
    for j in range(dst.shape[0]//D):
        pltpu.make_async_copy(w.at[:,pl.ds(off+j*D,D)],dst.at[pl.ds(j*D,D),:],sems.at[j]).start()
def arrived_down(dst,sems):
    D=dst.shape[1]
    for j in range(dst.shape[0]//D):
        arrived(dst.at[pl.ds(j*D,D),:],sems.at[j])
def post_kernel(TR,mode,len_ref,*refs):
    w,*parts,hid_ref,vec_ref,lo_ref,u1_ref,u2_ref,sc_ref,nl_ref,act_ref,gp_ref,fr_ref,os_ref,ow_ref,uw_ref,dw_ref,sems=refs
    D=hid_ref.shape[1];F=uw_ref.shape[1]
    i=pl.program_id(0)
    @pl.when(i==0)
    def _():
        fetch(w,0,ow_ref,sems.at[4])
        fetch(w,D,uw_ref,sems.at[5])
        fetch_down(w,D+F,dw_ref,sems)
        arrived(ow_ref,sems.at[4])
        arrived(uw_ref,sems.at[5])
        arrived_down(dw_ref,sems)
    vec=lambda n: vec_ref[n:n+1,:]
    HR=TR//SUB
    halves=[slice(q*HR,(q+1)*HR) for q in range(SUB)]
    def one(h):
        r=hid_ref[h,:].astype(f32)+(dg(jnp.concatenate([m[h,:] for m in parts],axis=1),ow_ref[...])+vec(OB))
        return norm(r)
    def two(h,u1):
        u1_ref[h,:]=u1.astype(bf)
        n=u1*vec(G1)+vec(S1)
        nl=n.astype(bf)
        nl_ref[h,:]=nl
        return n,nl
    def three(h,nl):
        br=None
        for c in range(F//D):
            x=dg(nl,uw_ref[:,c*D:(c+1)*D])+vec(UB+c)
            a,gp=gelu_both(x,mode)
            a=a.astype(bf)
            act_ref[h,c*D:(c+1)*D]=a
            gp_ref[h,c*D:(c+1)*D]=gp.astype(bf)
            b=dg(a,dw_ref[c*D:(c+1)*D,:])
            br=b if br is None else br+b
        return br
    def four(q,h,n,br,s1):
        u2,s2=norm(n+(br+vec(DB)))
        u2_ref[h,:]=u2.astype(bf)
        fin=u2*vec(G2)+vec(S2)
        row=lax.broadcasted_iota(jnp.int32,(HR,D),0)+i*TR+q*HR
        lo_ref[h,:]=jnp.where(row<len_ref[0],fin,0.0).astype(bf)
        lane=lax.broadcasted_iota(jnp.int32,(HR,128),1)
        sc_ref[h,:]=jnp.where(lane==0,s1,s2)
        return fin
    us=[one(h) for h in halves]
    ns=[two(h,u[0]) for h,u in zip(halves,us)]
    brs=[three(h,n[1]) for h,n in zip(halves,ns)]
    fin=[four(q,h,ns[q][0],brs[q],us[q][1]) for q,h in enumerate(halves)][0]
    @pl.when(i==0)
    def _():
        fr_ref[...]=fin[:8]
        own=jnp.sum(fin[:1]*vec(SW),axis=1,keepdims=True)
        os_ref[...]=jnp.broadcast_to(own,(8,128))
def post_fwd(length,w,mixed,hid,vec,TR=512,mode="erf"):
    R,D=hid.shape;F=4*D
    rb=lambda n: pl.BlockSpec((TR,n),lambda i:(i,0))
    cb=lambda a: pl.BlockSpec(a.shape,lambda i:(0,0))
    return pl.pallas_call(functools.partial(post_kernel,TR,mode),cost_estimate=takes(25),grid=(R//TR,),
        in_specs=[SMEM,ANYS]+[rb(m.shape[1]) for m in mixed]+[rb(D),cb(vec)],
        out_specs=[rb(D),rb(D),rb(D),rb(128),rb(D),rb(F),rb(F),pl.BlockSpec((8,D),lambda i:(0,0)),pl.BlockSpec((8,128),lambda i:(0,0))],
        out_shape=[sd((R,D),bf),sd((R,D),bf),sd((R,D),bf),sd((R,128),f32),sd((R,D),bf),sd((R,F),bf),sd((R,F),bf),sd((8,D),f32),sd((8,128),f32)],
        scratch_shapes=[pltpu.VMEM((D,D),bf),pltpu.VMEM((D,F),bf),pltpu.VMEM((F,D),bf),pltpu.SemaphoreType.DMA((6,))],
        compiler_params=pltpu.CompilerParams(vmem_limit_bytes=60*2**20))(length,w,*mixed,hid,vec)
def listwise(pos,ncol,d1,scores,vec_ref,info_ref):
    lane=lax.broadcasted_iota(jnp.int32,(1,vec_ref.shape[1]),1)
    pb,col=pos[4],pos[5]
    counts=vec_ref[CT:CT+1,:]
    targets=vec_ref[TG:TG+1,:]+vec_ref[TG+1:TG+2,:]+vec_ref[TG+2:TG+3,:]
    pick=lambda row,dev: jnp.sum(jnp.where(lane==dev*d1,row,0.0),axis=1,keepdims=True)
    total=jnp.sum(counts,axis=1,keepdims=True)*(1.0/ncol)
    mine=pick(counts,pb*ncol)
    n=len(scores)
    live=[(col^r).astype(f32)<mine for r in range(n)]
    share=[jnp.where(live[r],pick(targets,pb*ncol+(col^r)),0.0) for r in range(n)]
    def pairs(f,v):
        while len(v)>1: v=[f(v[i],v[i+1]) for i in range(0,len(v),2)]
        return v[0]
    add=lambda a,b: a+b
    whole=pairs(add,share)
    masked=[jnp.where(live[r],scores[r],-1e30) for r in range(n)]
    top=pairs(jnp.maximum,masked)
    log=top+jnp.log(pairs(add,[jnp.exp(m-top) for m in masked]))
    entropy=log-pairs(add,[share[r]/whole*scores[r] for r in range(n)])
    prob=jnp.where(live[0],jnp.exp(masked[0]-log),0.0)
    gs=mine/total*(prob-share[0]/whole)
    weighted=jnp.where(col==0,mine*entropy,0.0)
    row=lax.broadcasted_iota(jnp.int32,(8,128),0)
    info_ref[...]=jnp.where(row==0,gs,jnp.where(row==1,weighted,total))
def whole1(a): return pl.BlockSpec(a.shape,lambda i:(0,)*len(a.shape),pipeline_mode=pl.Buffered(1))
def mid_kernel(TR,ncol,d1,nm,pos,len_ref,*refs):
    s_refs=refs[:ncol]
    w,act,nl=refs[ncol:ncol+3]
    mixed=refs[ncol+3:ncol+3+nm]
    (og_ref,u2_ref,u1_ref,sc_ref,gp_ref,vec_ref,ga_ref,gm_ref,vg_ref,info_ref,keep,send,
     ow_s,uw_s,dw_s,act_s,nl_s,mix_s,gb_s,gi_s,ga_s,stage,sems,outs)=refs[ncol+3+nm:]
    D=og_ref.shape[1];F=gp_ref.shape[1];H=D//2
    i=pl.program_id(0);n=pl.num_programs(0)
    def whole_copies():
        at=0
        todo=[(act,act_s,6),(nl,nl_s,7)]
        for j,m in enumerate(mixed):
            todo.append((m,mix_s.at[:,at:at+m.shape[1]],8+j)); at+=m.shape[1]
        return [pltpu.make_async_copy(a,b,sems.at[k]) for a,b,k in todo]
    @pl.when(i==0)
    def _():
        fetch_down(w,D+F,dw_s,sems)
        fetch(w,D,uw_s,sems.at[4])
        fetch(w,0,ow_s,sems.at[5])
        for c in whole_copies(): c.start()
        listwise(pos,ncol,d1,[r[0:1,0:1] for r in s_refs],vec_ref,info_ref)
        vg_ref[...]=jnp.zeros_like(vg_ref)
        arrived_down(dw_s,sems)
        arrived(uw_s,sems.at[4])
        arrived(ow_s,sems.at[5])
    vec=lambda k: vec_ref[k:k+1,:]
    def add(k,v): vg_ref[k:k+1,:]+=jnp.sum(v,axis=0,keepdims=True)
    HR=TR
    halves=[slice(0,TR)]
    def one(q,h):
        row=lax.broadcasted_iota(jnp.int32,(HR,D),0)+i*TR+q*HR
        gf=og_ref[h,:].astype(f32)
        gf=gf+jnp.where(row==0,info_ref[0:1,0:1]*vec(SW),0.0)
        gf=jnp.where(row<len_ref[0],gf,0.0)
        u2=u2_ref[h,:].astype(f32)
        add(G2,gf*u2); add(S2,gf)
        gr2=norm_bwd(gf,u2,sc_ref[h,1:2],vec(G2))
        gb=gr2.astype(bf)
        here=pl.ds(pl.multiple_of(i*TR+q*HR,HR),HR)
        gb_s[here,:]=gb
        add(DB,gb.astype(f32))
        return here,gr2,gb
    def two(h,here,gr2,gb):
        gn=gr2
        for c in range(F//D):
            g=dg(gb,dw_s[c*D:(c+1)*D,:],NT)
            gi=(g*gp_ref[h,c*D:(c+1)*D].astype(f32)).astype(bf)
            gi_s[here,c*D:(c+1)*D]=gi
            add(UB+c,gi.astype(f32))
            gn=gn+dg(gi,uw_s[:,c*D:(c+1)*D],NT)
        return gn
    def three(h,here,gn):
        u1=u1_ref[h,:].astype(f32)
        add(G1,gn*u1); add(S1,gn)
        ga=norm_bwd(gn,u1,sc_ref[h,0:1],vec(G1)).astype(bf)
        ga_ref[h,:]=ga
        ga_s[here,:]=ga
        add(OB,ga.astype(f32))
        return ga
    a=[one(q,h) for q,h in enumerate(halves)]
    gns=[two(h,*v) for h,v in zip(halves,a)]
    gas=[three(h,v[0],gn) for h,v,gn in zip(halves,a,gns)]
    for h,ga in zip(halves,gas): gm_ref[h,:]=dg(ga,ow_s[...],NT).astype(bf)
    @pl.when(i==n-1)
    def _():
        for c in whole_copies(): c.wait()
        core=pos[C_]
        slots=[slot(pos,k) for k in range(BLK)]
        U=H+F//2
        jobs=[]
        for ref,h in ((send,1-core),(keep,core)):
            for c in range(F//D//2):
                jobs.append((ref,h,c,"down"))
            for c in range(F//D//2):
                jobs.append((ref,h,c,"up"))
        jobs.append((None,None,0,"out"))
        copies=[]
        for j,(ref,h,c,kind) in enumerate(jobs):
            b=j&1
            if j>=2:
                for v in copies[j-2]: v.wait()
            if kind!="out":
                cols=pl.ds(pl.multiple_of(h*(F//2)+c*D,D),D)
            if kind=="down":
                t=dg(act_s[:,cols],gb_s[...],TN)
            elif kind=="up":
                t=dg(nl_s[...],gi_s[:,cols],TN)
            else:
                t=dg(mix_s[...],ga_s[...],TN)
            t=t.astype(bf)
            for k in range(BLK):
                stage[b,slots[k]]=t[k*(D//BLK):(k+1)*(D//BLK)]
            if kind=="out":
                halves=[pl.ds(pl.multiple_of(v*H,H),H) for v in (core,1-core)]
                made=[pltpu.make_async_copy(stage.at[b,:,:,halves[m]],r.at[:,:,pl.ds(0,H)],outs.at[j+m]) for m,r in enumerate((keep,send))]
            else:
                off=(U if kind=="down" else H)+c*D
                made=[pltpu.make_async_copy(stage.at[b],ref.at[:,:,pl.ds(off,D)],outs.at[j])]
            for v in made: v.start()
            copies.append(made)
        for made in copies[-2:]:
            for v in made: v.wait()
def mid(pos,length,scores,d1,w,og,u2,u1,sc,act,gp,nl,mixed,vec,TR=256):
    R,D=og.shape;F=act.shape[1]
    rb=lambda n: pl.BlockSpec((TR,n),lambda i:(i,0))
    o=sd((BLK,D//BLK,(D+2*F)//2),bf)
    return pl.pallas_call(functools.partial(mid_kernel,TR,len(scores),d1,len(mixed)),cost_estimate=takes(32),grid=(R//TR,),
        in_specs=[SMEM]*2+[whole1(v) for v in scores]+[ANYS]*(3+len(mixed))+[rb(D),rb(D),rb(D),rb(128),rb(F),whole1(vec)],
        out_specs=[rb(D),rb(D),whole1(vec),whole1(scores[0]),ANYS,ANYS],
        out_shape=[sd((R,D),bf),sd((R,D),bf),vec,sd((8,128),f32),o,o],
        scratch_shapes=[pltpu.VMEM((D,D),bf),pltpu.VMEM((D,F),bf),pltpu.VMEM((F,D),bf),pltpu.VMEM((R,F),bf),pltpu.VMEM((R,D),bf),pltpu.VMEM((R,D),bf),
                        pltpu.VMEM((R,D),bf),pltpu.VMEM((R,F),bf),pltpu.VMEM((R,D),bf),pltpu.VMEM((2,BLK,D//BLK,D),bf),
                        pltpu.SemaphoreType.DMA((8+len(mixed),)),pltpu.SemaphoreType.DMA((10,))],
        compiler_params=pltpu.CompilerParams(vmem_limit_bytes=60*2**20))(pos,length,*scores,w,act,nl,*mixed,og,u2,u1,sc,gp,vec)
VM=pl.BlockSpec(memory_space=pltpu.VMEM)
def small_kernel(buckets,n,vg,info,first,*refs):
    diags,sums,sm_ref=refs[:n],refs[n:2*n],refs[2*n]
    D=first.shape[1]
    sm_ref[...]=jnp.zeros_like(sm_ref)
    sm_ref[:CT]=vg[:CT]
    at=0
    for r in sums:
        sm_ref[CT:CT+2,at:at+r.shape[1]]=r[0:2]
        at+=r.shape[1]
    sm_ref[CT+2:CT+3]=info[0:1,0:1]*first[0:1]
    place=lax.broadcasted_iota(jnp.int32,(4*T,128),0)
    off=jnp.where(place<3*T,place-T,place-5*T)
    which=jnp.where(off>0,buckets//2,0)
    for e in EDGES: which=which+(jnp.abs(off)>=e).astype(jnp.int32)
    onehot=(which==lax.broadcasted_iota(jnp.int32,(4*T,128),1)).astype(f32)
    diag=jnp.concatenate([d[h,0:1] for d in diags for h in range(d.shape[0])],axis=0)
    sums=lax.dot_general(diag,onehot,NN,precision=lax.Precision.HIGHEST,preferred_element_type=f32)
    sm_ref[CT+3:CT+3+diag.shape[0],:128]=sums
    sm_ref[31:32]=jnp.broadcast_to(info[1:2,0:1],(1,D))
def small_sums(buckets,vg,info,first,diags,sums):
    return pl.pallas_call(functools.partial(small_kernel,buckets,len(diags)),cost_estimate=takes(2),in_specs=[VM]*(3+2*len(diags)),out_specs=VM,
        out_shape=sd((32,first.shape[1]),f32))(vg,info,first,*diags,*sums)
def wqkv_kernel(pos,hid_ref,*refs):
    *parts,k_ref,s_ref,g_s=refs
    D=hid_ref.shape[1];N=3*D
    at=0
    for r in parts:
        g_s[:,at:at+r.shape[1]]=r[...]
        at+=r.shape[1]
    x=hid_ref[...]
    core=pos[C_]
    slots=[slot(pos,k) for k in range(BLK)]
    for ref,h in ((s_ref,1-core),(k_ref,core)):
        t=dg(x,g_s[:,pl.ds(pl.multiple_of(h*(N//2),N//2),N//2)],TN).astype(bf)
        for k in range(BLK):
            ref[slots[k]]=t[k*(D//BLK):(k+1)*(D//BLK)]
def wqkv(pos,hid,parts):
    R,D=hid.shape;N=3*D
    g=sd((BLK,D//BLK,N//2),bf)
    return pl.pallas_call(wqkv_kernel,cost_estimate=takes(9),
        in_specs=[SMEM,VM]+[VM]*len(parts),out_specs=[VM]*2,out_shape=[g,g],
        scratch_shapes=[pltpu.VMEM((R,N),bf)],
        compiler_params=pltpu.CompilerParams(vmem_limit_bytes=60*2**20))(pos,hid,*parts)
def hgrad_kernel(pos,*refs):
    pieces=refs[:8]
    *parts,gr1_ref,hg_ref,w_s,sems=refs[8:]
    D=gr1_ref.shape[1];N=3*D
    @pl.when(pl.program_id(0)==0)
    def _():
        load(pos,pieces,[(0,N//2,w_s)],sems.at[0])
        arrived(w_s,sems.at[0])
    g=jnp.concatenate([r[...] for r in parts],axis=1)
    hg_ref[...]=(gr1_ref[...].astype(f32)+dg(g,w_s[...],NT)).astype(bf)
def hgrad(pos,pieces,parts,gr1,TR=256):
    R,D=gr1.shape;N=3*D
    rb=lambda n: pl.BlockSpec((TR,n),lambda i:(i,0))
    return pl.pallas_call(hgrad_kernel,cost_estimate=takes(10),grid=(R//TR,),
        in_specs=[SMEM]+[ANYS]*8+[rb(p.shape[1]) for p in parts]+[rb(D)],
        out_specs=rb(D),out_shape=sd((R,D),bf),
        scratch_shapes=[pltpu.VMEM((D,N),bf),pltpu.SemaphoreType.DMA((1,))],
        compiler_params=pltpu.CompilerParams(vmem_limit_bytes=60*2**20))(pos,*pieces,*parts,gr1)

ALL=("pb","col")
def staged():
    return lax.axis_size("pb")==8 and lax.axis_size("col")==4
def swap_core(v): return lax.ppermute(v,"col",[(i,i^1) for i in range(4)])
def swap_col(v,k): return lax.ppermute(v,"col",[(i,i^k) for i in range(lax.axis_size("col"))])
def swap_x(v): return lax.ppermute(v,"col",[(i,i^2) for i in range(4)])
def swap_y(v): return lax.ppermute(v,"pb",[(i,i^1) for i in range(8)])
def flip_z(v,m): return lax.ppermute(v,"pb",[(i,i^(2*m)) for i in range(8)])
def shift_z(v,k): return lax.ppermute(v,"pb",[(i,(i+2*k)%8) for i in range(8)])
def cat(a): return jnp.concatenate(a,axis=0)
def after(v,*first):
    return lax.optimization_barrier((v,)+first)[0]
def spread1(block):
    o=block[None]
    return [o,shift_z(o,1),shift_z(o,2),shift_z(o,3)]
def spread2(v):
    a=cat(v[:2]);b=cat(v[2:])
    return [cat([a,swap_y(a)]),cat([b,swap_x(b)])]
def spread3(v):
    a,b=v
    return [a,b,swap_x(a),swap_y(b)]
def spread4(own):
    return own+[swap_core(v) for v in own]
def own_order():
    zero=(0,0,0,0)
    return [[place(zero,rel) for rel in rels] for rels in RELS]
def spread_plain(full):
    out=[]
    for half in (0,1):
        cols=jnp.concatenate([w.reshape(BLK,w.shape[0]//BLK,2,w.shape[1]//2)[:,:,half] for w in full],axis=2)
        for order in own_order():
            out.append(jnp.stack([cols[k] for k in order]))
    return out
def add2(a,b): return (a.astype(f32)+b.astype(f32)).astype(bf)
def collect1(keep,r):
    sa,sb,ka,kb=[add2(keep[4*s:4*s+4],r[4*s:4*s+4]) for s in range(4)]
    return ka,kb,swap_x(sa),swap_y(sb)
def collect2(ka,kb,ra,rb):
    ka2,sa2=add2(ka[:2],ra[:2]),add2(ka[2:],ra[2:])
    kb2,sb2=add2(kb[:2],rb[:2]),add2(kb[2:],rb[2:])
    return ka2,kb2,swap_y(sa2),swap_x(sb2)
def collect3(*panels):
    t=[[ka2[0].astype(f32)+ra[0].astype(f32),add2(ka2[1],ra[1]),add2(kb2[0],rb[0]),add2(kb2[1],rb[1])] for ka2,kb2,ra,rb in panels]
    return [jnp.concatenate(v,axis=1) if len(v)>1 else v[0] for v in zip(*t)]
def send3(t0,t1,t2,t3): return t0,shift_z(t1,3),shift_z(t2,2),shift_z(t3,1)
def collect4(t0,t1,t2,t3):
    t=t0+t1.astype(f32)+t2.astype(f32)+t3.astype(f32)
    c=lax.axis_index("col")&1
    h=t.shape[0]//2
    mine=lax.dynamic_slice_in_dim(t,c*h,h,0)
    other=swap_core(lax.dynamic_slice_in_dim(t,(1-c)*h,h,0).astype(bf)).astype(f32)
    return mine,other
def afters(vs,*first):
    return list(lax.optimization_barrier(tuple(vs)+tuple(first))[:len(vs)])
def sides(mine,other,c):
    return jnp.where(c==0,jnp.concatenate([mine,other],axis=1),jnp.concatenate([other,mine],axis=1))
def natural(keep,send):
    order=[int(v) for v in NATURAL]
    keep,send=[jnp.concatenate([v[k] for k in order],axis=0) for v in (keep,send)]
    return jnp.concatenate([keep,send],axis=1)
def slot0(k):
    xr,yr,zr=k&1,(k>>1)&1,(-(k>>2))&3
    return (1-xr)*8+yr*2+zr if zr<2 else 2+(1-yr)*8+xr*2+zr
NATURAL=[slot0(k) for k in range(BLK)]

def shards(hidden, lengths, counts, targets, out_grad, qkv_weight, qv_bias, out_weight, out_bias,
           norm1_gain, norm1_bias, up_weight, up_bias, down_weight, down_bias, norm2_gain,
           norm2_bias, rel_bias, score_weight):
    _, _, S, D = hidden.shape
    F = down_weight.shape[0] * lax.axis_size(ALL)
    n_dev = lax.axis_size(ALL)
    dev = lax.axis_index(ALL)
    d1, f1 = D // n_dev, F // n_dev
    tokens = hidden.reshape(S, D)
    length = lengths.reshape(1)
    fast = staged()
    count_f = counts.astype(f32)
    npb, ncol = lax.axis_size("pb"), lax.axis_size("col")
    pb, col = lax.axis_index("pb"), lax.axis_index("col")
    t1 = targets.astype(bf)
    t2 = (targets - t1.astype(f32)).astype(bf)
    t3 = (targets - t1.astype(f32) - t2.astype(f32)).astype(bf)
    columns = [qv_bias[0], qv_bias[1], out_bias, norm1_gain, norm1_bias, down_bias, norm2_gain, norm2_bias, score_weight]
    columns += [up_bias[j * d1 : (j + 1) * d1] for j in range(4)]
    lane = lax.broadcasted_iota(jnp.int32, (d1, 128), 1)
    panel = jnp.zeros((d1, 128), bf)
    for j, v in enumerate(columns):
        panel = jnp.where(lane == j, v[:, None], panel)
    place0 = lax.broadcasted_iota(jnp.int32, (d1, 128), 0) == 0
    for j, v in enumerate((count_f.reshape(1, 1).astype(bf), t1, t2, t3)):
        panel = jnp.where((lane == CT + j) & place0, v, panel)
    ups = up_weight.reshape(d1, n_dev, 4, d1).transpose(0, 2, 1, 3).reshape(d1, F)
    rest = jnp.concatenate([out_weight, ups] + [down_weight[j * d1 : (j + 1) * d1] for j in range(4)], axis=1)
    w_rest = lax.all_gather(rest, ALL, axis=0, tiled=True)
    if fast:
        c = col & 1
        pos = jnp.stack([col >> 1, pb & 1, pb >> 1, c, pb, col]).astype(jnp.int32)
        half = lambda h: jnp.concatenate([lax.dynamic_slice_in_dim(qkv_weight, h * (3 * D // 2), 3 * D // 2, 1), panel], axis=1)
        got, mine = swap_core(half(1 - c)), half(c)
        q1 = spread1(jnp.where(c == 0, cat([mine, got]), cat([got, mine])))
        p_qkv = spread4(spread3(spread2(q1)))
    else:
        pos = jnp.stack([0 * pb, 0 * pb, 0 * pb, 0 * pb, pb, col]).astype(jnp.int32)
        both = lax.all_gather(jnp.concatenate([qkv_weight, panel], axis=1), ALL, axis=0, tiled=True)
        panel = both[:, 3 * D :]
        p_qkv = spread_plain([both[:, : 3 * D], jnp.concatenate([panel, panel], axis=1)])
    strips, kx = tables(rel_bias, length[0], S)
    qkv, vec = qkv_fwd(pos, p_qkv, tokens)
    calls = ((0, 2), (2, rel_bias.shape[1] // 2 - 2))
    attn = [attn_fwd(qkv, kx, strips, *call) for call in calls]
    mixed = [v[0] for v in attn]
    layer_out, u1, u2, sc, nl, act, gp, first, own_score = post_fwd(length, w_rest, mixed, tokens, vec)
    scores = [own_score] + [swap_col(own_score, r) for r in range(1, ncol)]
    ga, gm, vg, info, keep, send = mid(pos, length, scores, d1, w_rest, out_grad.reshape(S, D), u2, u1, sc, act, gp, nl, mixed, vec)
    def home(down, up):
        down = cat([down[:, j * D : (j + 1) * D] for j in range(4)])
        return down, up.reshape(d1, 4, n_dev, d1).transpose(0, 2, 1, 3).reshape(d1, F)
    def own_part(v):
        part = lax.dynamic_slice_in_dim(v, dev * d1, d1, axis=1)
        return part, v[31, 0] / info[2, 0], v[CT + 3 : CT + 3 + rel_bias.shape[1], : rel_bias.shape[0]].T
    if fast:
        r0 = swap_core(send)
    back = lambda i, g: attn_bwd(qkv, g, attn[i][2], attn[i][1], attn[i][3], *calls[i])
    grads = [back(0, gm)]
    if fast:
        c1 = collect1(*afters([keep, r0], grads[0][0]))
        gm_2 = afters([gm], c1[0], c1[1])[0]
    else:
        gm_2 = gm
    grads.append(back(1, gm_2))
    parts = [g[j] for j in range(3) for g in grads]
    smalls = small_sums(rel_bias.shape[0], vg, info, first, [g[3] for g in grads], [g[4] for g in grads])
    h = D // 2
    if fast:
        smalls = smalls + swap_core(smalls)
        travel = swap_x(smalls)
        c2 = collect2(*afters(c1, smalls))
        smalls = smalls + afters([travel], c2[0], c2[1])[0]
        travel = swap_y(smalls)
        parts = afters(parts, smalls, c2[0], c2[1])
    kq, sq = wqkv(pos, tokens, parts)
    if fast:
        smalls = smalls + afters([travel], kq)[0]
        rq0 = swap_core(afters([sq], smalls)[0])
        smalls = smalls + flip_z(smalls, 1)
        travel = flip_z(smalls, 2)
        c3 = collect3(afters(c2, kq, smalls))
        smalls = smalls + afters([travel], *c3)[0]
        c3 = afters(c3, smalls)
        cq1 = collect1(kq, afters([rq0], *c3)[0])
        c3 = send3(*c3)
        parts = afters(parts, cq1[0], cq1[1], smalls)
        hidden_grad = hgrad(pos, p_qkv, parts, ga)
        cq2 = collect2(*afters(cq1, hidden_grad))
        cq3 = collect3(cq2)
        m, o = collect4(*afters(c3, *cq3))
        cq3 = send3(*cq3)
        n = (D + F) // 2
        d_out = sides(m[:, :h], o[:, :h], c)
        d_up = sides(m[:, h:n], o[:, h:n], c)
        d_down = sides(m[:, n:], o[:, n:], c)
        d_down, d_up = home(d_down, d_up)
        little = own_part(smalls)
        m, o = collect4(*afters(cq3, d_out, d_up, d_down, *little))
        d_qkv = sides(m, o, c)
    else:
        hidden_grad = hgrad(pos, p_qkv, parts, ga)
        scatter = lambda w: lax.psum_scatter(w, ALL, scatter_dimension=0, tiled=True).astype(f32)
        n = (D + F) // 2
        d_qkv = scatter(natural(kq, sq))
        d_out = scatter(natural(keep[:, :, :h], send[:, :, :h]))
        d_up = scatter(natural(keep[:, :, h:n], send[:, :, h:n]))
        d_down = scatter(natural(keep[:, :, n:], send[:, :, n:]))
        d_down, d_up = home(d_down, d_up)
        little = own_part(lax.psum(smalls, ALL))
    part, loss, bucket = little
    return (layer_out.reshape(hidden.shape), loss, hidden_grad.reshape(hidden.shape), d_qkv, part[CT : CT + 2],
            d_out, part[OB], part[G1], part[S1], d_up, part[UB : UB + 4].reshape(-1), d_down, part[DB], part[G2], part[S2],
            bucket, part[CT + 2])


def solution(mesh):
    lead = P(("pb", "col"))
    row = P(("pb", "col"), None)
    act = P("pb", "col", None, None)
    side = P(None, ("pb", "col"))
    return jax.shard_map(
        shards,
        mesh=mesh,
        in_specs=(act, P("pb", "col"), P("pb"), P("pb", "col"), act, row, side, row, lead, lead, lead, row, lead, row, lead, lead, lead, P(), lead),
        out_specs=(act, P(), act, row, side, row, lead, lead, lead, row, lead, row, lead, lead, lead, P(), lead),
        check_vma=False,
    )
```

```python
import functools

import jax
import jax.numpy as jnp
from jax import lax
from jax.experimental import pallas as pl
from jax.experimental.pallas import tpu as pltpu
from jax.sharding import PartitionSpec as P

f32=jnp.float32; bf=jnp.bfloat16
NT=(((1,),(1,)),((),())); NN=(((1,),(0,)),((),())); TN=(((0,),(0,)),((),()))
T=128
EDGES = (1, 2, 3, 4, 5, 6, 7, 8, 12, 16, 23, 32, 45, 64, 91)
def strip_ids():
    r=jnp.arange(3*T,dtype=jnp.int32)[None,:]-T-jnp.arange(T,dtype=jnp.int32)[:,None]
    m=jnp.abs(r); ids=jnp.where(r>0,16,0).astype(jnp.int32)
    for e in EDGES: ids=ids+(m>=e).astype(jnp.int32)
    return ids
def tables(rel_bias, length, S):
    ids=strip_ids()
    nb=rel_bias.shape[0]
    oh=(ids[None]==jnp.arange(nb,dtype=jnp.int32)[:,None,None]).astype(bf)
    strips=jnp.einsum("bac,bh->hac",oh,rel_bias,preferred_element_type=f32)
    j=jnp.arange(S,dtype=jnp.int32)[:,None]; lane=jnp.arange(128,dtype=jnp.int32)[None,:]
    jb=j//T; nblk=S//T
    low=(jb<=lane-2)&(lane<nblk); up=(jb>=lane+2)&(lane<nblk)
    mk=jnp.where((lane==nblk)&(j>=length),-1e30,0.0)
    rb=rel_bias.astype(f32)
    kx=jnp.where(low[None],rb[15][:,None,None],jnp.where(up[None],rb[31][:,None,None],mk[None])).astype(bf)
    return strips,kx
def fwd_kernel(BQ, S, q_ref,k_ref,v_ref,kx_ref,st_ref,mix_ref,linv_ref,mf_ref,p_ref):
    nblk=S//T
    lane=lax.broadcasted_iota(jnp.int32,(1,128),1)
    row=lax.broadcasted_iota(jnp.int32,(BQ,128),0)//T
    lane2=lax.broadcasted_iota(jnp.int32,(BQ,128),1)
    q=q_ref[...];k=k_ref[...];v=v_ref[...]
    masks=[lane<64,lane>=64]
    kaug=[jnp.concatenate([k,kx_ref[h]],axis=1) for h in (0,1)]
    vaug=[jnp.where(masks[h],v,jnp.ones_like(v)) for h in (0,1)]
    for i in range(S//BQ):
        outs=[]
        qi=q[i*BQ:(i+1)*BQ]
        qx=((lane2==nblk)|(lane2==row+i*(BQ//T))).astype(f32).astype(bf)
        for h in (0,1):
            qa=jnp.concatenate([jnp.where(masks[h],qi,jnp.zeros_like(qi)),qx],axis=1)
            s=dg(qa,kaug[h],NT)
            rows=[]
            for b in range(BQ//T):
                I=i*(BQ//T)+b
                lo=max(0,(I-1)*T);hi=min(S,(I+2)*T)
                sb=s[b*T:(b+1)*T]
                parts=[]
                if lo>0: parts.append(sb[:,:lo])
                parts.append(sb[:,lo:hi]+st_ref[h,:,lo-(I-1)*T:hi-(I-1)*T])
                if hi<S: parts.append(sb[:,hi:])
                rows.append(jnp.concatenate(parts,axis=1) if len(parts)>1 else parts[0])
            s=jnp.concatenate(rows,axis=0) if len(rows)>1 else rows[0]
            m=jnp.max(s,axis=1,keepdims=True)
            p=jnp.exp(s-m).astype(bf)
            p_ref[h,i*BQ:(i+1)*BQ,:]=p
            outs.append(dg(p,vaug[h],NN))
        o0,o1=outs
        num=jnp.where(masks[0],o0,o1)
        den=jnp.where(masks[0],o1,o0)
        den=pltpu.roll(den,64,1)
        linv=1.0/den
        mf=num*linv
        mf_ref[i*BQ:(i+1)*BQ,:]=mf
        mix_ref[i*BQ:(i+1)*BQ,:]=mf.astype(bf)
        linv_ref[i*BQ:(i+1)*BQ,:]=linv
def attn_fwd(qkv,kx,strips,p0,n,BQ=512):
    S,W=qkv.shape; npair=W//3//128
    blk=lambda o: pl.BlockSpec((S,128),lambda p:(0,o*npair+p0+p))
    out=pl.BlockSpec((S,128),lambda p:(0,p))
    return pl.pallas_call(functools.partial(fwd_kernel,BQ,S),cost_estimate=takes(n*5),grid=(n,),
        in_specs=[blk(0),blk(1),blk(2),pl.BlockSpec((2,S,128),lambda p:(p0+p,0,0)),pl.BlockSpec((2,T,3*T),lambda p:(p0+p,0,0))],
        out_specs=[out]*3+[pl.BlockSpec((2,S,S),lambda p:(p,0,0))],
        out_shape=[sd((S,n*128),bf),sd((S,n*128),f32),sd((S,n*128),f32),sd((2*n,S,S),bf)],
        compiler_params=pltpu.CompilerParams(vmem_limit_bytes=56*2**20),
        )(qkv,qkv,qkv,kx,strips)
def bwd_kernel(BQ,S,form,scale,kscale,q_ref,k_ref,v_ref,gm_ref,mf_ref,linv_ref,p_ref,dq_ref,dk_ref,dv_ref,diag_ref,cs_ref,ds_ref):
    nblk=S//T
    lane=lax.broadcasted_iota(jnp.int32,(1,128),1)
    lanes=lax.broadcasted_iota(jnp.int32,(S,128),1)
    rows=lax.broadcasted_iota(jnp.int32,(S,128),0)
    masks=[lane<64,lane>=64]
    q=q_ref[...];k=k_ref[...];v=v_ref[...]
    gm=gm_ref[...].astype(f32);linv=linv_ref[...]
    do=(gm*linv).astype(bf)
    t=do.astype(f32)*mf_ref[...]
    kind=(lanes==rows//T).astype(f32).astype(bf)
    kaug=jnp.concatenate([k,kind],axis=1)
    vx=jnp.where(lanes<2,1.0,0.0).astype(bf)
    vaug=jnp.concatenate([v,vx],axis=1)
    dqs=[];dks=[];dvs=[]
    if form=="T":
        qT=q.T; doT=do.T
    for h in (0,1):
        delta=jnp.sum(jnp.where(masks[h],t,0.0),axis=1,keepdims=True)
        hi=delta.astype(bf).astype(f32); lo=delta-hi
        ex=jnp.where(lanes==0,-hi,jnp.where(lanes==1,-lo,0.0)).astype(bf)
        da=jnp.concatenate([jnp.where(masks[h],do,jnp.zeros_like(do)),ex],axis=1)
        near=[jnp.zeros((T,T),f32) for _ in range(3)]
        dq=[]
        for i in range(S//BQ):
            x=dg(da[i*BQ:(i+1)*BQ],vaug,NT)
            ds=p_ref[h,i*BQ:(i+1)*BQ,:]*x.astype(bf)
            ds_ref[i*BQ:(i+1)*BQ,:]=ds
            dq.append(dg(ds,kaug,NN))
            for b in range(BQ//T):
                I=i*(BQ//T)+b
                for n in (-1,0,1):
                    if 0<=I+n<nblk:
                        near[n+1]=near[n+1]+ds[b*T:(b+1)*T,(I+n)*T:(I+n+1)*T].astype(f32)
        dq=jnp.concatenate(dq,axis=0)
        dqs.append(dq[:,:128])
        far=dq[:,128:]
        ib=rows//T
        total=lambda m: jnp.sum(jnp.sum(jnp.where(m,far,0.0),axis=0,keepdims=True),axis=1,keepdims=True)
        low=total(lanes<=ib-2);up=total((lanes>=ib+2)&(lanes<nblk))
        W=4*T
        y=jnp.concatenate(near+[jnp.zeros((T,T),f32)],axis=1)
        n=T
        while n>8:
            n//=2
            y=y[:n]+pltpu.roll(y[n:],W-n,1)
        sub=lax.broadcasted_iota(jnp.int32,(8,W),0)
        for b in range(3): y=jnp.where(((sub>>b)&1)==1,pltpu.roll(y,W-(1<<b),1),y)
        place=lax.broadcasted_iota(jnp.int32,(1,W),1)
        y=jnp.sum(y,axis=0,keepdims=True)+jnp.where(place==W-1,low,0.0)+jnp.where(place==2*T+1,up,0.0)
        diag_ref[h]=jnp.broadcast_to(y,(8,W))
        if form=="T":
            dks.append(dg(qT[h*64:(h+1)*64],ds_ref[...],NN))
            dvs.append(dg(doT[h*64:(h+1)*64],p_ref[h],NN))
        else:
            dks.append(dg(ds_ref[...],q,TN))
            dvs.append(dg(p_ref[h],do,TN))
    dq=(jnp.where(masks[0],dqs[0],dqs[1])*scale).astype(bf)
    dq_ref[...]=dq
    if form=="T":
        dk_ref[...]=(jnp.concatenate(dks,axis=0)*kscale).T.astype(bf)
        dv=jnp.concatenate(dvs,axis=0).T.astype(bf)
    else:
        dk_ref[...]=(jnp.where(masks[0],dks[0],dks[1])*kscale).astype(bf)
        dv=jnp.where(masks[0],dvs[0],dvs[1]).astype(bf)
    dv_ref[...]=dv
    part=lax.broadcasted_iota(jnp.int32,(8,128),0)
    cs_ref[...]=jnp.where(part==0,jnp.sum(dq.astype(f32),axis=0,keepdims=True),jnp.sum(dv.astype(f32),axis=0,keepdims=True))
def attn_bwd(qkv,gm,mixed,linv,p,p0,n,BQ=512,form="T",scale=0.125,kscale=1.0):
    S,W=qkv.shape; npair=W//3//128
    blk=lambda o: pl.BlockSpec((S,128),lambda i:(0,o*npair+p0+i))
    own=pl.BlockSpec((S,128),lambda i:(0,i))
    return pl.pallas_call(functools.partial(bwd_kernel,BQ,S,form,scale,kscale),cost_estimate=takes(n*6),grid=(n,),
        in_specs=[blk(0),blk(1),blk(2),blk(0),own,own,pl.BlockSpec((2,S,S),lambda i:(i,0,0))],
        out_specs=[own]*3+[pl.BlockSpec((2,8,4*T),lambda i:(i,0,0)),pl.BlockSpec((8,128),lambda i:(0,i))],
        out_shape=[sd((S,n*128),bf)]*3+[sd((2*n,8,4*T),f32),sd((8,n*128),f32)],
        scratch_shapes=[pltpu.VMEM((S,S),bf)],
        compiler_params=pltpu.CompilerParams(vmem_limit_bytes=56*2**20),
        )(qkv,qkv,qkv,gm,mixed,linv,p)
sd=jax.ShapeDtypeStruct
def takes(us): return pl.CostEstimate(flops=int(us*1.15e9),bytes_accessed=int(us*1e6),transcendentals=0)
def dg(a,b,d=NN): return lax.dot_general(a,b,d,preferred_element_type=f32)
QB,VB,OB,G1,S1,DB,G2,S2,SW,UB,CT,TG,NV=0,1,2,3,4,5,6,7,8,9,13,14,24
def gelu_both(x,mode="poly"):
    e=jnp.exp(x*x*-0.5)
    if mode=="erf":
        cdf=0.5*(1.0+lax.erf(x*0.7071067811865476))
    else:
        t=1.0/(1.0+(0.3275911*0.7071067811865476)*jnp.abs(x))
        q=t*(0.127414796+t*(-0.142248368+t*(0.7107068705+t*(-0.7265760135+t*0.5307027145))))*e
        cdf=jnp.where(x>=0,1.0-q,q)
    return x*cdf, cdf+x*e*0.3989422804014327
def norm(r):
    c=r-jnp.mean(r,axis=-1,keepdims=True)
    s=lax.rsqrt(jnp.mean(c*c,axis=-1,keepdims=True)+1e-05)
    return c*s,s
def norm_bwd(up,u,s,g):
    p=up*g
    return (p-jnp.mean(p,axis=-1,keepdims=True)-u*jnp.mean(p*u,axis=-1,keepdims=True))*s
def whole(a): return pl.BlockSpec(memory_space=pltpu.VMEM)

BLK=16
SUB=2
RELA=((0,0,0),(0,0,1),(0,1,0),(0,1,1))
RELB=((0,0,2),(0,0,3),(1,0,2),(1,0,3))
RELXA=((1,0,0),(1,0,1),(1,1,0),(1,1,1))
RELYB=((0,1,2),(0,1,3),(1,1,2),(1,1,3))
RELS=(RELA,RELB,RELXA,RELYB)
X_,Y_,Z_,C_=0,1,2,3
def place(pos,rel):
    xr,yr,zr=rel
    return (((pos[Z_]-zr)&3)*2+(pos[Y_]^yr))*2+(pos[X_]^xr)
def slot(pos,k):
    x,y,z=k&1,(k>>1)&1,k>>2
    xr,yr,zr=pos[X_]^x,pos[Y_]^y,(pos[Z_]-z)&3
    return jnp.where(zr<2,(1-xr)*8+yr*2+zr,2+(1-yr)*8+xr*2+zr)
def load(pos,pieces,parts,sem):
    for s in range(8):
        half=pos[C_] if s<4 else 1-pos[C_]
        for b,rel in enumerate(RELS[s%4]):
            k=place(pos,rel)
            R=pieces[s].shape[1]
            rows=pl.ds(pl.multiple_of(k*R,R),R)
            for off,w,dst in parts:
                cols=pl.ds(pl.multiple_of(half*w,w),w)
                pltpu.make_async_copy(pieces[s].at[b,:,pl.ds(off,w)],dst.at[rows,cols],sem).start()
def arrived(dst,sem):
    pltpu.make_async_copy(dst,dst,sem).wait()
ANYS=pl.BlockSpec(memory_space=pltpu.HBM)
SMEM=pl.BlockSpec(memory_space=pltpu.SMEM)
def qkv_kernel(pos,*refs):
    pieces=refs[:8]; hid_ref,o_ref,vec_ref,w_s,sm_s,sems=refs[8:]
    D=hid_ref.shape[1]; N=3*D
    @pl.when(pl.program_id(0)==0)
    def _():
        for s in range(4):
            for b,rel in enumerate(RELS[s]):
                R=pieces[s].shape[1]
                rows=pl.ds(pl.multiple_of(place(pos,rel)*R,R),R)
                pltpu.make_async_copy(pieces[s].at[b,:,pl.ds(N//2,128)],sm_s.at[rows,:],sems.at[1]).start()
        load(pos,pieces,[(0,N//2,w_s)],sems.at[0])
        arrived(sm_s,sems.at[1])
        vec_ref[...]=sm_s[...].astype(f32).T[:NV]
        arrived(w_s,sems.at[0])
    x=hid_ref[...]
    o_ref[:,:D]=((dg(x,w_s[:,:D])+vec_ref[QB:QB+1,:])*0.125).astype(bf)
    o_ref[:,D:2*D]=dg(x,w_s[:,D:2*D]).astype(bf)
    o_ref[:,2*D:]=(dg(x,w_s[:,2*D:])+vec_ref[VB:VB+1,:]).astype(bf)
def qkv_fwd(pos,pieces,hid,TR=256):
    R,D=hid.shape;N=3*D
    return pl.pallas_call(qkv_kernel,cost_estimate=takes(9),grid=(R//TR,),
        in_specs=[SMEM]+[ANYS]*8+[pl.BlockSpec((TR,D),lambda i:(i,0))],
        out_specs=[pl.BlockSpec((TR,N),lambda i:(i,0)),pl.BlockSpec((NV,D),lambda i:(0,0))],
        out_shape=[sd((R,N),bf),sd((NV,D),f32)],
        scratch_shapes=[pltpu.VMEM((D,N),bf),pltpu.VMEM((D,128),bf),pltpu.SemaphoreType.DMA((2,))],
        compiler_params=pltpu.CompilerParams(vmem_limit_bytes=56*2**20))(pos,*pieces,hid)
def fetch(w,off,dst,sem):
    pltpu.make_async_copy(w.at[:,pl.ds(off,dst.shape[1])],dst,sem).start()
def fetch_down(w,off,dst,sems):
    D=dst.shape[1]
    for j in range(dst.shape[0]//D):
        pltpu.make_async_copy(w.at[:,pl.ds(off+j*D,D)],dst.at[pl.ds(j*D,D),:],sems.at[j]).start()
def arrived_down(dst,sems):
    D=dst.shape[1]
    for j in range(dst.shape[0]//D):
        arrived(dst.at[pl.ds(j*D,D),:],sems.at[j])
def post_kernel(TR,mode,len_ref,*refs):
    w,*parts,hid_ref,vec_ref,lo_ref,u1_ref,u2_ref,sc_ref,nl_ref,act_ref,gp_ref,fr_ref,os_ref,ow_ref,uw_ref,dw_ref,sems=refs
    D=hid_ref.shape[1];F=uw_ref.shape[1]
    i=pl.program_id(0)
    @pl.when(i==0)
    def _():
        fetch(w,0,ow_ref,sems.at[4])
        fetch(w,D,uw_ref,sems.at[5])
        fetch_down(w,D+F,dw_ref,sems)
        arrived(ow_ref,sems.at[4])
    vec=lambda n: vec_ref[n:n+1,:]
    HR=TR//SUB
    halves=[slice(q*HR,(q+1)*HR) for q in range(SUB)]
    def one(h):
        r=hid_ref[h,:].astype(f32)+(dg(jnp.concatenate([m[h,:] for m in parts],axis=1),ow_ref[...])+vec(OB))
        return norm(r)
    def two(h,u1):
        u1_ref[h,:]=u1.astype(bf)
        n=u1*vec(G1)+vec(S1)
        nl=n.astype(bf)
        nl_ref[h,:]=nl
        return n,nl
    def three(h,nl):
        br=None
        for c in range(F//D):
            x=dg(nl,uw_ref[:,c*D:(c+1)*D])+vec(UB+c)
            a,gp=gelu_both(x,mode)
            a=a.astype(bf)
            act_ref[h,c*D:(c+1)*D]=a
            gp_ref[h,c*D:(c+1)*D]=gp.astype(bf)
            b=dg(a,dw_ref[c*D:(c+1)*D,:])
            br=b if br is None else br+b
        return br
    def four(q,h,n,br,s1):
        u2,s2=norm(n+(br+vec(DB)))
        u2_ref[h,:]=u2.astype(bf)
        fin=u2*vec(G2)+vec(S2)
        row=lax.broadcasted_iota(jnp.int32,(HR,D),0)+i*TR+q*HR
        lo_ref[h,:]=jnp.where(row<len_ref[0],fin,0.0).astype(bf)
        lane=lax.broadcasted_iota(jnp.int32,(HR,128),1)
        sc_ref[h,:]=jnp.where(lane==0,s1,s2)
        return fin
    us=[one(h) for h in halves]
    ns=[two(h,u[0]) for h,u in zip(halves,us)]
    @pl.when(i==0)
    def _():
        arrived(uw_ref,sems.at[5])
        arrived_down(dw_ref,sems)
    brs=[three(h,n[1]) for h,n in zip(halves,ns)]
    fin=[four(q,h,ns[q][0],brs[q],us[q][1]) for q,h in enumerate(halves)][0]
    @pl.when(i==0)
    def _():
        fr_ref[...]=fin[:8]
        own=jnp.sum(fin[:1]*vec(SW),axis=1,keepdims=True)
        os_ref[...]=jnp.broadcast_to(own,(8,128))
def post_fwd(length,w,mixed,hid,vec,TR=512,mode="erf"):
    R,D=hid.shape;F=4*D
    rb=lambda n: pl.BlockSpec((TR,n),lambda i:(i,0))
    cb=lambda a: pl.BlockSpec(a.shape,lambda i:(0,0))
    return pl.pallas_call(functools.partial(post_kernel,TR,mode),cost_estimate=takes(25),grid=(R//TR,),
        in_specs=[SMEM,ANYS]+[rb(m.shape[1]) for m in mixed]+[rb(D),cb(vec)],
        out_specs=[rb(D),rb(D),rb(D),rb(128),rb(D),rb(F),rb(F),pl.BlockSpec((8,D),lambda i:(0,0)),pl.BlockSpec((8,128),lambda i:(0,0))],
        out_shape=[sd((R,D),bf),sd((R,D),bf),sd((R,D),bf),sd((R,128),f32),sd((R,D),bf),sd((R,F),bf),sd((R,F),bf),sd((8,D),f32),sd((8,128),f32)],
        scratch_shapes=[pltpu.VMEM((D,D),bf),pltpu.VMEM((D,F),bf),pltpu.VMEM((F,D),bf),pltpu.SemaphoreType.DMA((6,))],
        compiler_params=pltpu.CompilerParams(vmem_limit_bytes=60*2**20))(length,w,*mixed,hid,vec)
def listwise(pos,ncol,d1,scores,vec_ref,info_ref):
    lane=lax.broadcasted_iota(jnp.int32,(1,vec_ref.shape[1]),1)
    pb,col=pos[4],pos[5]
    counts=vec_ref[CT:CT+1,:]
    targets=vec_ref[TG:TG+1,:]+vec_ref[TG+1:TG+2,:]+vec_ref[TG+2:TG+3,:]
    pick=lambda row,dev: jnp.sum(jnp.where(lane==dev*d1,row,0.0),axis=1,keepdims=True)
    total=jnp.sum(counts,axis=1,keepdims=True)*(1.0/ncol)
    mine=pick(counts,pb*ncol)
    n=len(scores)
    live=[(col^r).astype(f32)<mine for r in range(n)]
    share=[jnp.where(live[r],pick(targets,pb*ncol+(col^r)),0.0) for r in range(n)]
    def pairs(f,v):
        while len(v)>1: v=[f(v[i],v[i+1]) for i in range(0,len(v),2)]
        return v[0]
    add=lambda a,b: a+b
    whole=pairs(add,share)
    masked=[jnp.where(live[r],scores[r],-1e30) for r in range(n)]
    top=pairs(jnp.maximum,masked)
    log=top+jnp.log(pairs(add,[jnp.exp(m-top) for m in masked]))
    entropy=log-pairs(add,[share[r]/whole*scores[r] for r in range(n)])
    prob=jnp.where(live[0],jnp.exp(masked[0]-log),0.0)
    gs=mine/total*(prob-share[0]/whole)
    weighted=jnp.where(col==0,mine*entropy,0.0)
    row=lax.broadcasted_iota(jnp.int32,(8,128),0)
    info_ref[...]=jnp.where(row==0,gs,jnp.where(row==1,weighted,total))
def whole1(a): return pl.BlockSpec(a.shape,lambda i:(0,)*len(a.shape),pipeline_mode=pl.Buffered(1))
def mid_kernel(TR,ncol,d1,nm,pos,len_ref,*refs):
    s_refs=refs[:ncol]
    w,act,nl=refs[ncol:ncol+3]
    mixed=refs[ncol+3:ncol+3+nm]
    (og_ref,u2_ref,u1_ref,sc_ref,gp_ref,vec_ref,ga_ref,gm_ref,vg_ref,info_ref,keep,send,
     ow_s,uw_s,dw_s,act_s,nl_s,mix_s,gb_s,gi_s,ga_s,stage,sems,outs)=refs[ncol+3+nm:]
    D=og_ref.shape[1];F=gp_ref.shape[1];H=D//2
    i=pl.program_id(0);n=pl.num_programs(0)
    def whole_copies():
        at=0
        todo=[(act,act_s,6),(nl,nl_s,7)]
        for j,m in enumerate(mixed):
            todo.append((m,mix_s.at[:,at:at+m.shape[1]],8+j)); at+=m.shape[1]
        return [pltpu.make_async_copy(a,b,sems.at[k]) for a,b,k in todo]
    @pl.when(i==0)
    def _():
        fetch_down(w,D+F,dw_s,sems)
        fetch(w,D,uw_s,sems.at[4])
        fetch(w,0,ow_s,sems.at[5])
        listwise(pos,ncol,d1,[r[0:1,0:1] for r in s_refs],vec_ref,info_ref)
        vg_ref[...]=jnp.zeros_like(vg_ref)
        arrived_down(dw_s,sems)
    @pl.when(i==1)
    def _():
        for c in whole_copies(): c.start()
    vec=lambda k: vec_ref[k:k+1,:]
    def add(k,v): vg_ref[k:k+1,:]+=jnp.sum(v,axis=0,keepdims=True)
    HR=TR
    halves=[slice(0,TR)]
    def one(q,h):
        row=lax.broadcasted_iota(jnp.int32,(HR,D),0)+i*TR+q*HR
        gf=og_ref[h,:].astype(f32)
        gf=gf+jnp.where(row==0,info_ref[0:1,0:1]*vec(SW),0.0)
        gf=jnp.where(row<len_ref[0],gf,0.0)
        u2=u2_ref[h,:].astype(f32)
        add(G2,gf*u2); add(S2,gf)
        gr2=norm_bwd(gf,u2,sc_ref[h,1:2],vec(G2))
        gb=gr2.astype(bf)
        here=pl.ds(pl.multiple_of(i*TR+q*HR,HR),HR)
        gb_s[here,:]=gb
        add(DB,gb.astype(f32))
        return here,gr2,gb
    def two(h,here,gr2,gb):
        gn=gr2
        for c in range(F//D):
            g=dg(gb,dw_s[c*D:(c+1)*D,:],NT)
            gi=(g*gp_ref[h,c*D:(c+1)*D].astype(f32)).astype(bf)
            gi_s[here,c*D:(c+1)*D]=gi
            add(UB+c,gi.astype(f32))
            gn=gn+dg(gi,uw_s[:,c*D:(c+1)*D],NT)
        return gn
    def three(h,here,gn):
        u1=u1_ref[h,:].astype(f32)
        add(G1,gn*u1); add(S1,gn)
        ga=norm_bwd(gn,u1,sc_ref[h,0:1],vec(G1)).astype(bf)
        ga_ref[h,:]=ga
        ga_s[here,:]=ga
        add(OB,ga.astype(f32))
        return ga
    a=[one(q,h) for q,h in enumerate(halves)]
    @pl.when(i==0)
    def _():
        arrived(uw_s,sems.at[4])
        arrived(ow_s,sems.at[5])
    gns=[two(h,*v) for h,v in zip(halves,a)]
    gas=[three(h,v[0],gn) for h,v,gn in zip(halves,a,gns)]
    for h,ga in zip(halves,gas): gm_ref[h,:]=dg(ga,ow_s[...],NT).astype(bf)
    @pl.when(i==n-1)
    def _():
        for c in whole_copies(): c.wait()
        core=pos[C_]
        slots=[slot(pos,k) for k in range(BLK)]
        U=H+F//2
        jobs=[]
        for ref,h in ((send,1-core),(keep,core)):
            for c in range(F//D//2):
                jobs.append((ref,h,c,"down"))
            for c in range(F//D//2):
                jobs.append((ref,h,c,"up"))
        jobs.append((None,None,0,"out"))
        copies=[]
        for j,(ref,h,c,kind) in enumerate(jobs):
            b=j&1
            if j>=2:
                for v in copies[j-2]: v.wait()
            if kind!="out":
                cols=pl.ds(pl.multiple_of(h*(F//2)+c*D,D),D)
            if kind=="down":
                t=dg(act_s[:,cols],gb_s[...],TN)
            elif kind=="up":
                t=dg(nl_s[...],gi_s[:,cols],TN)
            else:
                t=dg(mix_s[...],ga_s[...],TN)
            t=t.astype(bf)
            for k in range(BLK):
                stage[b,slots[k]]=t[k*(D//BLK):(k+1)*(D//BLK)]
            if kind=="out":
                halves=[pl.ds(pl.multiple_of(v*H,H),H) for v in (core,1-core)]
                made=[pltpu.make_async_copy(stage.at[b,:,:,halves[m]],r.at[:,:,pl.ds(0,H)],outs.at[j+m]) for m,r in enumerate((keep,send))]
            else:
                off=(U if kind=="down" else H)+c*D
                made=[pltpu.make_async_copy(stage.at[b],ref.at[:,:,pl.ds(off,D)],outs.at[j])]
            for v in made: v.start()
            copies.append(made)
        for made in copies[-2:]:
            for v in made: v.wait()
def mid(pos,length,scores,d1,w,og,u2,u1,sc,act,gp,nl,mixed,vec,TR=256):
    R,D=og.shape;F=act.shape[1]
    rb=lambda n: pl.BlockSpec((TR,n),lambda i:(i,0))
    o=sd((BLK,D//BLK,(D+2*F)//2),bf)
    return pl.pallas_call(functools.partial(mid_kernel,TR,len(scores),d1,len(mixed)),cost_estimate=takes(32),grid=(R//TR,),
        in_specs=[SMEM]*2+[whole1(v) for v in scores]+[ANYS]*(3+len(mixed))+[rb(D),rb(D),rb(D),rb(128),rb(F),whole1(vec)],
        out_specs=[rb(D),rb(D),whole1(vec),whole1(scores[0]),ANYS,ANYS],
        out_shape=[sd((R,D),bf),sd((R,D),bf),vec,sd((8,128),f32),o,o],
        scratch_shapes=[pltpu.VMEM((D,D),bf),pltpu.VMEM((D,F),bf),pltpu.VMEM((F,D),bf),pltpu.VMEM((R,F),bf),pltpu.VMEM((R,D),bf),pltpu.VMEM((R,D),bf),
                        pltpu.VMEM((R,D),bf),pltpu.VMEM((R,F),bf),pltpu.VMEM((R,D),bf),pltpu.VMEM((2,BLK,D//BLK,D),bf),
                        pltpu.SemaphoreType.DMA((8+len(mixed),)),pltpu.SemaphoreType.DMA((10,))],
        compiler_params=pltpu.CompilerParams(vmem_limit_bytes=60*2**20))(pos,length,*scores,w,act,nl,*mixed,og,u2,u1,sc,gp,vec)
VM=pl.BlockSpec(memory_space=pltpu.VMEM)
def small_kernel(buckets,n,vg,info,first,*refs):
    diags,sums,sm_ref=refs[:n],refs[n:2*n],refs[2*n]
    D=first.shape[1]
    sm_ref[...]=jnp.zeros_like(sm_ref)
    sm_ref[:CT]=vg[:CT]
    at=0
    for r in sums:
        sm_ref[CT:CT+2,at:at+r.shape[1]]=r[0:2]
        at+=r.shape[1]
    sm_ref[CT+2:CT+3]=info[0:1,0:1]*first[0:1]
    place=lax.broadcasted_iota(jnp.int32,(4*T,128),0)
    off=jnp.where(place<3*T,place-T,place-5*T)
    which=jnp.where(off>0,buckets//2,0)
    for e in EDGES: which=which+(jnp.abs(off)>=e).astype(jnp.int32)
    onehot=(which==lax.broadcasted_iota(jnp.int32,(4*T,128),1)).astype(f32)
    diag=jnp.concatenate([d[h,0:1] for d in diags for h in range(d.shape[0])],axis=0)
    sums=lax.dot_general(diag,onehot,NN,precision=lax.Precision.HIGHEST,preferred_element_type=f32)
    sm_ref[CT+3:CT+3+diag.shape[0],:128]=sums
    sm_ref[31:32]=jnp.broadcast_to(info[1:2,0:1],(1,D))
def small_sums(buckets,vg,info,first,diags,sums):
    return pl.pallas_call(functools.partial(small_kernel,buckets,len(diags)),cost_estimate=takes(2),in_specs=[VM]*(3+2*len(diags)),out_specs=VM,
        out_shape=sd((32,first.shape[1]),f32))(vg,info,first,*diags,*sums)
def wqkv_kernel(pos,hid_ref,*refs):
    *parts,k_ref,s_ref,g_s=refs
    D=hid_ref.shape[1];N=3*D
    at=0
    for r in parts:
        g_s[:,at:at+r.shape[1]]=r[...]
        at+=r.shape[1]
    x=hid_ref[...]
    core=pos[C_]
    slots=[slot(pos,k) for k in range(BLK)]
    for ref,h in ((s_ref,1-core),(k_ref,core)):
        t=dg(x,g_s[:,pl.ds(pl.multiple_of(h*(N//2),N//2),N//2)],TN).astype(bf)
        for k in range(BLK):
            ref[slots[k]]=t[k*(D//BLK):(k+1)*(D//BLK)]
def wqkv(pos,hid,parts):
    R,D=hid.shape;N=3*D
    g=sd((BLK,D//BLK,N//2),bf)
    return pl.pallas_call(wqkv_kernel,cost_estimate=takes(9),
        in_specs=[SMEM,VM]+[VM]*len(parts),out_specs=[VM]*2,out_shape=[g,g],
        scratch_shapes=[pltpu.VMEM((R,N),bf)],
        compiler_params=pltpu.CompilerParams(vmem_limit_bytes=60*2**20))(pos,hid,*parts)
def hgrad_kernel(pos,*refs):
    pieces=refs[:8]
    *parts,gr1_ref,hg_ref,w_s,sems=refs[8:]
    D=gr1_ref.shape[1];N=3*D
    @pl.when(pl.program_id(0)==0)
    def _():
        load(pos,pieces,[(0,N//2,w_s)],sems.at[0])
        arrived(w_s,sems.at[0])
    g=jnp.concatenate([r[...] for r in parts],axis=1)
    hg_ref[...]=(gr1_ref[...].astype(f32)+dg(g,w_s[...],NT)).astype(bf)
def hgrad(pos,pieces,parts,gr1,TR=256):
    R,D=gr1.shape;N=3*D
    rb=lambda n: pl.BlockSpec((TR,n),lambda i:(i,0))
    return pl.pallas_call(hgrad_kernel,cost_estimate=takes(10),grid=(R//TR,),
        in_specs=[SMEM]+[ANYS]*8+[rb(p.shape[1]) for p in parts]+[rb(D)],
        out_specs=rb(D),out_shape=sd((R,D),bf),
        scratch_shapes=[pltpu.VMEM((D,N),bf),pltpu.SemaphoreType.DMA((1,))],
        compiler_params=pltpu.CompilerParams(vmem_limit_bytes=60*2**20))(pos,*pieces,*parts,gr1)

ALL=("pb","col")
def staged():
    return lax.axis_size("pb")==8 and lax.axis_size("col")==4
def swap_core(v): return lax.ppermute(v,"col",[(i,i^1) for i in range(4)])
def swap_col(v,k): return lax.ppermute(v,"col",[(i,i^k) for i in range(lax.axis_size("col"))])
def swap_x(v): return lax.ppermute(v,"col",[(i,i^2) for i in range(4)])
def swap_y(v): return lax.ppermute(v,"pb",[(i,i^1) for i in range(8)])
def flip_z(v,m): return lax.ppermute(v,"pb",[(i,i^(2*m)) for i in range(8)])
def shift_z(v,k): return lax.ppermute(v,"pb",[(i,(i+2*k)%8) for i in range(8)])
def cat(a): return jnp.concatenate(a,axis=0)
def after(v,*first):
    return lax.optimization_barrier((v,)+first)[0]
def spread1(block):
    o=block[None]
    return [o,shift_z(o,1),shift_z(o,2),shift_z(o,3)]
def spread2(v):
    a=cat(v[:2]);b=cat(v[2:])
    return [cat([a,swap_y(a)]),cat([b,swap_x(b)])]
def spread3(v):
    a,b=v
    return [a,b,swap_x(a),swap_y(b)]
def spread4(own):
    return own+[swap_core(v) for v in own]
def own_order():
    zero=(0,0,0,0)
    return [[place(zero,rel) for rel in rels] for rels in RELS]
def spread_plain(full):
    out=[]
    for half in (0,1):
        cols=jnp.concatenate([w.reshape(BLK,w.shape[0]//BLK,2,w.shape[1]//2)[:,:,half] for w in full],axis=2)
        for order in own_order():
            out.append(jnp.stack([cols[k] for k in order]))
    return out
def add2(a,b): return (a.astype(f32)+b.astype(f32)).astype(bf)
def collect1(keep,r):
    sa,sb,ka,kb=[add2(keep[4*s:4*s+4],r[4*s:4*s+4]) for s in range(4)]
    return ka,kb,swap_x(sa),swap_y(sb)
def collect2(ka,kb,ra,rb):
    ka2,sa2=add2(ka[:2],ra[:2]),add2(ka[2:],ra[2:])
    kb2,sb2=add2(kb[:2],rb[:2]),add2(kb[2:],rb[2:])
    return ka2,kb2,swap_y(sa2),swap_x(sb2)
def collect3(*panels):
    t=[[ka2[0].astype(f32)+ra[0].astype(f32),add2(ka2[1],ra[1]),add2(kb2[0],rb[0]),add2(kb2[1],rb[1])] for ka2,kb2,ra,rb in panels]
    return [jnp.concatenate(v,axis=1) if len(v)>1 else v[0] for v in zip(*t)]
def send3(t0,t1,t2,t3): return t0,shift_z(t1,3),shift_z(t2,2),shift_z(t3,1)
def collect4(t0,t1,t2,t3):
    t=t0+t1.astype(f32)+t2.astype(f32)+t3.astype(f32)
    c=lax.axis_index("col")&1
    h=t.shape[0]//2
    mine=lax.dynamic_slice_in_dim(t,c*h,h,0)
    other=swap_core(lax.dynamic_slice_in_dim(t,(1-c)*h,h,0).astype(bf)).astype(f32)
    return mine,other
def afters(vs,*first):
    return list(lax.optimization_barrier(tuple(vs)+tuple(first))[:len(vs)])
def sides(mine,other,c):
    return jnp.where(c==0,jnp.concatenate([mine,other],axis=1),jnp.concatenate([other,mine],axis=1))
def natural(keep,send):
    order=[int(v) for v in NATURAL]
    keep,send=[jnp.concatenate([v[k] for k in order],axis=0) for v in (keep,send)]
    return jnp.concatenate([keep,send],axis=1)
def slot0(k):
    xr,yr,zr=k&1,(k>>1)&1,(-(k>>2))&3
    return (1-xr)*8+yr*2+zr if zr<2 else 2+(1-yr)*8+xr*2+zr
NATURAL=[slot0(k) for k in range(BLK)]

def shards(hidden, lengths, counts, targets, out_grad, qkv_weight, qv_bias, out_weight, out_bias,
           norm1_gain, norm1_bias, up_weight, up_bias, down_weight, down_bias, norm2_gain,
           norm2_bias, rel_bias, score_weight):
    _, _, S, D = hidden.shape
    F = down_weight.shape[0] * lax.axis_size(ALL)
    n_dev = lax.axis_size(ALL)
    dev = lax.axis_index(ALL)
    d1, f1 = D // n_dev, F // n_dev
    tokens = hidden.reshape(S, D)
    length = lengths.reshape(1)
    fast = staged()
    count_f = counts.astype(f32)
    npb, ncol = lax.axis_size("pb"), lax.axis_size("col")
    pb, col = lax.axis_index("pb"), lax.axis_index("col")
    t1 = targets.astype(bf)
    t2 = (targets - t1.astype(f32)).astype(bf)
    t3 = (targets - t1.astype(f32) - t2.astype(f32)).astype(bf)
    columns = [qv_bias[0], qv_bias[1], out_bias, norm1_gain, norm1_bias, down_bias, norm2_gain, norm2_bias, score_weight]
    columns += [up_bias[j * d1 : (j + 1) * d1] for j in range(4)]
    lane = lax.broadcasted_iota(jnp.int32, (d1, 128), 1)
    panel = jnp.zeros((d1, 128), bf)
    for j, v in enumerate(columns):
        panel = jnp.where(lane == j, v[:, None], panel)
    place0 = lax.broadcasted_iota(jnp.int32, (d1, 128), 0) == 0
    for j, v in enumerate((count_f.reshape(1, 1).astype(bf), t1, t2, t3)):
        panel = jnp.where((lane == CT + j) & place0, v, panel)
    ups = up_weight.reshape(d1, n_dev, 4, d1).transpose(0, 2, 1, 3).reshape(d1, F)
    rest = jnp.concatenate([out_weight, ups] + [down_weight[j * d1 : (j + 1) * d1] for j in range(4)], axis=1)
    w_rest = lax.all_gather(rest, ALL, axis=0, tiled=True)
    if fast:
        c = col & 1
        pos = jnp.stack([col >> 1, pb & 1, pb >> 1, c, pb, col]).astype(jnp.int32)
        half = lambda h: jnp.concatenate([lax.dynamic_slice_in_dim(qkv_weight, h * (3 * D // 2), 3 * D // 2, 1), panel], axis=1)
        got, mine = swap_core(half(1 - c)), half(c)
        q1 = spread1(jnp.where(c == 0, cat([mine, got]), cat([got, mine])))
        p_qkv = spread4(spread3(spread2(q1)))
    else:
        pos = jnp.stack([0 * pb, 0 * pb, 0 * pb, 0 * pb, pb, col]).astype(jnp.int32)
        both = lax.all_gather(jnp.concatenate([qkv_weight, panel], axis=1), ALL, axis=0, tiled=True)
        panel = both[:, 3 * D :]
        p_qkv = spread_plain([both[:, : 3 * D], jnp.concatenate([panel, panel], axis=1)])
    strips, kx = tables(rel_bias, length[0], S)
    qkv, vec = qkv_fwd(pos, p_qkv, tokens)
    calls = ((0, 2), (2, rel_bias.shape[1] // 2 - 2))
    attn = [attn_fwd(qkv, kx, strips, *call) for call in calls]
    mixed = [v[0] for v in attn]
    layer_out, u1, u2, sc, nl, act, gp, first, own_score = post_fwd(length, w_rest, mixed, tokens, vec)
    scores = [own_score] + [swap_col(own_score, r) for r in range(1, ncol)]
    ga, gm, vg, info, keep, send = mid(pos, length, scores, d1, w_rest, out_grad.reshape(S, D), u2, u1, sc, act, gp, nl, mixed, vec)
    def home(down, up):
        down = cat([down[:, j * D : (j + 1) * D] for j in range(4)])
        return down, up.reshape(d1, 4, n_dev, d1).transpose(0, 2, 1, 3).reshape(d1, F)
    def own_part(v):
        part = lax.dynamic_slice_in_dim(v, dev * d1, d1, axis=1)
        return part, v[31, 0] / info[2, 0], v[CT + 3 : CT + 3 + rel_bias.shape[1], : rel_bias.shape[0]].T
    if fast:
        r0 = swap_core(send)
    back = lambda i, g: attn_bwd(qkv, g, attn[i][2], attn[i][1], attn[i][3], *calls[i])
    grads = [back(0, gm)]
    if fast:
        c1 = collect1(*afters([keep, r0], grads[0][0]))
        gm_2 = afters([gm], c1[0], c1[1])[0]
    else:
        gm_2 = gm
    grads.append(back(1, gm_2))
    parts = [g[j] for j in range(3) for g in grads]
    smalls = small_sums(rel_bias.shape[0], vg, info, first, [g[3] for g in grads], [g[4] for g in grads])
    h = D // 2
    if fast:
        smalls = smalls + swap_core(smalls)
        travel = swap_x(smalls)
        c2 = collect2(*afters(c1, smalls))
        smalls = smalls + afters([travel], c2[0], c2[1])[0]
        travel = swap_y(smalls)
        parts = afters(parts, smalls, c2[0], c2[1])
    kq, sq = wqkv(pos, tokens, parts)
    if fast:
        smalls = smalls + afters([travel], kq)[0]
        rq0 = swap_core(afters([sq], smalls)[0])
        smalls = smalls + flip_z(smalls, 1)
        travel = flip_z(smalls, 2)
        c3 = collect3(afters(c2, kq, smalls))
        smalls = smalls + afters([travel], *c3)[0]
        c3 = afters(c3, smalls)
        cq1 = collect1(kq, afters([rq0], *c3)[0])
        c3 = send3(*c3)
        parts = afters(parts, cq1[0], cq1[1], smalls)
        hidden_grad = hgrad(pos, p_qkv, parts, ga)
        cq2 = collect2(*afters(cq1, hidden_grad))
        cq3 = collect3(cq2)
        m, o = collect4(*afters(c3, *cq3))
        cq3 = send3(*cq3)
        n = (D + F) // 2
        d_out = sides(m[:, :h], o[:, :h], c)
        d_up = sides(m[:, h:n], o[:, h:n], c)
        d_down = sides(m[:, n:], o[:, n:], c)
        d_down, d_up = home(d_down, d_up)
        little = own_part(smalls)
        m, o = collect4(*afters(cq3, d_out, d_up, d_down, *little))
        d_qkv = sides(m, o, c)
    else:
        hidden_grad = hgrad(pos, p_qkv, parts, ga)
        scatter = lambda w: lax.psum_scatter(w, ALL, scatter_dimension=0, tiled=True).astype(f32)
        n = (D + F) // 2
        d_qkv = scatter(natural(kq, sq))
        d_out = scatter(natural(keep[:, :, :h], send[:, :, :h]))
        d_up = scatter(natural(keep[:, :, h:n], send[:, :, h:n]))
        d_down = scatter(natural(keep[:, :, n:], send[:, :, n:]))
        d_down, d_up = home(d_down, d_up)
        little = own_part(lax.psum(smalls, ALL))
    part, loss, bucket = little
    return (layer_out.reshape(hidden.shape), loss, hidden_grad.reshape(hidden.shape), d_qkv, part[CT : CT + 2],
            d_out, part[OB], part[G1], part[S1], d_up, part[UB : UB + 4].reshape(-1), d_down, part[DB], part[G2], part[S2],
            bucket, part[CT + 2])


def solution(mesh):
    lead = P(("pb", "col"))
    row = P(("pb", "col"), None)
    act = P("pb", "col", None, None)
    side = P(None, ("pb", "col"))
    return jax.shard_map(
        shards,
        mesh=mesh,
        in_specs=(act, P("pb", "col"), P("pb"), P("pb", "col"), act, row, side, row, lead, lead, lead, row, lead, row, lead, lead, lead, P(), lead),
        out_specs=(act, P(), act, row, side, row, lead, lead, lead, row, lead, row, lead, lead, lead, P(), lead),
        check_vma=False,
    )
```
